32 devices in a mesh: fsdp: 8 (over y, x, core), rep: 4 (over z).
Axes of the slice: x: 2, y: 2, z: 4, core: 2. Of those that a mesh axis runs over, the one named last changes fastest.
Arguments:
- tokens: bfloat16 [16384, 768], P(('fsdp', 'rep')), may hold values from -6 to 6
- cotangent: bfloat16 [16384, 768], P(('fsdp', 'rep')), may hold values from -6 to 6
- segment_ids: int32 [64, 256], P(('fsdp', 'rep')), may hold values from 0 to 2, never falling along the last dimension, each value on 1 to 128 neighbouring positions
- block_slot_index: int32 [108], replicated, may hold values from 0 to 111, as said below
- weights: float32 [112, 256, 256], P('fsdp')
- first_moment: float32 [112, 256, 256], P('fsdp')
- second_moment: float32 [112, 256, 256], P('fsdp'), as said below
- left_basis: float32 [112, 256, 256], P('fsdp'), as said below
- right_basis: float32 [112, 256, 256], P('fsdp'), as said below
- norm_gains: float32 [2, 768], replicated, may hold values from 0.25 to 1.75
- gain_first: float32 [2, 768], replicated, may hold values from -768 to 768
- gain_second: float32 [2, 768], replicated, may hold values from 8192 to 131072
Outputs:
- block_out: bfloat16 [16384, 768], P(('fsdp', 'rep'))
- token_grad: bfloat16 [16384, 768], P(('fsdp', 'rep'))
- weight_gradients: float32 [112, 256, 256], P('fsdp')
- first_new: float32 [112, 256, 256], P('fsdp')
- second_new: float32 [112, 256, 256], P('fsdp')
- weights_new: float32 [112, 256, 256], P('fsdp')
- weights_low: bfloat16 [112, 256, 256], P('fsdp')
- gain_first_new: float32 [2, 768], replicated
- gain_second_new: float32 [2, 768], replicated
- gains_new: float32 [2, 768], replicated
The draws below stay inside these ranges and needn't reach their ends.
Inputs may be any that keep to these rules, and one draw needn't show every extreme that they name: `block_slot_index`: distinct slot numbers. Slot s lies on fsdp device s // 14; slots that no block names are empty. `left_basis`: every 256 x 256 block is orthogonal. `right_basis`: every 256 x 256 block is orthogonal. `second_moment`: Positive.
All inputs are finite; a program needn't handle non-finite values.
Results may differ from the reference program's by a relative error of at most 0.015.
Values may be sent and summed in bfloat16 or wider, within the bound.
No kernel may reach another device: no remote copies, remote signals or barrier semaphores. Data moves between devices by JAX's collectives and lax.ppermute only.
A program may use at most 384 MiB of HBM per device.

```python
import math
import jax
import jax.numpy as jnp
import numpy as np
from jax import lax

D = 768
HEADS = 12
HEAD_DIM = 64
FF = 2048
SEQ = 256
BLOCK_ORDER = 256
STEP = 10
ROWS = 64
TOKENS = 16384
BLOCK_TOTAL = 108
SLOT_COUNT = 112


def slot_lookup_table(key):
    key_center, key_ordering = jax.random.split(jax.random.fold_in(key, 101))
    center_part = jax.random.permutation(key_center, SLOT_COUNT - 2) + 1
    released_slots = center_part[:SLOT_COUNT - BLOCK_TOTAL]
    filled_mask = jnp.ones((SLOT_COUNT,), jnp.int32).at[released_slots].set(0)
    occupied = jnp.nonzero(filled_mask, size=BLOCK_TOTAL)[0].astype(jnp.int32)
    return occupied[jax.random.permutation(key_ordering, BLOCK_TOTAL)]


def slot_kinds(key):
    block_counts = [D // BLOCK_ORDER * (D // BLOCK_ORDER)] * 4 + [D // BLOCK_ORDER * (FF // BLOCK_ORDER)] * 3
    kind_code_list = []
    for kind_code, count_here in enumerate(block_counts):
        kind_code_list.append(jnp.full((count_here,), kind_code, jnp.int32))
    return jnp.full((SLOT_COUNT,), 7, jnp.int32).at[slot_lookup_table(key)].set(jnp.concatenate(kind_code_list))


def kind_lookup(kind_code_list, table_values):
    return jnp.array(table_values, jnp.float32)[kind_code_list]


def gradient_size(kind_code_list):
    return TOKENS ** 0.5 * kind_lookup(kind_code_list, [0.7, 0.7, 0.7, 0.2, 0.5, 0.6, 0.45, 0.5])


def trig_values():
    freq_index = jnp.arange(BLOCK_ORDER, dtype=jnp.float32)[:, None]
    sample_index = jnp.arange(BLOCK_ORDER, dtype=jnp.float32)[None, :]
    table_here = (2.0 / BLOCK_ORDER) ** 0.5 * jnp.cos(jnp.pi * (2.0 * sample_index + 1.0) * (2.0 * freq_index) / (4.0 * BLOCK_ORDER))
    return table_here * jnp.where(freq_index == 0.0, 0.5 ** 0.5, 1.0)


def signed_bases(key):
    key_ordering, key_row_list, key_columns = jax.random.split(key, 3)

    def single_ordering(slot_key):
        return jax.random.permutation(slot_key, BLOCK_ORDER)
    ordering_list = jax.vmap(single_ordering)(jax.random.split(key_ordering, SLOT_COUNT))
    row_sign_values = jax.random.rademacher(key_row_list, (SLOT_COUNT, BLOCK_ORDER, 1), jnp.float32)
    column_signs = jax.random.rademacher(key_columns, (SLOT_COUNT, 1, BLOCK_ORDER), jnp.float32)
    return row_sign_values * trig_values()[ordering_list] * column_signs


def draw_block_slot_index(key, part):
    return slot_lookup_table(key)


def draw_weights(key, part):
    kind_code_list = slot_kinds(key)
    key = jax.random.fold_in(key, 2)
    spread = kind_lookup(kind_code_list, [D ** (-0.5), D ** (-0.5), D ** (-0.5), (D // 16) ** (-0.5), D ** (-0.5), D ** (-0.5), (FF // 2) ** (-0.5), D ** (-0.5)])
    noise_samples = jax.random.normal(key, (SLOT_COUNT, BLOCK_ORDER, BLOCK_ORDER), jnp.float32)
    return spread[:, None, None] * noise_samples


def draw_first_moment(key, part):
    kind_code_list = slot_kinds(key)
    key = jax.random.fold_in(key, 3)
    return gradient_size(kind_code_list)[:, None, None] * jax.random.normal(key, (SLOT_COUNT, BLOCK_ORDER, BLOCK_ORDER), jnp.float32)


def draw_second_moment(key, part):
    kind_code_list = slot_kinds(key)
    key = jax.random.fold_in(key, 4)
    factor_matrix = jnp.exp(jax.random.uniform(key, (SLOT_COUNT, BLOCK_ORDER, BLOCK_ORDER), jnp.float32, jnp.log(0.5), jnp.log(8.0)))
    sizes_here = gradient_size(kind_code_list)
    return (sizes_here * sizes_here)[:, None, None] * factor_matrix


def draw_left_basis(key, part):
    key = jax.random.fold_in(key, 5)
    return signed_bases(key)


def draw_right_basis(key, part):
    key = jax.random.fold_in(key, 6)
    return signed_bases(key)


def block_scale(rng, extent, cuts, least, top_value):
    def one(axis_at, shards_of):
        heights = jax.random.uniform(jax.random.fold_in(jax.random.fold_in(rng, 6), axis_at), (shards_of,), jnp.float32, least / len(cuts), top_value / len(cuts))
        return jnp.repeat(jnp.exp(heights), extent[axis_at] // shards_of).reshape((-1,) + (1,) * (len(extent) - axis_at - 1))

    loudness = one(*cuts[0])
    for cut in cuts[1:]:
        loudness = loudness * one(*cut)
    return loudness


def length_profile(number_of, total, reach, skew):
    loads = [(1 << 20) // math.isqrt(grade ** skew) + 1 for grade in range(2, number_of + 1)]
    rest, counts = total - reach - (number_of - 1), [1] * (number_of - 1)
    while rest > 0:
        candidates = [i for i in range(number_of - 1) if counts[i] < reach]
        mass, remaining = sum([loads[i] for i in candidates]), rest
        for i in candidates:
            more = min(reach - counts[i], max(1, remaining * loads[i] // mass), rest)
            counts[i] = counts[i] + more
            rest = rest - more
    return np.array([reach] + counts)


def uneven_parts(own_key, number_of, total, bound, skew):
    if number_of == 2:
        one = jax.random.randint(own_key, (), max(1, total - bound), min(bound, total - 1) + 1)
        return jnp.stack([one, total - one])
    tallies = jnp.asarray(length_profile(number_of, total, bound, skew), jnp.int32)
    couples = (number_of - 1) // 2
    giver, sink = tallies[1:1 + 2 * couples:2], tallies[2:2 + 2 * couples:2]
    room = jnp.minimum(giver - 1, bound - sink)
    passed = jax.random.randint(jax.random.fold_in(own_key, 1), (couples,), 0, 1 << 20) % (room + 1)
    tallies = tallies.at[1:1 + 2 * couples:2].set(giver - passed).at[2:2 + 2 * couples:2].set(sink + passed)
    return tallies[jax.random.permutation(jax.random.fold_in(own_key, 2), number_of)]


def centred(key, shape, scale, reach, shards=(), kind=jnp.bfloat16):
    level = block_scale(key, shape, shards, -0.22, 0.18) if shards else 1.0
    drawn = jax.random.normal(key, shape, jnp.float32) * scale * level
    return jnp.minimum(jnp.maximum(drawn, -reach), reach).astype(kind)


def setup_inputs(seed: int = 0) -> dict:
    key_list = jax.random.split(jax.random.key(seed), 13)
    tokens = centred(key_list[0], (TOKENS, D), 1.0, 6.0, ((0, 32),))
    cotangent = centred(key_list[1], (TOKENS, D), 1.0, 6.0, ((0, 32),))
    segment_ids = jax.vmap(lambda own: jnp.searchsorted(jnp.cumsum(uneven_parts(own, max(3, SEQ // 128), SEQ, SEQ // 2, 0)), jnp.arange(SEQ), side="right"))(jax.random.split(key_list[2], ROWS)).reshape((ROWS, SEQ)).astype(jnp.int32)
    block_slot_index = draw_block_slot_index(jax.random.fold_in(key_list[12], 71), 0)
    weights = draw_weights(jax.random.fold_in(key_list[12], 71), 0)
    first_moment = draw_first_moment(jax.random.fold_in(key_list[12], 71), 0)
    second_moment = draw_second_moment(jax.random.fold_in(key_list[12], 71), 0)
    left_basis = draw_left_basis(jax.random.fold_in(key_list[12], 71), 0)
    right_basis = draw_right_basis(jax.random.fold_in(key_list[12], 71), 0)
    norm_gains = jnp.clip(1.0 + 0.15 * jax.random.normal(key_list[9], (2, D), jnp.float32), 0.25, 1.75)
    gain_first = centred(key_list[10], (2, D), (TOKENS ** 0.5), 768.0, (), jnp.float32)
    gain_second = jnp.clip(jnp.exp(jax.random.uniform(key_list[11], (2, D), jnp.float32, math.log(8192.0), math.log(131072.0))), 8192.0, 131072.0)
    return {"tokens": tokens, "cotangent": cotangent, "segment_ids": segment_ids, "block_slot_index": block_slot_index, "weights": weights, "first_moment": first_moment, "second_moment": second_moment, "left_basis": left_basis, "right_basis": right_basis, "norm_gains": norm_gains, "gain_first": gain_first, "gain_second": gain_second}


@jax.custom_vjp
def low(v):
    return lax.optimization_barrier(v.astype(jnp.bfloat16)).astype(jnp.float32)

@jax.custom_vjp
def low_back(v):
    return v

def low_keep(v):
    return (low(v), None)

def low_pass(kept, grad):
    return (grad,)

def back_keep(v):
    return (v, None)

def back_low(kept, grad):
    return (low(grad),)
low.defvjp(low_keep, low_pass)
low_back.defvjp(back_keep, back_low)
NORM_EPS = 1e-05
ROPE_BASE = 10000.0
BETA_ONE = 0.5
BETA_TWO = 0.5
ADAM_EPS = 1e-08
RATE = 0.03
GAIN_RATE = 0.4
DECAY = 0.01
MASKED = -1e+30

def matrix_shapes():
    return [(D, D), (D, D), (D, D), (D, D), (D, FF), (D, FF), (FF, D)]

def to_matrices(blocks):
    result = []
    offset = 0
    for height, breadth in matrix_shapes():
        grid_rows = height // BLOCK_ORDER
        grid_cols = breadth // BLOCK_ORDER
        block_count = grid_rows * grid_cols
        block_grid = blocks[offset:offset + block_count].reshape(grid_rows, grid_cols, BLOCK_ORDER, BLOCK_ORDER)
        result.append(block_grid.transpose(0, 2, 1, 3).reshape(height, breadth))
        offset = offset + block_count
    return result

def split_into_blocks(matrices):
    pieces = []
    for matrix in matrices:
        height, breadth = matrix.shape
        grid_rows = height // BLOCK_ORDER
        grid_cols = breadth // BLOCK_ORDER
        pieces.append(matrix.reshape(grid_rows, BLOCK_ORDER, grid_cols, BLOCK_ORDER).transpose(0, 2, 1, 3).reshape(grid_rows * grid_cols, BLOCK_ORDER, BLOCK_ORDER))
    return jnp.concatenate(pieces, axis=0)

def positions_of(segments):
    places = jnp.arange(segments.shape[0], dtype=jnp.int32)
    starts = jnp.concatenate([jnp.ones((1,), jnp.bool_), segments[1:] != segments[:-1]])
    first_place = lax.cummax(jnp.where(starts, places, 0), axis=0)
    return places - first_place

def rope_tables(positions):
    half_dim = HEAD_DIM // 2
    frequency = ROPE_BASE ** (-2.0 * jnp.arange(half_dim, dtype=jnp.float32) / HEAD_DIM)
    angles = positions.astype(jnp.float32)[:, None] * frequency[None, :]
    return (jnp.cos(angles)[:, None, :], jnp.sin(angles)[:, None, :])

def rotate(values, cosine, sine_table):
    half_dim = HEAD_DIM // 2
    lower_half = values[..., :half_dim]
    upper_half = values[..., half_dim:]
    return jnp.concatenate([lower_half * cosine - upper_half * sine_table, upper_half * cosine + lower_half * sine_table], axis=-1)

def rms_norm(values, gain):
    inv_rms = lax.rsqrt(lax.optimization_barrier(jnp.mean(values * values, axis=-1, keepdims=True)) + NORM_EPS)
    return values * inv_rms * gain

def product(operand_a, operand_b):
    return jnp.dot(operand_a, operand_b, precision=lax.Precision.HIGHEST, preferred_element_type=jnp.float32)

def split_heads(matrix):
    return matrix.reshape(matrix.shape[0], HEADS, HEAD_DIM)

def attend_block(query_block, key_heads, values, visible_block):
    raw_scores = jnp.einsum('qhd,khd->hqk', query_block, key_heads, precision=lax.Precision.HIGHEST)
    scores = low_back(raw_scores * HEAD_DIM ** (-0.5))
    scores = jnp.where(visible_block[None], scores, MASKED)
    row_max = lax.optimization_barrier(jnp.max(scores, axis=-1, keepdims=True))
    exp_scores = jnp.exp(scores - row_max)
    probabilities = low(exp_scores / lax.optimization_barrier(jnp.sum(exp_scores, axis=-1, keepdims=True)))
    return jnp.einsum('hqk,khd->qhd', probabilities, values, precision=lax.Precision.HIGHEST)

def attend_row(queries, key_heads, values, segments):
    block_rows = min(512, SEQ)
    block_count = SEQ // block_rows
    places = jnp.arange(SEQ, dtype=jnp.int32)
    visible = (segments[:, None] == segments[None, :]) & (places[None, :] <= places[:, None])

    def one_block(pieces):
        return attend_block(pieces[0], key_heads, values, pieces[1])
    mixed_heads = lax.map(jax.checkpoint(one_block), (queries.reshape(block_count, block_rows, HEADS, HEAD_DIM), visible.reshape(block_count, block_rows, SEQ)))
    return mixed_heads.reshape(SEQ, D)

def row_forward(token_row, segments, matrices, norm_gains):
    w_query, w_key, w_value, w_out, w_gate, w_up, w_down = matrices
    cosine, sine_table = rope_tables(positions_of(segments))
    queries = low(rotate(split_heads(low_back(product(token_row, w_query))), cosine, sine_table))
    key_heads = low(rotate(split_heads(low_back(product(token_row, w_key))), cosine, sine_table))
    values = low(split_heads(low_back(product(token_row, w_value))))
    attended = low(low_back(attend_row(queries, key_heads, values, segments)))
    hidden_one = token_row + low_back(product(attended, w_out))
    normed_one = rms_norm(hidden_one, norm_gains[0])
    normed_low = low(normed_one)
    gate_proj = low_back(product(normed_low, w_gate))
    up_proj = low_back(product(normed_low, w_up))
    activation = low(jax.nn.silu(gate_proj) * up_proj)
    hidden_two = normed_one + low_back(product(activation, w_down))
    return rms_norm(hidden_two, norm_gains[1])

def adam_blocks(grads, weights, first_moment, second_moment, left_basis, right_basis):
    highest = lax.Precision.HIGHEST
    turned = jnp.einsum('sij,sik->sjk', left_basis, grads, precision=highest)
    turned = jnp.einsum('sjk,skl->sjl', turned, right_basis, precision=highest)
    first_new = BETA_ONE * first_moment + (1.0 - BETA_ONE) * turned
    second_new = BETA_TWO * second_moment + (1.0 - BETA_TWO) * turned * turned
    step_ratio = first_new / (1.0 - BETA_ONE ** STEP) / (jnp.sqrt(second_new / (1.0 - BETA_TWO ** STEP)) + ADAM_EPS)
    rotated_back = jnp.einsum('sij,sjk->sik', left_basis, step_ratio, precision=highest)
    rotated_back = jnp.einsum('sik,slk->sil', rotated_back, right_basis, precision=highest)
    weights_new = weights - RATE * (rotated_back + DECAY * weights)
    return (first_new, second_new, weights_new)

def adam_plain(grads, values, first_moment, second_moment):
    first_new = BETA_ONE * first_moment + (1.0 - BETA_ONE) * grads
    second_new = BETA_TWO * second_moment + (1.0 - BETA_TWO) * grads * grads
    step_ratio = first_new / (1.0 - BETA_ONE ** STEP) / (jnp.sqrt(second_new / (1.0 - BETA_TWO ** STEP)) + ADAM_EPS)
    return (first_new, second_new, values - GAIN_RATE * step_ratio)

def reference(tokens, cotangent, segment_ids, block_slot_index, weights, first_moment, second_moment, left_basis, right_basis, norm_gains, gain_first, gain_second):
    matrices = to_matrices(weights[block_slot_index])
    group_rows = math.gcd(ROWS, max(1, 4096 // SEQ))
    token_groups = tokens.astype(jnp.float32).reshape(ROWS // group_rows, group_rows, SEQ, D)
    segment_groups = segment_ids.reshape(ROWS // group_rows, group_rows, SEQ)

    def forward(token_values, matrix_values, gain_values):
        lowered = [low(matrix) for matrix in matrix_values]

        def group_forward(token_block, segment_block):
            return jax.vmap(row_forward, in_axes=(0, 0, None, None))(token_block, segment_block, lowered, gain_values)
        checked = jax.checkpoint(group_forward)

        def scan_step(scan_carry, pieces):
            return (scan_carry, checked(pieces[0], pieces[1]))
        final_carry, result = lax.scan(scan_step, jnp.zeros((), jnp.float32), (token_values, segment_groups))
        return result
    block_out, pullback = jax.vjp(forward, token_groups, matrices, norm_gains)
    token_grad, matrix_gradients, gain_grads = pullback(cotangent.astype(jnp.float32).reshape(ROWS // group_rows, group_rows, SEQ, D))
    weight_gradients = jnp.zeros((SLOT_COUNT, BLOCK_ORDER, BLOCK_ORDER), jnp.float32).at[block_slot_index].set(split_into_blocks(matrix_gradients))
    first_new, second_new, weights_new = adam_blocks(weight_gradients, weights, first_moment, second_moment, left_basis, right_basis)
    gain_first_new, gain_second_new, gains_new = adam_plain(gain_grads, norm_gains, gain_first, gain_second)
    return (block_out.reshape(TOKENS, D).astype(jnp.bfloat16), token_grad.reshape(TOKENS, D).astype(jnp.bfloat16), weight_gradients, first_new, second_new, weights_new, weights_new.astype(jnp.bfloat16), gain_first_new, gain_second_new, gains_new)
```

```python
import functools

import jax
import jax.numpy as jnp
import numpy as np
from jax import lax
from jax.experimental import pallas as pl
from jax.experimental.pallas import tpu as pltpu
from jax.sharding import PartitionSpec as P

D = 768
HEADS = 12
HEAD_DIM = 64
FF = 2048
BLOCK_ORDER = 256
STEP = 10


NORM_EPS = 1e-05
ROPE_BASE = 10000.0
BETA_ONE = 0.5
BETA_TWO = 0.5
ADAM_EPS = 1e-08
RATE = 0.03
GAIN_RATE = 0.4
DECAY = 0.01
MASKED = -1e30

B = BLOCK_ORDER
BF16 = jnp.bfloat16
F32 = jnp.float32
MIB = 1024 * 1024

LEFT_X, LEFT_A, LEFT_Y, LEFT_ACT = 0, D // B, 2 * D // B, 3 * D // B
LEFT_ROWS = 3 * D + FF
RIGHT_Q, RIGHT_K, RIGHT_V, RIGHT_O = 0, D, 2 * D, 3 * D
RIGHT_G, RIGHT_U, RIGHT_D = 4 * D, 4 * D + FF, 4 * D + 2 * FF
RIGHT_COLS = 5 * D + 2 * FF


def matrix_table():
    return [
        (D // B, D // B, LEFT_X, RIGHT_Q // B),
        (D // B, D // B, LEFT_X, RIGHT_K // B),
        (D // B, D // B, LEFT_X, RIGHT_V // B),
        (D // B, D // B, LEFT_A, RIGHT_O // B),
        (D // B, FF // B, LEFT_Y, RIGHT_G // B),
        (D // B, FF // B, LEFT_Y, RIGHT_U // B),
        (FF // B, D // B, LEFT_ACT, RIGHT_D // B),
    ]


def factor_tables():
    lefts, rights = [], []
    for grid_rows, grid_cols, left, right in matrix_table():
        for i in range(grid_rows):
            for j in range(grid_cols):
                lefts.append(left + i)
                rights.append(right + j)
    return np.array(lefts, np.int32), np.array(rights, np.int32)


def positions_of(segments):
    places = jnp.arange(segments.shape[-1], dtype=jnp.int32)[None, :]
    starts = jnp.concatenate(
        [jnp.ones((segments.shape[0], 1), jnp.bool_), segments[:, 1:] != segments[:, :-1]], axis=1
    )
    first_place = lax.cummax(jnp.where(starts, places, 0), axis=1)
    return places - first_place


def dot_nn(a, b):
    return jnp.dot(a, b, preferred_element_type=F32)


def dot_nt(a, b):
    return lax.dot_general(a, b, (((1,), (1,)), ((), ())), preferred_element_type=F32)


def half_swap(values, low_half):
    return jnp.where(low_half, pltpu.roll(values, 96, 1), pltpu.roll(values, 32, 1))


def layer_kernel(
    micro,
    slots,
    piece_slots,
    index_ref,
    left_ref,
    right_ref,
    x_ref,
    dy_ref,
    bias_ref,
    cos_ref,
    sin_ref,
    cos_t_ref,
    sin_t_ref,
    gains_ref,
    *rest,
):
    pieces = rest[: len(piece_slots)]
    out_ref, token_grad_ref, gain_ref, grads_ref = rest[len(piece_slots) : len(piece_slots) + 4]
    (
        w_qkv,
        w_o,
        w_gu,
        w_d,
        lefts,
        rights,
        q_scr,
        k_scr,
        v_scr,
        p_scr,
        a_scr,
        act_scr,
        cg_scr,
        cu_scr,
        y1_scr,
        y1_low_scr,
        h1_scr,
        dh2_scr,
        r1_scr,
        ring,
        w_sems,
        ring_sems,
    ) = rest[len(piece_slots) + 4 :]
    seq = bias_ref.shape[1]
    tokens = micro * seq

    def fetch(block, target, row, col, sem):
        slot = index_ref[block]
        first = 0
        for piece, count in zip(pieces, piece_slots):

            @pl.when((slot >= first) & (slot < first + count))
            def _(piece=piece, first=first):
                pltpu.make_async_copy(
                    piece.at[slot - first],
                    target.at[
                        pl.ds(pl.multiple_of(row * B, B), B), pl.ds(pl.multiple_of(col * B, B), B)
                    ],
                    sem,
                ).start()

            first += count

    def fetch_matrix(first_block, grid_rows, grid_cols, target, col_offset, sem):
        def one(t, carry):
            i = t // grid_cols
            j = t - i * grid_cols
            fetch(first_block + t, target, i, j + col_offset, sem)
            return carry

        lax.fori_loop(0, grid_rows * grid_cols, one, 0)

    nd, nf = D // B, FF // B
    for m in range(3):
        fetch_matrix(m * nd * nd, nd, nd, w_qkv, m * nd, w_sems.at[0])
    fetch_matrix(3 * nd * nd, nd, nd, w_o, 0, w_sems.at[1])
    for m in range(2):
        fetch_matrix(4 * nd * nd + m * nd * nf, nd, nf, w_gu, m * nf, w_sems.at[2])
    fetch_matrix(4 * nd * nd + 2 * nd * nf, nf, nd, w_d, 0, w_sems.at[3])

    def wait_for(target, sem):
        pltpu.make_async_copy(target, target, sem).wait()

    lefts[0:D, :] = x_ref[...].T
    lane = lax.broadcasted_iota(jnp.int32, (1, 128), 1)
    low_half = lax.rem(lane, HEAD_DIM) < HEAD_DIM // 2
    head_lanes = [lane < HEAD_DIM, lane >= HEAD_DIM]

    def of_head(values, h):
        return jnp.where(head_lanes[h], values, jnp.zeros_like(values))

    wait_for(w_qkv, w_sems.at[0])

    def attend(jb, carry):
        def columns(offset):
            return pl.ds(pl.multiple_of(offset + jb * B, B), B)

        x = x_ref[...]
        q_raw = dot_nn(x, w_qkv[:, columns(0)])
        k_raw = dot_nn(x, w_qkv[:, columns(D)])
        v_raw = dot_nn(x, w_qkv[:, columns(2 * D)])
        cosine = cos_ref[...]
        sine = sin_ref[...]
        for sub in range(2):
            part = slice(sub * 128, sub * 128 + 128)
            slab = pl.ds(pl.multiple_of(jb * B + sub * 128, 128), 128)
            q = q_raw[:, part]
            k = k_raw[:, part]
            q = ((q * cosine + half_swap(q, low_half) * sine) * HEAD_DIM**-0.5).astype(BF16)
            k = (k * cosine + half_swap(k, low_half) * sine).astype(BF16)
            v = v_raw[:, part].astype(BF16)
            q_scr[:, slab] = q
            k_scr[:, slab] = k
            v_scr[:, slab] = v
            for r in range(micro):
                rows = slice(r * seq, (r + 1) * seq)
                v_t = v[rows].T
                outs = []
                for h in range(2):
                    scores = dot_nt(k[rows], of_head(q[rows], h)) + bias_ref[r]
                    top = jnp.max(scores, axis=0, keepdims=True)
                    exps = jnp.exp(scores - top)
                    total = jnp.sum(exps, axis=0, keepdims=True)
                    probs = (exps * (1.0 / total)).astype(BF16)
                    p_scr[(jb * 2 + sub) * 2 * micro + 2 * r + h] = probs
                    outs.append(dot_nn(v_t[h * HEAD_DIM : (h + 1) * HEAD_DIM], probs))
                a_t = jnp.concatenate(outs, axis=0).astype(BF16)
                lefts[pl.ds(pl.multiple_of(D + jb * B + sub * 128, 128), 128), rows] = a_t
                a_scr[rows, slab] = a_t.T
        return carry

    lax.fori_loop(0, nd, attend, 0)

    wait_for(w_o, w_sems.at[1])
    for r in range(micro):
        rows = slice(r * seq, (r + 1) * seq)
        h1 = x_ref[rows, :].astype(F32) + dot_nn(a_scr[rows, :], w_o[...])
        r1 = lax.rsqrt(jnp.mean(h1 * h1, axis=-1, keepdims=True) + NORM_EPS)
        y1 = h1 * r1 * gains_ref[0:1, :]
        y1_low = y1.astype(BF16)
        h1_scr[rows, :] = h1
        r1_scr[rows, :] = r1
        y1_scr[rows, :] = y1
        y1_low_scr[rows, :] = y1_low
        lefts[2 * D : 3 * D, rows] = y1_low.T

    wait_for(w_gu, w_sems.at[2])

    def feed(j, carry):
        y1_low = y1_low_scr[...]
        cols = pl.ds(pl.multiple_of(j * B, B), B)
        gate = dot_nn(y1_low, w_gu[:, cols])
        up = dot_nn(y1_low, w_gu[:, pl.ds(pl.multiple_of(FF + j * B, B), B)])
        sig = 1.0 / (1.0 + jnp.exp(-gate))
        silu = gate * sig
        act = (silu * up).astype(BF16)
        act_scr[:, cols] = act
        cu_scr[:, cols] = silu.astype(BF16)
        cg_scr[:, cols] = (up * sig * (1.0 + gate * (1.0 - sig))).astype(BF16)
        lefts[pl.ds(pl.multiple_of(3 * D + j * B, B), B), :] = act.T
        return carry

    lax.fori_loop(0, nf, feed, 0)

    wait_for(w_d, w_sems.at[3])
    gain_two = jnp.zeros((1, D), F32)
    for r in range(micro):
        rows = slice(r * seq, (r + 1) * seq)
        h2 = y1_scr[rows, :] + dot_nn(act_scr[rows, :], w_d[...])
        r2 = lax.rsqrt(jnp.mean(h2 * h2, axis=-1, keepdims=True) + NORM_EPS)
        scaled = h2 * r2
        gain = gains_ref[1:2, :]
        out_ref[rows, :] = (scaled * gain).astype(BF16)
        dy = dy_ref[rows, :].astype(F32)
        gain_two += jnp.sum(dy * scaled, axis=0, keepdims=True)
        dyg = dy * gain
        dh2 = r2 * (dyg - scaled * jnp.mean(scaled * dyg, axis=-1, keepdims=True))
        dh2_scr[rows, :] = dh2
        rights[rows, RIGHT_D:] = dh2.astype(BF16)
    gain_ref[1:2, :] = gain_two

    def feed_back(j, carry):
        cols = pl.ds(pl.multiple_of(j * B, B), B)
        dact = dot_nt(rights[:, RIGHT_D:], w_d[cols, :])
        rights[:, pl.ds(pl.multiple_of(RIGHT_G + j * B, B), B)] = (
            dact * cg_scr[:, cols].astype(F32)
        ).astype(BF16)
        rights[:, pl.ds(pl.multiple_of(RIGHT_U + j * B, B), B)] = (
            dact * cu_scr[:, cols].astype(F32)
        ).astype(BF16)
        return carry

    lax.fori_loop(0, nf, feed_back, 0)

    def feed_in(j, carry):
        cols = pl.ds(pl.multiple_of(j * B, B), B)
        dh2_scr[:, cols] += dot_nt(rights[:, RIGHT_G:RIGHT_D], w_gu[cols, :])
        return carry

    lax.fori_loop(0, nd, feed_in, 0)

    gain_one = jnp.zeros((1, D), F32)
    for r in range(micro):
        rows = slice(r * seq, (r + 1) * seq)
        dy1 = dh2_scr[rows, :]
        r1 = r1_scr[rows, :]
        scaled = h1_scr[rows, :] * r1
        gain_one += jnp.sum(dy1 * scaled, axis=0, keepdims=True)
        dyg = dy1 * gains_ref[0:1, :]
        dh1 = r1 * (dyg - scaled * jnp.mean(scaled * dyg, axis=-1, keepdims=True))
        h1_scr[rows, :] = dh1
        do = dh1.astype(BF16)
        rights[rows, RIGHT_O : RIGHT_O + D] = do
        a_scr[rows, :] = dot_nt(do, w_o[...]).astype(BF16)
    gain_ref[0:1, :] = gain_one

    def attend_back(jb, carry):
        for sub in range(2):
            slab = pl.ds(pl.multiple_of(jb * B + sub * 128, 128), 128)
            for r in range(micro):
                rows = slice(r * seq, (r + 1) * seq)
                q = q_scr[rows, slab]
                k = k_scr[rows, slab]
                v = v_scr[rows, slab]
                da = a_scr[rows, slab]
                k_t = k.T
                dv = jnp.zeros((seq, 128), F32)
                dk = jnp.zeros((seq, 128), F32)
                dq_t = []
                for h in range(2):
                    probs = p_scr[(jb * 2 + sub) * 2 * micro + 2 * r + h]
                    da_h = of_head(da, h)
                    probs_wide = probs.astype(F32)
                    dprobs = dot_nt(v, da_h)
                    weighted = probs_wide * dprobs
                    row_sum = jnp.sum(weighted, axis=0, keepdims=True)
                    ds = (weighted - probs_wide * row_sum).astype(BF16)
                    dv += dot_nn(probs, da_h)
                    dk += dot_nn(ds, of_head(q, h))
                    dq_h = dot_nn(k_t[h * HEAD_DIM : (h + 1) * HEAD_DIM], ds) * HEAD_DIM**-0.5
                    low, high = dq_h[: HEAD_DIM // 2], dq_h[HEAD_DIM // 2 :]
                    cosine = cos_t_ref[:, rows]
                    sine = sin_t_ref[:, rows]
                    dq_t.append(low * cosine + high * sine)
                    dq_t.append(high * cosine - low * sine)
                dq = jnp.concatenate(dq_t, axis=0).astype(BF16).T
                dk = dk * cos_ref[rows, :] - half_swap(dk, low_half) * sin_ref[rows, :]
                rights[rows, slab] = dq
                rights[rows, pl.ds(pl.multiple_of(RIGHT_K + jb * B + sub * 128, 128), 128)] = (
                    dk.astype(BF16)
                )
                rights[rows, pl.ds(pl.multiple_of(RIGHT_V + jb * B + sub * 128, 128), 128)] = (
                    dv.astype(BF16)
                )
        return carry

    lax.fori_loop(0, nd, attend_back, 0)

    def token_back(j, carry):
        cols = pl.ds(pl.multiple_of(j * B, B), B)
        token_grad_ref[:, cols] = (
            h1_scr[:, cols] + dot_nt(rights[:, : 3 * D], w_qkv[cols, :])
        ).astype(BF16)
        return carry

    lax.fori_loop(0, nd, token_back, 0)

    group = ring.shape[1]
    groups = slots // group

    def ring_copy(g, half):
        return pltpu.make_async_copy(
            ring.at[half], grads_ref.at[pl.ds(g * group, group)], ring_sems.at[half]
        )

    def weigh(g, carry):
        half = lax.rem(g, 2)

        @pl.when(g >= 2)
        def _():
            ring_copy(g - 2, half).wait()

        for n in range(group):
            slot = g * group + n
            left = jnp.maximum(left_ref[slot], 0)
            grad = dot_nn(
                lefts[pl.ds(pl.multiple_of(left * B, B), B), :],
                rights[:, pl.ds(pl.multiple_of(right_ref[slot] * B, B), B)],
            )
            keep = jnp.where(left_ref[slot] >= 0, 1.0, 0.0)
            ring[half, n] = (grad * keep).astype(BF16)
        ring_copy(g, half).start()
        return carry

    lax.fori_loop(0, groups, weigh, 0)
    for g in range(max(0, groups - 2), groups):
        ring_copy(g, g % 2).wait()


def run_layer(tokens, cotangent, segment_ids, block_slot_index, norm_gains, pieces, slots):
    micro, seq = segment_ids.shape
    count = micro * seq
    half_dim = HEAD_DIM // 2
    frequency = ROPE_BASE ** (-2.0 * jnp.arange(half_dim, dtype=F32) / HEAD_DIM)
    angles = positions_of(segment_ids).reshape(count).astype(F32)[:, None] * frequency[None, :]
    cosine, sine = jnp.cos(angles), jnp.sin(angles)
    cos_wide = jnp.tile(cosine, (1, 4))
    sin_wide = jnp.concatenate([-sine, sine, -sine, sine], axis=1)
    places = jnp.arange(seq, dtype=jnp.int32)
    visible = (segment_ids[:, :, None] == segment_ids[:, None, :]) & (
        places[:, None] <= places[None, :]
    )
    bias = jnp.where(visible, 0.0, MASKED).astype(F32)
    left_table, right_table = factor_tables()
    slot_left = jnp.full((slots,), -1, jnp.int32).at[block_slot_index].set(left_table)
    slot_right = jnp.zeros((slots,), jnp.int32).at[block_slot_index].set(right_table)
    group = 4
    assert slots % group == 0

    vmem = pl.BlockSpec(memory_space=pltpu.VMEM)
    smem = pl.BlockSpec(memory_space=pltpu.SMEM)
    hbm = pl.BlockSpec(memory_space=pl.ANY)
    return pl.pallas_call(
        functools.partial(layer_kernel, micro, slots, [p.shape[0] for p in pieces]),
        out_shape=(
            jax.ShapeDtypeStruct((count, D), BF16),
            jax.ShapeDtypeStruct((count, D), BF16),
            jax.ShapeDtypeStruct((2, D), F32),
            jax.ShapeDtypeStruct((slots, B, B), BF16),
        ),
        in_specs=[smem] * 3 + [vmem] * 8 + [hbm] * len(pieces),
        out_specs=(vmem, vmem, vmem, hbm),
        scratch_shapes=[
            pltpu.VMEM((D, 3 * D), BF16),
            pltpu.VMEM((D, D), BF16),
            pltpu.VMEM((D, 2 * FF), BF16),
            pltpu.VMEM((FF, D), BF16),
            pltpu.VMEM((LEFT_ROWS, count), BF16),
            pltpu.VMEM((count, RIGHT_COLS), BF16),
            pltpu.VMEM((count, D), BF16),
            pltpu.VMEM((count, D), BF16),
            pltpu.VMEM((count, D), BF16),
            pltpu.VMEM((HEADS * micro, seq, seq), BF16),
            pltpu.VMEM((count, D), BF16),
            pltpu.VMEM((count, FF), BF16),
            pltpu.VMEM((count, FF), BF16),
            pltpu.VMEM((count, FF), BF16),
            pltpu.VMEM((count, D), F32),
            pltpu.VMEM((count, D), BF16),
            pltpu.VMEM((count, D), F32),
            pltpu.VMEM((count, D), F32),
            pltpu.VMEM((count, 1), F32),
            pltpu.VMEM((2, group, B, B), BF16),
            pltpu.SemaphoreType.DMA((4,)),
            pltpu.SemaphoreType.DMA((2,)),
        ],
        compiler_params=pltpu.CompilerParams(vmem_limit_bytes=60 * MIB),
        cost_estimate=pl.CostEstimate(
            flops=23_000_000_000, bytes_accessed=32_000_000, transcendentals=3_000_000
        ),
        name="layer",
    )(
        block_slot_index,
        slot_left,
        slot_right,
        tokens,
        cotangent,
        bias,
        cos_wide,
        sin_wide,
        cosine.T,
        sine.T,
        norm_gains,
        *pieces,
    )


def split_two(values):
    high = values.astype(BF16)
    return high, (values - high.astype(F32)).astype(BF16)


def dot_split(dot, a, b):
    a_high, a_low = a
    b_high, b_low = b
    total = dot(a_high, b_high)
    if b_low is not None:
        total = total + dot(a_high, b_low)
    if a_low is not None:
        total = total + dot(a_low, b_high)
    return total


def adam_kernel(
    grad_ref, weight_ref, first_ref, second_ref, left_ref, right_ref,
    grad_out, first_out, second_out, weight_out, low_out,
):
    for n in range(grad_ref.shape[0]):
        grad = grad_ref[n]
        left = left_ref[n]
        left_pair = split_two(left)
        left_t_pair = tuple(part.T for part in left_pair)
        right_pair = split_two(right_ref[n])
        grad_out[n] = grad.astype(F32)
        turned = dot_split(dot_nn, (grad, None), right_pair)
        turned = dot_split(dot_nn, left_t_pair, split_two(turned))
        first_new = BETA_ONE * first_ref[n] + (1.0 - BETA_ONE) * turned
        second_new = BETA_TWO * second_ref[n] + (1.0 - BETA_TWO) * turned * turned
        first_out[n] = first_new
        second_out[n] = second_new
        ratio = (
            first_new
            / (1.0 - BETA_ONE**STEP)
            / (jnp.sqrt(second_new / (1.0 - BETA_TWO**STEP)) + ADAM_EPS)
        )
        back = dot_split(dot_nn, left_pair, split_two(ratio))
        back = dot_split(dot_nt, split_two(back), right_pair)
        weight = weight_ref[n]
        weight_new = weight - RATE * (back + DECAY * weight)
        weight_out[n] = weight_new
        low_out[n] = weight_new.astype(BF16)


def adam_blocks(grads, weights, first_moment, second_moment, left_basis, right_basis):
    own = weights.shape[0]
    step = 2 if own % 2 == 0 else 1
    spec = pl.BlockSpec((step, B, B), lambda s: (s, 0, 0))
    wide = jax.ShapeDtypeStruct(weights.shape, F32)
    return pl.pallas_call(
        adam_kernel,
        grid=(own // step,),
        out_shape=(wide, wide, wide, wide, jax.ShapeDtypeStruct(weights.shape, BF16)),
        in_specs=[spec] * 6,
        out_specs=(spec,) * 5,
        compiler_params=pltpu.CompilerParams(vmem_limit_bytes=32 * MIB),
        cost_estimate=pl.CostEstimate(
            flops=own * 12 * 2 * B**3, bytes_accessed=own * B * B * 40, transcendentals=own * B * B
        ),
        name="adam",
    )(grads, weights, first_moment, second_moment, left_basis, right_basis)


def adam_plain(grads, values, first_moment, second_moment):
    first_new = BETA_ONE * first_moment + (1.0 - BETA_ONE) * grads
    second_new = BETA_TWO * second_moment + (1.0 - BETA_TWO) * grads * grads
    step_ratio = (
        first_new
        / (1.0 - BETA_ONE**STEP)
        / (jnp.sqrt(second_new / (1.0 - BETA_TWO**STEP)) + ADAM_EPS)
    )
    return (first_new, second_new, values - GAIN_RATE * step_ratio)


def sum_everywhere(values, axis):
    size = lax.axis_size(axis)
    if size & (size - 1):
        return lax.psum(values, axis)
    reach = 1
    while reach < size:
        values = values + lax.ppermute(values, axis, [(i, i ^ reach) for i in range(size)])
        reach *= 2
    return values


def shards(
    tokens,
    cotangent,
    segment_ids,
    block_slot_index,
    weights,
    first_moment,
    second_moment,
    left_basis,
    right_basis,
    norm_gains,
    gain_first,
    gain_second,
):
    slots = weights.shape[0] * lax.axis_size("fsdp")
    owned_low = weights.astype(BF16)
    pieces = [lax.all_gather(owned_low, "fsdp", axis=0, tiled=True)]
    block_out, token_grad, gain_grad, slot_grads = run_layer(
        tokens, cotangent, segment_ids, block_slot_index, norm_gains, pieces, slots
    )
    gain_grads = sum_everywhere(sum_everywhere(gain_grad, "fsdp"), "rep")
    owner_sums = lax.psum_scatter(slot_grads, "fsdp", scatter_dimension=0, tiled=True)
    owner_grads = lax.psum(owner_sums, "rep")
    grads_wide, first_new, second_new, weights_new, weights_low = adam_blocks(
        owner_grads, weights, first_moment, second_moment, left_basis, right_basis
    )
    gain_first_new, gain_second_new, gains_new = adam_plain(
        gain_grads, norm_gains, gain_first, gain_second
    )
    return (
        block_out,
        token_grad,
        grads_wide,
        first_new,
        second_new,
        weights_new,
        weights_low,
        gain_first_new,
        gain_second_new,
        gains_new,
    )


def solution(mesh):
    return jax.shard_map(
        shards,
        mesh=mesh,
        in_specs=(
            P(("fsdp", "rep"), None),
            P(("fsdp", "rep"), None),
            P(("fsdp", "rep"), None),
            P(),
            P("fsdp", None, None),
            P("fsdp", None, None),
            P("fsdp", None, None),
            P("fsdp", None, None),
            P("fsdp", None, None),
            P(),
            P(),
            P(),
        ),
        out_specs=(
            P(("fsdp", "rep"), None),
            P(("fsdp", "rep"), None),
            P("fsdp", None, None),
            P("fsdp", None, None),
            P("fsdp", None, None),
            P("fsdp", None, None),
            P("fsdp", None, None),
            P(),
            P(),
            P(),
        ),
        check_vma=False,
    )
```

```python
import functools

import jax
import jax.numpy as jnp
import numpy as np
from jax import lax
from jax.experimental import pallas as pl
from jax.experimental.pallas import tpu as pltpu
from jax.sharding import PartitionSpec as P

D = 768
HEADS = 12
HEAD_DIM = 64
FF = 2048
BLOCK_ORDER = 256
STEP = 10


NORM_EPS = 1e-05
ROPE_BASE = 10000.0
BETA_ONE = 0.5
BETA_TWO = 0.5
ADAM_EPS = 1e-08
RATE = 0.03
GAIN_RATE = 0.4
DECAY = 0.01
MASKED = -1e30

B = BLOCK_ORDER
BF16 = jnp.bfloat16
F32 = jnp.float32
MIB = 1024 * 1024

LEFT_X, LEFT_A, LEFT_Y, LEFT_ACT = 0, D // B, 2 * D // B, 3 * D // B
LEFT_ROWS = 3 * D + FF
RIGHT_Q, RIGHT_K, RIGHT_V, RIGHT_O = 0, D, 2 * D, 3 * D
RIGHT_G, RIGHT_U, RIGHT_D = 4 * D, 4 * D + FF, 4 * D + 2 * FF
RIGHT_COLS = 5 * D + 2 * FF


def matrix_table():
    return [
        (D // B, D // B, LEFT_X, RIGHT_Q // B),
        (D // B, D // B, LEFT_X, RIGHT_K // B),
        (D // B, D // B, LEFT_X, RIGHT_V // B),
        (D // B, D // B, LEFT_A, RIGHT_O // B),
        (D // B, FF // B, LEFT_Y, RIGHT_G // B),
        (D // B, FF // B, LEFT_Y, RIGHT_U // B),
        (FF // B, D // B, LEFT_ACT, RIGHT_D // B),
    ]


def factor_tables():
    lefts, rights = [], []
    for grid_rows, grid_cols, left, right in matrix_table():
        for i in range(grid_rows):
            for j in range(grid_cols):
                lefts.append(left + i)
                rights.append(right + j)
    return np.array(lefts, np.int32), np.array(rights, np.int32)


def positions_of(segments):
    places = jnp.arange(segments.shape[-1], dtype=jnp.int32)[None, :]
    starts = jnp.concatenate(
        [jnp.ones((segments.shape[0], 1), jnp.bool_), segments[:, 1:] != segments[:, :-1]], axis=1
    )
    first_place = lax.cummax(jnp.where(starts, places, 0), axis=1)
    return places - first_place


def dot_nn(a, b):
    return jnp.dot(a, b, preferred_element_type=F32)


def dot_nt(a, b):
    return lax.dot_general(a, b, (((1,), (1,)), ((), ())), preferred_element_type=F32)


def half_swap(values, low_half):
    return jnp.where(low_half, pltpu.roll(values, 96, 1), pltpu.roll(values, 32, 1))


def layer_kernel(
    micro,
    piece_slots,
    grad_slots,
    index_ref,
    piece_first_ref,
    grad_first_ref,
    left_ref,
    right_ref,
    x_ref,
    dy_ref,
    bias_ref,
    cos_ref,
    sin_ref,
    cos_t_ref,
    sin_t_ref,
    gains_ref,
    *rest,
):
    pieces = rest[: len(piece_slots)]
    rest = rest[len(piece_slots) :]
    out_ref, token_grad_ref, gain_ref = rest[:3]
    grad_refs = rest[3 : 3 + len(grad_slots)]
    (
        w_qkv,
        w_o,
        w_gu,
        w_d,
        lefts,
        rights,
        q_scr,
        k_scr,
        v_scr,
        p_scr,
        a_scr,
        act_scr,
        cg_scr,
        cu_scr,
        y1_scr,
        y1_low_scr,
        h1_scr,
        dh2_scr,
        r1_scr,
        ring,
        w_sems,
        ring_sems,
    ) = rest[3 + len(grad_slots) :]
    seq = bias_ref.shape[1]

    def fetch(block, target, row, col, sem):
        slot = index_ref[block]
        for number, (piece, count) in enumerate(zip(pieces, piece_slots)):
            place = slot - piece_first_ref[number]

            @pl.when((place >= 0) & (place < count))
            def _(piece=piece, place=place):
                pltpu.make_async_copy(
                    piece.at[place],
                    target.at[
                        pl.ds(pl.multiple_of(row * B, B), B), pl.ds(pl.multiple_of(col * B, B), B)
                    ],
                    sem,
                ).start()

    def fetch_matrix(first_block, grid_rows, grid_cols, target, col_offset, sem):
        def one(t, carry):
            i = t // grid_cols
            j = t - i * grid_cols
            fetch(first_block + t, target, i, j + col_offset, sem)
            return carry

        lax.fori_loop(0, grid_rows * grid_cols, one, 0)

    nd, nf = D // B, FF // B
    for m in range(3):
        fetch_matrix(m * nd * nd, nd, nd, w_qkv, m * nd, w_sems.at[0])
    fetch_matrix(3 * nd * nd, nd, nd, w_o, 0, w_sems.at[1])
    for m in range(2):
        fetch_matrix(4 * nd * nd + m * nd * nf, nd, nf, w_gu, m * nf, w_sems.at[2])
    fetch_matrix(4 * nd * nd + 2 * nd * nf, nf, nd, w_d, 0, w_sems.at[3])

    def wait_for(target, sem):
        pltpu.make_async_copy(target, target, sem).wait()

    lefts[0:D, :] = x_ref[...].T
    lane = lax.broadcasted_iota(jnp.int32, (1, 128), 1)
    low_half = lax.rem(lane, HEAD_DIM) < HEAD_DIM // 2
    head_lanes = [lane < HEAD_DIM, lane >= HEAD_DIM]

    def of_head(values, h):
        return jnp.where(head_lanes[h], values, jnp.zeros_like(values))

    wait_for(w_qkv, w_sems.at[0])

    def attend(jb, carry):
        def columns(offset):
            return pl.ds(pl.multiple_of(offset + jb * B, B), B)

        x = x_ref[...]
        q_raw = dot_nn(x, w_qkv[:, columns(0)])
        k_raw = dot_nn(x, w_qkv[:, columns(D)])
        v_raw = dot_nn(x, w_qkv[:, columns(2 * D)])
        cosine = cos_ref[...]
        sine = sin_ref[...]
        for sub in range(2):
            part = slice(sub * 128, sub * 128 + 128)
            slab = pl.ds(pl.multiple_of(jb * B + sub * 128, 128), 128)
            q = q_raw[:, part]
            k = k_raw[:, part]
            q = ((q * cosine + half_swap(q, low_half) * sine) * HEAD_DIM**-0.5).astype(BF16)
            k = (k * cosine + half_swap(k, low_half) * sine).astype(BF16)
            v = v_raw[:, part].astype(BF16)
            q_scr[:, slab] = q
            k_scr[:, slab] = k
            v_scr[:, slab] = v
            for r in range(micro):
                rows = slice(r * seq, (r + 1) * seq)
                v_t = v[rows].T
                outs = []
                for h in range(2):
                    scores = dot_nt(k[rows], of_head(q[rows], h)) + bias_ref[r]
                    top = jnp.max(scores, axis=0, keepdims=True)
                    exps = jnp.exp(scores - top)
                    total = jnp.sum(exps, axis=0, keepdims=True)
                    probs = (exps * (1.0 / total)).astype(BF16)
                    p_scr[(jb * 2 + sub) * 2 * micro + 2 * r + h] = probs
                    outs.append(dot_nn(v_t[h * HEAD_DIM : (h + 1) * HEAD_DIM], probs))
                a_t = jnp.concatenate(outs, axis=0).astype(BF16)
                lefts[pl.ds(pl.multiple_of(D + jb * B + sub * 128, 128), 128), rows] = a_t
                a_scr[rows, slab] = a_t.T
        return carry

    lax.fori_loop(0, nd, attend, 0)

    wait_for(w_o, w_sems.at[1])
    for r in range(micro):
        rows = slice(r * seq, (r + 1) * seq)
        h1 = x_ref[rows, :].astype(F32) + dot_nn(a_scr[rows, :], w_o[...])
        r1 = lax.rsqrt(jnp.mean(h1 * h1, axis=-1, keepdims=True) + NORM_EPS)
        y1 = h1 * r1 * gains_ref[0:1, :]
        y1_low = y1.astype(BF16)
        h1_scr[rows, :] = h1
        r1_scr[rows, :] = r1
        y1_scr[rows, :] = y1
        y1_low_scr[rows, :] = y1_low
        lefts[2 * D : 3 * D, rows] = y1_low.T

    wait_for(w_gu, w_sems.at[2])

    def feed(j, carry):
        y1_low = y1_low_scr[...]
        cols = pl.ds(pl.multiple_of(j * B, B), B)
        gate = dot_nn(y1_low, w_gu[:, cols])
        up = dot_nn(y1_low, w_gu[:, pl.ds(pl.multiple_of(FF + j * B, B), B)])
        sig = 1.0 / (1.0 + jnp.exp(-gate))
        silu = gate * sig
        act = (silu * up).astype(BF16)
        act_scr[:, cols] = act
        cu_scr[:, cols] = silu.astype(BF16)
        cg_scr[:, cols] = (up * sig * (1.0 + gate * (1.0 - sig))).astype(BF16)
        lefts[pl.ds(pl.multiple_of(3 * D + j * B, B), B), :] = act.T
        return carry

    lax.fori_loop(0, nf, feed, 0)

    wait_for(w_d, w_sems.at[3])
    gain_two = jnp.zeros((1, D), F32)
    for r in range(micro):
        rows = slice(r * seq, (r + 1) * seq)
        h2 = y1_scr[rows, :] + dot_nn(act_scr[rows, :], w_d[...])
        r2 = lax.rsqrt(jnp.mean(h2 * h2, axis=-1, keepdims=True) + NORM_EPS)
        scaled = h2 * r2
        gain = gains_ref[1:2, :]
        out_ref[rows, :] = (scaled * gain).astype(BF16)
        dy = dy_ref[rows, :].astype(F32)
        gain_two += jnp.sum(dy * scaled, axis=0, keepdims=True)
        dyg = dy * gain
        dh2 = r2 * (dyg - scaled * jnp.mean(scaled * dyg, axis=-1, keepdims=True))
        dh2_scr[rows, :] = dh2
        rights[rows, RIGHT_D:] = dh2.astype(BF16)
    gain_ref[1:2, :] = gain_two

    def feed_back(j, carry):
        cols = pl.ds(pl.multiple_of(j * B, B), B)
        dact = dot_nt(rights[:, RIGHT_D:], w_d[cols, :])
        rights[:, pl.ds(pl.multiple_of(RIGHT_G + j * B, B), B)] = (
            dact * cg_scr[:, cols].astype(F32)
        ).astype(BF16)
        rights[:, pl.ds(pl.multiple_of(RIGHT_U + j * B, B), B)] = (
            dact * cu_scr[:, cols].astype(F32)
        ).astype(BF16)
        return carry

    lax.fori_loop(0, nf, feed_back, 0)

    def feed_in(j, carry):
        cols = pl.ds(pl.multiple_of(j * B, B), B)
        dh2_scr[:, cols] += dot_nt(rights[:, RIGHT_G:RIGHT_D], w_gu[cols, :])
        return carry

    lax.fori_loop(0, nd, feed_in, 0)

    gain_one = jnp.zeros((1, D), F32)
    for r in range(micro):
        rows = slice(r * seq, (r + 1) * seq)
        dy1 = dh2_scr[rows, :]
        r1 = r1_scr[rows, :]
        scaled = h1_scr[rows, :] * r1
        gain_one += jnp.sum(dy1 * scaled, axis=0, keepdims=True)
        dyg = dy1 * gains_ref[0:1, :]
        dh1 = r1 * (dyg - scaled * jnp.mean(scaled * dyg, axis=-1, keepdims=True))
        h1_scr[rows, :] = dh1
        do = dh1.astype(BF16)
        rights[rows, RIGHT_O : RIGHT_O + D] = do
        a_scr[rows, :] = dot_nt(do, w_o[...]).astype(BF16)
    gain_ref[0:1, :] = gain_one

    def attend_back(jb, carry):
        for sub in range(2):
            slab = pl.ds(pl.multiple_of(jb * B + sub * 128, 128), 128)
            for r in range(micro):
                rows = slice(r * seq, (r + 1) * seq)
                q = q_scr[rows, slab]
                k = k_scr[rows, slab]
                v = v_scr[rows, slab]
                da = a_scr[rows, slab]
                k_t = k.T
                dv = jnp.zeros((seq, 128), F32)
                dk = jnp.zeros((seq, 128), F32)
                dq_t = []
                for h in range(2):
                    probs = p_scr[(jb * 2 + sub) * 2 * micro + 2 * r + h]
                    da_h = of_head(da, h)
                    probs_wide = probs.astype(F32)
                    dprobs = dot_nt(v, da_h)
                    weighted = probs_wide * dprobs
                    row_sum = jnp.sum(weighted, axis=0, keepdims=True)
                    ds = (weighted - probs_wide * row_sum).astype(BF16)
                    dv += dot_nn(probs, da_h)
                    dk += dot_nn(ds, of_head(q, h))
                    dq_h = dot_nn(k_t[h * HEAD_DIM : (h + 1) * HEAD_DIM], ds) * HEAD_DIM**-0.5
                    low, high = dq_h[: HEAD_DIM // 2], dq_h[HEAD_DIM // 2 :]
                    cosine = cos_t_ref[:, rows]
                    sine = sin_t_ref[:, rows]
                    dq_t.append(low * cosine + high * sine)
                    dq_t.append(high * cosine - low * sine)
                dq = jnp.concatenate(dq_t, axis=0).astype(BF16).T
                dk = dk * cos_ref[rows, :] - half_swap(dk, low_half) * sin_ref[rows, :]
                rights[rows, slab] = dq
                rights[rows, pl.ds(pl.multiple_of(RIGHT_K + jb * B + sub * 128, 128), 128)] = (
                    dk.astype(BF16)
                )
                rights[rows, pl.ds(pl.multiple_of(RIGHT_V + jb * B + sub * 128, 128), 128)] = (
                    dv.astype(BF16)
                )
        return carry

    lax.fori_loop(0, nd, attend_back, 0)

    def token_back(j, carry):
        cols = pl.ds(pl.multiple_of(j * B, B), B)
        token_grad_ref[:, cols] = (
            h1_scr[:, cols] + dot_nt(rights[:, : 3 * D], w_qkv[cols, :])
        ).astype(BF16)
        return carry

    lax.fori_loop(0, nd, token_back, 0)

    group = ring.shape[1]
    steps = [count // group for count in grad_slots]
    total = sum(steps)

    def ring_copy(target, half):
        return pltpu.make_async_copy(ring.at[half], target, ring_sems.at[half])

    def weigh(g, carry):
        half = lax.rem(g, 2)

        @pl.when(g >= 2)
        def _():
            ring_copy(ring.at[half], half).wait()

        first = jnp.int32(0)
        start = 0
        for number, count in enumerate(steps):
            inside = (g >= start) & (g < start + count)
            first = jnp.where(inside, grad_first_ref[number] + (g - start) * group, first)
            start += count
        for n in range(group):
            left = left_ref[first + n]
            grad = dot_nn(
                lefts[pl.ds(pl.multiple_of(jnp.maximum(left, 0) * B, B), B), :],
                rights[:, pl.ds(pl.multiple_of(right_ref[first + n] * B, B), B)],
            )
            keep = jnp.where(left >= 0, 1.0, 0.0)
            ring[half, n] = (grad * keep).astype(BF16)
        start = 0
        for target, count in zip(grad_refs, steps):

            @pl.when((g >= start) & (g < start + count))
            def _(target=target, start=start):
                ring_copy(target.at[pl.ds((g - start) * group, group)], half).start()

            start += count
        return carry

    lax.fori_loop(0, total, weigh, 0)
    for g in range(max(0, total - 2), total):
        ring_copy(ring.at[g % 2], g % 2).wait()


def run_layer(
    tokens, cotangent, segment_ids, block_slot_index, norm_gains, pieces, piece_firsts,
    grad_slots, grad_firsts, slots,
):
    micro, seq = segment_ids.shape
    count = micro * seq
    half_dim = HEAD_DIM // 2
    frequency = ROPE_BASE ** (-2.0 * jnp.arange(half_dim, dtype=F32) / HEAD_DIM)
    angles = positions_of(segment_ids).reshape(count).astype(F32)[:, None] * frequency[None, :]
    cosine, sine = jnp.cos(angles), jnp.sin(angles)
    cos_wide = jnp.tile(cosine, (1, 4))
    sin_wide = jnp.concatenate([-sine, sine, -sine, sine], axis=1)
    places = jnp.arange(seq, dtype=jnp.int32)
    visible = (segment_ids[:, :, None] == segment_ids[:, None, :]) & (
        places[:, None] <= places[None, :]
    )
    bias = jnp.where(visible, 0.0, MASKED).astype(F32)
    left_table, right_table = factor_tables()
    slot_left = jnp.full((slots,), -1, jnp.int32).at[block_slot_index].set(left_table)
    slot_right = jnp.zeros((slots,), jnp.int32).at[block_slot_index].set(right_table)
    group = next(g for g in (7, 4, 2, 1) if all(count % g == 0 for count in grad_slots))

    vmem = pl.BlockSpec(memory_space=pltpu.VMEM)
    smem = pl.BlockSpec(memory_space=pltpu.SMEM)
    hbm = pl.BlockSpec(memory_space=pl.ANY)
    return pl.pallas_call(
        functools.partial(layer_kernel, micro, [p.shape[0] for p in pieces], grad_slots),
        out_shape=(
            jax.ShapeDtypeStruct((count, D), BF16),
            jax.ShapeDtypeStruct((count, D), BF16),
            jax.ShapeDtypeStruct((2, D), F32),
            *(jax.ShapeDtypeStruct((n, B, B), BF16) for n in grad_slots),
        ),
        in_specs=[smem] * 5 + [vmem] * 8 + [hbm] * len(pieces),
        out_specs=(vmem,) * 3 + (hbm,) * len(grad_slots),
        scratch_shapes=[
            pltpu.VMEM((D, 3 * D), BF16),
            pltpu.VMEM((D, D), BF16),
            pltpu.VMEM((D, 2 * FF), BF16),
            pltpu.VMEM((FF, D), BF16),
            pltpu.VMEM((LEFT_ROWS, count), BF16),
            pltpu.VMEM((count, RIGHT_COLS), BF16),
            pltpu.VMEM((count, D), BF16),
            pltpu.VMEM((count, D), BF16),
            pltpu.VMEM((count, D), BF16),
            pltpu.VMEM((HEADS * micro, seq, seq), BF16),
            pltpu.VMEM((count, D), BF16),
            pltpu.VMEM((count, FF), BF16),
            pltpu.VMEM((count, FF), BF16),
            pltpu.VMEM((count, FF), BF16),
            pltpu.VMEM((count, D), F32),
            pltpu.VMEM((count, D), BF16),
            pltpu.VMEM((count, D), F32),
            pltpu.VMEM((count, D), F32),
            pltpu.VMEM((count, 1), F32),
            pltpu.VMEM((2, group, B, B), BF16),
            pltpu.SemaphoreType.DMA((4,)),
            pltpu.SemaphoreType.DMA((2,)),
        ],
        compiler_params=pltpu.CompilerParams(vmem_limit_bytes=60 * MIB),
        cost_estimate=pl.CostEstimate(
            flops=23_000_000_000, bytes_accessed=32_000_000, transcendentals=3_000_000
        ),
        name="layer",
    )(
        block_slot_index,
        jnp.stack(piece_firsts).astype(jnp.int32),
        jnp.stack(grad_firsts).astype(jnp.int32),
        slot_left,
        slot_right,
        tokens,
        cotangent,
        bias,
        cos_wide,
        sin_wide,
        cosine.T,
        sine.T,
        norm_gains,
        *pieces,
    )


def split_two(values):
    high = values.astype(BF16)
    return high, (values - high.astype(F32)).astype(BF16)


def dot_split(dot, a, b):
    a_high, a_low = a
    b_high, b_low = b
    total = dot(a_high, b_high)
    if b_low is not None:
        total = total + dot(a_high, b_low)
    if a_low is not None:
        total = total + dot(a_low, b_high)
    return total


def adam_kernel(
    grad_ref, weight_ref, first_ref, second_ref, left_ref, right_ref, *rest
):
    grad_out, first_out, second_out, weight_out, low_out = rest[-5:]
    for n in range(grad_ref.shape[0]):
        grad = grad_ref[n]
        left = left_ref[n]
        left_pair = split_two(left)
        left_t_pair = tuple(part.T for part in left_pair)
        right_pair = split_two(right_ref[n])
        grad_out[n] = grad.astype(F32)
        turned = dot_split(dot_nn, (grad, None), right_pair)
        turned = dot_split(dot_nn, left_t_pair, split_two(turned))
        first_new = BETA_ONE * first_ref[n] + (1.0 - BETA_ONE) * turned
        second_new = BETA_TWO * second_ref[n] + (1.0 - BETA_TWO) * turned * turned
        first_out[n] = first_new
        second_out[n] = second_new
        ratio = (
            first_new
            / (1.0 - BETA_ONE**STEP)
            / (jnp.sqrt(second_new / (1.0 - BETA_TWO**STEP)) + ADAM_EPS)
        )
        back = dot_split(dot_nn, left_pair, split_two(ratio))
        back = dot_split(dot_nt, split_two(back), right_pair)
        weight = weight_ref[n]
        weight_new = weight - RATE * (back + DECAY * weight)
        weight_out[n] = weight_new
        low_out[n] = weight_new.astype(BF16)


def adam_blocks(grads, start, state, done):
    own = state[0].shape[0]
    count = grads.shape[0]
    step = next(n for n in (2, 1) if count % n == 0 and start % n == 0)
    local = pl.BlockSpec((step, B, B), lambda s: (s, 0, 0))
    offset = pl.BlockSpec((step, B, B), lambda s: (s + start // step, 0, 0))
    hbm = pl.BlockSpec(memory_space=pl.ANY)
    wide = jax.ShapeDtypeStruct((own, B, B), F32)
    return pl.pallas_call(
        adam_kernel,
        grid=(count // step,),
        out_shape=(wide, wide, wide, wide, jax.ShapeDtypeStruct((own, B, B), BF16)),
        in_specs=[local] + [offset] * 5 + [hbm] * len(done),
        out_specs=(offset,) * 5,
        input_output_aliases={6 + n: n for n in range(len(done))},
        compiler_params=pltpu.CompilerParams(vmem_limit_bytes=32 * MIB),
        cost_estimate=pl.CostEstimate(
            flops=count * 12 * 2 * B**3,
            bytes_accessed=count * B * B * 40,
            transcendentals=count * B * B,
        ),
        name="adam",
    )(grads, *state, *done)


def adam_plain(grads, values, first_moment, second_moment):
    first_new = BETA_ONE * first_moment + (1.0 - BETA_ONE) * grads
    second_new = BETA_TWO * second_moment + (1.0 - BETA_TWO) * grads * grads
    step_ratio = (
        first_new
        / (1.0 - BETA_ONE**STEP)
        / (jnp.sqrt(second_new / (1.0 - BETA_TWO**STEP)) + ADAM_EPS)
    )
    return (first_new, second_new, values - GAIN_RATE * step_ratio)


def sum_everywhere(values, axis):
    size = lax.axis_size(axis)
    if size & (size - 1):
        return lax.psum(values, axis)
    reach = 1
    while reach < size:
        values = values + lax.ppermute(values, axis, [(i, i ^ reach) for i in range(size)])
        reach *= 2
    return values


def add_low(*terms):
    return sum(term.astype(F32) for term in terms).astype(BF16)


CORE, ACROSS, ALONG = 1, 2, 4
DIAGONAL = ACROSS | ALONG


def exchange(values, bit):
    return lax.ppermute(values, "fsdp", [(i, i ^ bit) for i in range(lax.axis_size("fsdp"))])


def gather_pieces(owned, me):
    own = owned.shape[0]
    half = own // 2
    first_half, second_half = owned[:half], owned[half:]
    pieces, firsts = [owned], [me * own]

    def keep(piece, relation, start):
        pieces.append(piece)
        firsts.append((me ^ relation) * own + start)

    def keep_both(piece, relation, start):
        keep(piece, relation, start)
        keep(exchange(piece, CORE), relation | CORE, start)

    keep(exchange(owned, CORE), CORE, 0)
    along_first = exchange(first_half, ALONG)
    across_second = exchange(second_half, ACROSS)
    along_second = exchange(second_half, ALONG)
    across_first = exchange(first_half, ACROSS)
    keep_both(along_first, ALONG, 0)
    keep_both(across_second, ACROSS, half)
    keep_both(along_second, ALONG, half)
    keep_both(across_first, ACROSS, 0)
    keep_both(exchange(along_first, ACROSS), DIAGONAL, 0)
    keep_both(exchange(across_second, ALONG), DIAGONAL, half)
    return pieces, firsts


def sum_along_line(values):
    inner = lax.ppermute(values, "rep", [(0, 1), (3, 2)])
    halfway = add_low(values, inner)
    other = lax.ppermute(halfway, "rep", [(1, 2), (2, 1)])
    total = add_low(halfway, other)
    back = lax.ppermute(total, "rep", [(1, 0), (2, 3)])
    place = lax.axis_index("rep")
    return jnp.where((place == 1) | (place == 2), total, back)


def shards(
    tokens,
    cotangent,
    segment_ids,
    block_slot_index,
    weights,
    first_moment,
    second_moment,
    left_basis,
    right_basis,
    norm_gains,
    gain_first,
    gain_second,
):
    owners = lax.axis_size("fsdp")
    own = weights.shape[0]
    slots = own * owners
    me = lax.axis_index("fsdp")
    state = (weights, first_moment, second_moment, left_basis, right_basis)
    owned_low = weights.astype(BF16)
    small = owners == 8 and lax.axis_size("rep") == 4 and own % 2 == 0

    if small:
        pieces, piece_firsts = gather_pieces(owned_low, me)
        relations = [DIAGONAL | CORE, DIAGONAL, ACROSS | CORE, ALONG | CORE, ACROSS, ALONG, CORE, 0]
        grad_slots = [own] * owners
        grad_firsts = [(me ^ relation) * own for relation in relations]
    else:
        pieces = [lax.all_gather(owned_low, "fsdp", axis=0, tiled=True)]
        piece_firsts = [jnp.int32(0)]
        grad_slots = [slots]
        grad_firsts = [jnp.int32(0)]
    block_out, token_grad, gain_grad, *grads = run_layer(
        tokens, cotangent, segment_ids, block_slot_index, norm_gains, pieces, piece_firsts,
        grad_slots, grad_firsts, slots,
    )
    done = ()
    if small:
        by_relation = dict(zip(relations, grads))
        arrived = {
            relation: exchange(by_relation[relation | CORE], CORE)
            for relation in (DIAGONAL, ACROSS, ALONG, 0)
        }

        def chip_sum(relation, start, count):
            part = slice(start, start + count)
            return add_low(by_relation[relation][part], arrived[relation][part])

        start = 0
        while start < own:
            half = min(2, (own - start) // 2)
            a, b = (start, half), (start + half, half)
            diagonal_a = exchange(chip_sum(DIAGONAL, *a), ACROSS)
            diagonal_b = exchange(chip_sum(DIAGONAL, *b), ALONG)
            across_a = exchange(chip_sum(ACROSS, *a), ACROSS)
            along_b = exchange(chip_sum(ALONG, *b), ALONG)
            across_b = exchange(add_low(chip_sum(ACROSS, *b), diagonal_b), ACROSS)
            along_a = exchange(add_low(chip_sum(ALONG, *a), diagonal_a), ALONG)
            total = jnp.concatenate(
                [
                    add_low(chip_sum(0, *a), across_a, along_a),
                    add_low(chip_sum(0, *b), across_b, along_b),
                ]
            )
            done = adam_blocks(sum_along_line(total), start, state, done)
            start += 2 * half
    else:
        owner_sums = lax.psum_scatter(grads[0], "fsdp", scatter_dimension=0, tiled=True)
        done = adam_blocks(lax.psum(owner_sums, "rep"), 0, state, done)
    grads_wide, first_new, second_new, weights_new, weights_low = done
    gain_grads = sum_everywhere(sum_everywhere(gain_grad, "fsdp"), "rep")
    gain_first_new, gain_second_new, gains_new = adam_plain(
        gain_grads, norm_gains, gain_first, gain_second
    )
    return (
        block_out,
        token_grad,
        grads_wide,
        first_new,
        second_new,
        weights_new,
        weights_low,
        gain_first_new,
        gain_second_new,
        gains_new,
    )


def solution(mesh):
    return jax.shard_map(
        shards,
        mesh=mesh,
        in_specs=(
            P(("fsdp", "rep"), None),
            P(("fsdp", "rep"), None),
            P(("fsdp", "rep"), None),
            P(),
            P("fsdp", None, None),
            P("fsdp", None, None),
            P("fsdp", None, None),
            P("fsdp", None, None),
            P("fsdp", None, None),
            P(),
            P(),
            P(),
        ),
        out_specs=(
            P(("fsdp", "rep"), None),
            P(("fsdp", "rep"), None),
            P("fsdp", None, None),
            P("fsdp", None, None),
            P("fsdp", None, None),
            P("fsdp", None, None),
            P("fsdp", None, None),
            P(),
            P(),
            P(),
        ),
        check_vma=False,
    )
```

```python
import functools

import jax
import jax.numpy as jnp
import numpy as np
from jax import lax
from jax.experimental import pallas as pl
from jax.experimental.pallas import tpu as pltpu
from jax.sharding import PartitionSpec as P

D = 768
HEADS = 12
HEAD_DIM = 64
FF = 2048
BLOCK_ORDER = 256
STEP = 10


NORM_EPS = 1e-05
ROPE_BASE = 10000.0
BETA_ONE = 0.5
BETA_TWO = 0.5
ADAM_EPS = 1e-08
RATE = 0.03
GAIN_RATE = 0.4
DECAY = 0.01
MASKED = -1e30

B = BLOCK_ORDER
BF16 = jnp.bfloat16
F32 = jnp.float32
MIB = 1024 * 1024

LEFT_X, LEFT_A, LEFT_Y, LEFT_ACT = 0, D // B, 2 * D // B, 3 * D // B
LEFT_ROWS = 3 * D + FF
RIGHT_Q, RIGHT_K, RIGHT_V, RIGHT_O = 0, D, 2 * D, 3 * D
RIGHT_G, RIGHT_U, RIGHT_D = 4 * D, 4 * D + FF, 4 * D + 2 * FF
RIGHT_COLS = 5 * D + 2 * FF


def matrix_table():
    return [
        (D // B, D // B, LEFT_X, RIGHT_Q // B),
        (D // B, D // B, LEFT_X, RIGHT_K // B),
        (D // B, D // B, LEFT_X, RIGHT_V // B),
        (D // B, D // B, LEFT_A, RIGHT_O // B),
        (D // B, FF // B, LEFT_Y, RIGHT_G // B),
        (D // B, FF // B, LEFT_Y, RIGHT_U // B),
        (FF // B, D // B, LEFT_ACT, RIGHT_D // B),
    ]


def factor_tables():
    lefts, rights = [], []
    for grid_rows, grid_cols, left, right in matrix_table():
        for i in range(grid_rows):
            for j in range(grid_cols):
                lefts.append(left + i)
                rights.append(right + j)
    return np.array(lefts, np.int32), np.array(rights, np.int32)


def positions_of(segments):
    places = jnp.arange(segments.shape[-1], dtype=jnp.int32)[None, :]
    starts = jnp.concatenate(
        [jnp.ones((segments.shape[0], 1), jnp.bool_), segments[:, 1:] != segments[:, :-1]], axis=1
    )
    first_place = lax.cummax(jnp.where(starts, places, 0), axis=1)
    return places - first_place


def dot_nn(a, b):
    return jnp.dot(a, b, preferred_element_type=F32)


def dot_nt(a, b):
    return lax.dot_general(a, b, (((1,), (1,)), ((), ())), preferred_element_type=F32)


def half_swap(values, low_half):
    return jnp.where(low_half, pltpu.roll(values, 96, 1), pltpu.roll(values, 32, 1))


def weigh_slots(count, first_ref, at, left_ref, right_ref, lefts, rights, outs, ring, sems):
    per_out = outs[0].shape[0] // count
    total = per_out * len(outs)

    def put(target, half):
        return pltpu.make_async_copy(ring.at[half, pl.ds(0, count)], target, sems.at[half])

    def run(g, carry):
        half = lax.rem(g, 2)

        @pl.when(g >= 2)
        def _():
            put(ring.at[half, pl.ds(0, count)], half).wait()

        first = first_ref[at + g]
        for n in range(count):
            left = left_ref[first + n]
            grad = dot_nn(
                lefts[pl.ds(pl.multiple_of(jnp.maximum(left, 0) * B, B), B), :],
                rights[:, pl.ds(pl.multiple_of(right_ref[first + n] * B, B), B)],
            )
            keep = jnp.where(left >= 0, 1.0, 0.0)
            ring[half, n] = (grad * keep).astype(BF16)
        for number, out in enumerate(outs):

            @pl.when((g >= number * per_out) & (g < (number + 1) * per_out))
            def _(number=number, out=out):
                put(out.at[pl.ds((g - number * per_out) * count, count)], half).start()

        return carry

    lax.fori_loop(0, total, run, 0)
    for g in range(max(0, total - 2), total):
        put(ring.at[g % 2, pl.ds(0, count)], g % 2).wait()


def layer_kernel(
    micro,
    piece_slots,
    counts,
    index_ref,
    piece_first_ref,
    slot_first_ref,
    left_ref,
    right_ref,
    x_ref,
    dy_ref,
    bias_ref,
    cos_ref,
    sin_ref,
    cos_t_ref,
    sin_t_ref,
    gains_ref,
    *rest,
):
    pieces = rest[: len(piece_slots)]
    rest = rest[len(piece_slots) :]
    out_ref, token_grad_ref, gain_ref = rest[:3]
    grad_refs, rest = rest[3 : 3 + 2 * len(counts)], rest[3 + 2 * len(counts) :]
    (
        w_qkv,
        w_o,
        w_gu,
        w_d,
        lefts,
        rights,
        q_scr,
        k_scr,
        v_scr,
        p_scr,
        a_scr,
        act_scr,
        cg_scr,
        cu_scr,
        y1_scr,
        y1_low_scr,
        h1_scr,
        dh2_scr,
        r1_scr,
        w_sems,
        ring,
        ring_sems,
    ) = rest
    seq = bias_ref.shape[1]

    def fetch(block, target, row, col, sem):
        slot = index_ref[block]
        for number, (piece, count) in enumerate(zip(pieces, piece_slots)):
            place = slot - piece_first_ref[number]

            @pl.when((place >= 0) & (place < count))
            def _(piece=piece, place=place):
                pltpu.make_async_copy(
                    piece.at[place],
                    target.at[
                        pl.ds(pl.multiple_of(row * B, B), B), pl.ds(pl.multiple_of(col * B, B), B)
                    ],
                    sem,
                ).start()

    def fetch_matrix(first_block, grid_rows, grid_cols, target, col_offset, sem):
        def one(t, carry):
            i = t // grid_cols
            j = t - i * grid_cols
            fetch(first_block + t, target, i, j + col_offset, sem)
            return carry

        lax.fori_loop(0, grid_rows * grid_cols, one, 0)

    nd, nf = D // B, FF // B
    for m in range(3):
        fetch_matrix(m * nd * nd, nd, nd, w_qkv, m * nd, w_sems.at[0])
    fetch_matrix(3 * nd * nd, nd, nd, w_o, 0, w_sems.at[1])
    for m in range(2):
        fetch_matrix(4 * nd * nd + m * nd * nf, nd, nf, w_gu, m * nf, w_sems.at[2])
    fetch_matrix(4 * nd * nd + 2 * nd * nf, nf, nd, w_d, 0, w_sems.at[3])

    def wait_for(target, sem):
        pltpu.make_async_copy(target, target, sem).wait()

    lefts[0:D, :] = x_ref[...].T
    lane = lax.broadcasted_iota(jnp.int32, (1, 128), 1)
    low_half = lax.rem(lane, HEAD_DIM) < HEAD_DIM // 2
    head_lanes = [lane < HEAD_DIM, lane >= HEAD_DIM]

    def of_head(values, h):
        return jnp.where(head_lanes[h], values, jnp.zeros_like(values))

    wait_for(w_qkv, w_sems.at[0])

    def attend(jb, carry):
        def columns(offset):
            return pl.ds(pl.multiple_of(offset + jb * B, B), B)

        x = x_ref[...]
        q_raw = dot_nn(x, w_qkv[:, columns(0)])
        k_raw = dot_nn(x, w_qkv[:, columns(D)])
        v_raw = dot_nn(x, w_qkv[:, columns(2 * D)])
        cosine = cos_ref[...]
        sine = sin_ref[...]
        for sub in range(2):
            part = slice(sub * 128, sub * 128 + 128)
            slab = pl.ds(pl.multiple_of(jb * B + sub * 128, 128), 128)
            q = q_raw[:, part]
            k = k_raw[:, part]
            q = ((q * cosine + half_swap(q, low_half) * sine) * HEAD_DIM**-0.5).astype(BF16)
            k = (k * cosine + half_swap(k, low_half) * sine).astype(BF16)
            v = v_raw[:, part].astype(BF16)
            q_scr[:, slab] = q
            k_scr[:, slab] = k
            v_scr[:, slab] = v
            for r in range(micro):
                rows = slice(r * seq, (r + 1) * seq)
                v_t = v[rows].T
                outs = []
                for h in range(2):
                    scores = dot_nt(k[rows], of_head(q[rows], h)) + bias_ref[r]
                    top = jnp.max(scores, axis=0, keepdims=True)
                    exps = jnp.exp(scores - top)
                    total = jnp.sum(exps, axis=0, keepdims=True)
                    probs = (exps * (1.0 / total)).astype(BF16)
                    p_scr[(jb * 2 + sub) * 2 * micro + 2 * r + h] = probs
                    outs.append(dot_nn(v_t[h * HEAD_DIM : (h + 1) * HEAD_DIM], probs))
                a_t = jnp.concatenate(outs, axis=0).astype(BF16)
                lefts[pl.ds(pl.multiple_of(D + jb * B + sub * 128, 128), 128), rows] = a_t
                a_scr[rows, slab] = a_t.T
        return carry

    lax.fori_loop(0, nd, attend, 0)

    wait_for(w_o, w_sems.at[1])
    for r in range(micro):
        rows = slice(r * seq, (r + 1) * seq)
        h1 = x_ref[rows, :].astype(F32) + dot_nn(a_scr[rows, :], w_o[...])
        r1 = lax.rsqrt(jnp.mean(h1 * h1, axis=-1, keepdims=True) + NORM_EPS)
        y1 = h1 * r1 * gains_ref[0:1, :]
        y1_low = y1.astype(BF16)
        h1_scr[rows, :] = h1
        r1_scr[rows, :] = r1
        y1_scr[rows, :] = y1
        y1_low_scr[rows, :] = y1_low
        lefts[2 * D : 3 * D, rows] = y1_low.T

    wait_for(w_gu, w_sems.at[2])

    def feed(j, carry):
        y1_low = y1_low_scr[...]
        cols = pl.ds(pl.multiple_of(j * B, B), B)
        gate = dot_nn(y1_low, w_gu[:, cols])
        up = dot_nn(y1_low, w_gu[:, pl.ds(pl.multiple_of(FF + j * B, B), B)])
        sig = 1.0 / (1.0 + jnp.exp(-gate))
        silu = gate * sig
        act = (silu * up).astype(BF16)
        act_scr[:, cols] = act
        cu_scr[:, cols] = silu.astype(BF16)
        cg_scr[:, cols] = (up * sig * (1.0 + gate * (1.0 - sig))).astype(BF16)
        lefts[pl.ds(pl.multiple_of(3 * D + j * B, B), B), :] = act.T
        return carry

    lax.fori_loop(0, nf, feed, 0)

    wait_for(w_d, w_sems.at[3])
    gain_two = jnp.zeros((1, D), F32)
    for r in range(micro):
        rows = slice(r * seq, (r + 1) * seq)
        h2 = y1_scr[rows, :] + dot_nn(act_scr[rows, :], w_d[...])
        r2 = lax.rsqrt(jnp.mean(h2 * h2, axis=-1, keepdims=True) + NORM_EPS)
        scaled = h2 * r2
        gain = gains_ref[1:2, :]
        out_ref[rows, :] = (scaled * gain).astype(BF16)
        dy = dy_ref[rows, :].astype(F32)
        gain_two += jnp.sum(dy * scaled, axis=0, keepdims=True)
        dyg = dy * gain
        dh2 = r2 * (dyg - scaled * jnp.mean(scaled * dyg, axis=-1, keepdims=True))
        dh2_scr[rows, :] = dh2
        rights[rows, RIGHT_D:] = dh2.astype(BF16)
    gain_ref[1:2, :] = gain_two

    def feed_back(j, carry):
        cols = pl.ds(pl.multiple_of(j * B, B), B)
        dact = dot_nt(rights[:, RIGHT_D:], w_d[cols, :])
        rights[:, pl.ds(pl.multiple_of(RIGHT_G + j * B, B), B)] = (
            dact * cg_scr[:, cols].astype(F32)
        ).astype(BF16)
        rights[:, pl.ds(pl.multiple_of(RIGHT_U + j * B, B), B)] = (
            dact * cu_scr[:, cols].astype(F32)
        ).astype(BF16)
        return carry

    lax.fori_loop(0, nf, feed_back, 0)

    def feed_in(j, carry):
        cols = pl.ds(pl.multiple_of(j * B, B), B)
        dh2_scr[:, cols] += dot_nt(rights[:, RIGHT_G:RIGHT_D], w_gu[cols, :])
        return carry

    lax.fori_loop(0, nd, feed_in, 0)

    gain_one = jnp.zeros((1, D), F32)
    for r in range(micro):
        rows = slice(r * seq, (r + 1) * seq)
        dy1 = dh2_scr[rows, :]
        r1 = r1_scr[rows, :]
        scaled = h1_scr[rows, :] * r1
        gain_one += jnp.sum(dy1 * scaled, axis=0, keepdims=True)
        dyg = dy1 * gains_ref[0:1, :]
        dh1 = r1 * (dyg - scaled * jnp.mean(scaled * dyg, axis=-1, keepdims=True))
        h1_scr[rows, :] = dh1
        do = dh1.astype(BF16)
        rights[rows, RIGHT_O : RIGHT_O + D] = do
        a_scr[rows, :] = dot_nt(do, w_o[...]).astype(BF16)
    gain_ref[0:1, :] = gain_one

    def attend_back(jb, carry):
        for sub in range(2):
            slab = pl.ds(pl.multiple_of(jb * B + sub * 128, 128), 128)
            for r in range(micro):
                rows = slice(r * seq, (r + 1) * seq)
                q = q_scr[rows, slab]
                k = k_scr[rows, slab]
                v = v_scr[rows, slab]
                da = a_scr[rows, slab]
                k_t = k.T
                dv = jnp.zeros((seq, 128), F32)
                dk = jnp.zeros((seq, 128), F32)
                dq_t = []
                for h in range(2):
                    probs = p_scr[(jb * 2 + sub) * 2 * micro + 2 * r + h]
                    da_h = of_head(da, h)
                    probs_wide = probs.astype(F32)
                    dprobs = dot_nt(v, da_h)
                    weighted = probs_wide * dprobs
                    row_sum = jnp.sum(weighted, axis=0, keepdims=True)
                    ds = (weighted - probs_wide * row_sum).astype(BF16)
                    dv += dot_nn(probs, da_h)
                    dk += dot_nn(ds, of_head(q, h))
                    dq_h = dot_nn(k_t[h * HEAD_DIM : (h + 1) * HEAD_DIM], ds) * HEAD_DIM**-0.5
                    low, high = dq_h[: HEAD_DIM // 2], dq_h[HEAD_DIM // 2 :]
                    cosine = cos_t_ref[:, rows]
                    sine = sin_t_ref[:, rows]
                    dq_t.append(low * cosine + high * sine)
                    dq_t.append(high * cosine - low * sine)
                dq = jnp.concatenate(dq_t, axis=0).astype(BF16).T
                dk = dk * cos_ref[rows, :] - half_swap(dk, low_half) * sin_ref[rows, :]
                rights[rows, slab] = dq
                rights[rows, pl.ds(pl.multiple_of(RIGHT_K + jb * B + sub * 128, 128), 128)] = (
                    dk.astype(BF16)
                )
                rights[rows, pl.ds(pl.multiple_of(RIGHT_V + jb * B + sub * 128, 128), 128)] = (
                    dv.astype(BF16)
                )
        return carry

    lax.fori_loop(0, nd, attend_back, 0)

    def token_back(j, carry):
        cols = pl.ds(pl.multiple_of(j * B, B), B)
        token_grad_ref[:, cols] = (
            h1_scr[:, cols] + dot_nt(rights[:, : 3 * D], w_qkv[cols, :])
        ).astype(BF16)
        return carry

    lax.fori_loop(0, nd, token_back, 0)

    at = 0
    for group, count in enumerate(counts):
        outs = grad_refs[2 * group : 2 * group + 2]
        weigh_slots(
            count, slot_first_ref, at, left_ref, right_ref, lefts, rights, outs, ring, ring_sems
        )
        at += 2 * outs[0].shape[0] // count


def run_layer(
    tokens, cotangent, segment_ids, block_slot_index, norm_gains, tables, pieces, piece_firsts,
    slot_tables, slot_firsts, counts,
):
    micro, seq = segment_ids.shape
    count = micro * seq
    grads = [
        jax.ShapeDtypeStruct((slots * len(firsts) // 2, B, B), BF16)
        for slots, firsts in zip(counts, slot_firsts)
        for _ in range(2)
    ]
    vmem = pl.BlockSpec(memory_space=pltpu.VMEM)
    smem = pl.BlockSpec(memory_space=pltpu.SMEM)
    hbm = pl.BlockSpec(memory_space=pl.ANY)
    return pl.pallas_call(
        functools.partial(layer_kernel, micro, [p.shape[0] for p in pieces], counts),
        out_shape=(
            jax.ShapeDtypeStruct((count, D), BF16),
            jax.ShapeDtypeStruct((count, D), BF16),
            jax.ShapeDtypeStruct((2, D), F32),
            *grads,
        ),
        in_specs=[smem] * 5 + [vmem] * 8 + [hbm] * len(pieces),
        out_specs=(vmem,) * 3 + (hbm,) * len(grads),
        scratch_shapes=[
            pltpu.VMEM((D, 3 * D), BF16),
            pltpu.VMEM((D, D), BF16),
            pltpu.VMEM((D, 2 * FF), BF16),
            pltpu.VMEM((FF, D), BF16),
            pltpu.VMEM((LEFT_ROWS, count), BF16),
            pltpu.VMEM((count, RIGHT_COLS), BF16),
            pltpu.VMEM((count, D), BF16),
            pltpu.VMEM((count, D), BF16),
            pltpu.VMEM((count, D), BF16),
            pltpu.VMEM((HEADS * micro, seq, seq), BF16),
            pltpu.VMEM((count, D), BF16),
            pltpu.VMEM((count, FF), BF16),
            pltpu.VMEM((count, FF), BF16),
            pltpu.VMEM((count, FF), BF16),
            pltpu.VMEM((count, D), F32),
            pltpu.VMEM((count, D), BF16),
            pltpu.VMEM((count, D), F32),
            pltpu.VMEM((count, D), F32),
            pltpu.VMEM((count, 1), F32),
            pltpu.SemaphoreType.DMA((4,)),
            pltpu.VMEM((2, max(counts), B, B), BF16),
            pltpu.SemaphoreType.DMA((2,)),
        ],
        compiler_params=pltpu.CompilerParams(vmem_limit_bytes=56 * MIB),
        cost_estimate=pl.CostEstimate(
            flops=23_000_000_000, bytes_accessed=32_000_000, transcendentals=3_000_000
        ),
        name="layer",
    )(
        block_slot_index,
        jnp.stack(piece_firsts).astype(jnp.int32),
        jnp.stack([first for firsts in slot_firsts for first in firsts]).astype(jnp.int32),
        *slot_tables,
        tokens,
        cotangent,
        *tables,
        norm_gains,
        *pieces,
    )


def layer_tables(segment_ids):
    micro, seq = segment_ids.shape
    count = micro * seq
    half_dim = HEAD_DIM // 2
    frequency = ROPE_BASE ** (-2.0 * jnp.arange(half_dim, dtype=F32) / HEAD_DIM)
    angles = positions_of(segment_ids).reshape(count).astype(F32)[:, None] * frequency[None, :]
    cosine, sine = jnp.cos(angles), jnp.sin(angles)
    cos_wide = jnp.tile(cosine, (1, 4))
    sin_wide = jnp.concatenate([-sine, sine, -sine, sine], axis=1)
    places = jnp.arange(seq, dtype=jnp.int32)
    visible = (segment_ids[:, :, None] == segment_ids[:, None, :]) & (
        places[:, None] <= places[None, :]
    )
    bias = jnp.where(visible, 0.0, MASKED).astype(F32)
    return bias, cos_wide, sin_wide, cosine.T, sine.T


def slot_tables(block_slot_index, slots):
    left_table, right_table = factor_tables()
    slot_left = jnp.full((slots,), -1, jnp.int32).at[block_slot_index].set(left_table)
    slot_right = jnp.zeros((slots,), jnp.int32).at[block_slot_index].set(right_table)
    return slot_left, slot_right


def split_two(values):
    high = values.astype(BF16)
    return high, (values - high.astype(F32)).astype(BF16)


def adam_kernel(
    inner_ref, whole_ref, outward_ref, weight_ref, first_ref, second_ref, left_ref, right_ref, *rest
):
    grad_out, first_out, second_out, weight_out, low_out = rest[-5:]
    inner = inner_ref[0] != 0
    for n in range(weight_ref.shape[0]):
        block = pl.ds(n * B, B)
        grad = jnp.where(inner, whole_ref[block, :], outward_ref[block, :])
        left, left_rest = split_two(left_ref[n])
        right, right_rest = split_two(right_ref[n])
        grad_out[n] = grad.astype(F32)
        turned = (dot_nn(grad, right) + dot_nn(grad, right_rest)).astype(BF16)
        turned = dot_nn(left.T, turned) + dot_nn(left_rest.T, turned)
        first_new = BETA_ONE * first_ref[n] + (1.0 - BETA_ONE) * turned
        second_new = BETA_TWO * second_ref[n] + (1.0 - BETA_TWO) * turned * turned
        first_out[n] = first_new
        second_out[n] = second_new
        ratio = (
            first_new
            / (1.0 - BETA_ONE**STEP)
            / (jnp.sqrt(second_new / (1.0 - BETA_TWO**STEP)) + ADAM_EPS)
        )
        back = dot_nt(dot_nn(left, ratio.astype(BF16)).astype(BF16), right)
        weight = weight_ref[n]
        weight_new = weight - RATE * (back + DECAY * weight)
        weight_out[n] = weight_new
        low_out[n] = weight_new.astype(BF16)


def adam_blocks(whole, outward, inner, start, count, state, done):
    own = state[0].shape[0]
    step = next(n for n in (2, 1) if count % n == 0 and start % n == 0)
    local = pl.BlockSpec((step * B, B), lambda s: (s, 0))
    offset = pl.BlockSpec((step, B, B), lambda s: (s + start // step, 0, 0))
    hbm = pl.BlockSpec(memory_space=pl.ANY)
    smem = pl.BlockSpec(memory_space=pltpu.SMEM)
    wide = jax.ShapeDtypeStruct((own, B, B), F32)
    return pl.pallas_call(
        adam_kernel,
        grid=(count // step,),
        out_shape=(wide, wide, wide, wide, jax.ShapeDtypeStruct((own, B, B), BF16)),
        in_specs=[smem] + [local] * 2 + [offset] * 5 + [hbm] * len(done),
        out_specs=(offset,) * 5,
        input_output_aliases={8 + n: n for n in range(len(done))},
        compiler_params=pltpu.CompilerParams(vmem_limit_bytes=60 * MIB),
        cost_estimate=pl.CostEstimate(
            flops=count * 6 * 2 * B**3,
            bytes_accessed=count * B * B * 42,
            transcendentals=count * B * B,
        ),
        name="adam",
    )(inner.reshape(1), whole, outward, *state, *done)


def adam_plain(grads, values, first_moment, second_moment):
    first_new = BETA_ONE * first_moment + (1.0 - BETA_ONE) * grads
    second_new = BETA_TWO * second_moment + (1.0 - BETA_TWO) * grads * grads
    step_ratio = (
        first_new
        / (1.0 - BETA_ONE**STEP)
        / (jnp.sqrt(second_new / (1.0 - BETA_TWO**STEP)) + ADAM_EPS)
    )
    return (first_new, second_new, values - GAIN_RATE * step_ratio)


def sum_everywhere(values, axis):
    size = lax.axis_size(axis)
    if size & (size - 1):
        return lax.psum(values, axis)
    reach = 1
    while reach < size:
        values = values + lax.ppermute(values, axis, [(i, i ^ reach) for i in range(size)])
        reach *= 2
    return values


def add_low(*terms):
    return sum(term.astype(F32) for term in terms).astype(BF16)


CORE, ACROSS, ALONG = 1, 2, 4
DIAGONAL = ACROSS | ALONG


def exchange(values, bit):
    return lax.ppermute(values, "fsdp", [(i, i ^ bit) for i in range(lax.axis_size("fsdp"))])


def after(values, *others):
    return lax.optimization_barrier((values, *others))[0]


def gather_pieces(weights, me, make_tables):
    own = weights.shape[0]
    half = own // 2
    first_half = weights[:half].astype(BF16)
    second_half = weights[half:].astype(BF16)
    pieces, firsts = [], []

    def keep(piece, relation, start):
        pieces.append(piece)
        firsts.append((me ^ relation) * own + start)

    def keep_both(piece, relation, start):
        keep(piece, relation, start)
        keep(exchange(piece, CORE), relation | CORE, start)

    along_first = exchange(first_half, ALONG)
    across_second = exchange(second_half, ACROSS)
    along_second = exchange(second_half, ALONG)
    across_first = exchange(first_half, ACROSS)
    tables = make_tables(along_first, across_second)
    (along_first, across_second), tables = lax.optimization_barrier(
        ((along_first, across_second), tables)
    )
    keep_both(first_half, 0, 0)
    keep_both(second_half, 0, half)
    keep_both(along_first, ALONG, 0)
    keep_both(across_second, ACROSS, half)
    diagonal_first = exchange(along_first, ACROSS)
    diagonal_second = exchange(across_second, ALONG)
    keep_both(along_second, ALONG, half)
    keep_both(across_first, ACROSS, 0)
    keep_both(diagonal_first, DIAGONAL, 0)
    keep_both(diagonal_second, DIAGONAL, half)
    return pieces, firsts, tables


class Plan:
    def __init__(self):
        self.tasks = {}

    def core(self, name, needs, run):
        self.tasks[name] = (True, needs, run)

    def send(self, name, needs, run):
        self.tasks[name] = (False, needs, run)

    def run(self, order):
        assert sorted(order) == sorted(self.tasks)
        values, last = {}, None
        for name in order:
            on_core, needs, run = self.tasks[name]
            inputs = [values[n] for n in needs]
            if last is not None:
                *inputs, _ = lax.optimization_barrier((*inputs, last))
            values[name] = run(*inputs)
            if on_core:
                last = jax.tree.leaves(values[name])[0]
        return values


GROUPS = (((4, 1),), ((6, 2), (4, 2)))
ORDER = (
    "grads0 grads1 core0 gain_far near_sum0 near0 core1 near_sum1 near1 gain1 "
    "far_sum0_0 far0_0 plane_sum0_0 inward0_0a halfway0_0a middle0_0a far_sum1_0 far1_0 far_sum1_1 far1_1 gain_near "
    "whole0_0a outward0_0a plane_sum1_0 inward1_0a inward1_0b plane_sum1_1 inward1_1a inward1_1b gain2 gain_core "
    "halfway1_0a middle1_0a halfway1_0b middle1_0b gain3 gain_pair whole1_0a outward1_0a halfway1_1a middle1_1a "
    "whole1_0b outward1_0b halfway1_1b middle1_1b adam0_0a whole1_1a outward1_1a whole1_1b outward1_1b gain4 gain_line "
    "adam1_0a adam1_0b gain5 adam1_1a adam1_1b"
).split()


def group_sizes():
    return [sum(size for size, _ in sets) for sets in GROUPS]


def core_neighbours(me):
    near = jnp.where((me & CORE) == 0, ACROSS, ALONG)
    return near, DIAGONAL ^ near


def group_firsts(me, own):
    near, far = core_neighbours(me)
    relations = [DIAGONAL | CORE, far | CORE, near | CORE, CORE, DIAGONAL, near, far, 0]
    firsts, start = [], 0
    for size in group_sizes():
        firsts.append([(me ^ relation) * own + start for relation in relations])
        start += size
    return firsts


def flat(blocks):
    return blocks.reshape(-1, B)


def reduce_and_step(me, own, grads, state, gain_grad):
    plan = Plan()
    owners = lax.axis_size("fsdp")
    near_pairs = [(i, i ^ (ALONG if i & CORE else ACROSS)) for i in range(owners)]
    far_pairs = [(i, i ^ (ACROSS if i & CORE else ALONG)) for i in range(owners)]
    place = lax.axis_index("rep")
    inner = ((place == 1) | (place == 2)).astype(jnp.int32)
    done = ()

    start = 0
    for number, sets in enumerate(GROUPS):
        total = sum(size for size, _ in sets)

        def name(text, number=number):
            return text + str(number)

        both = [name("grads"), name("core")]

        def chip(pair, arrived, first, last):
            return flat(pair[1][first:last]), flat(arrived[first:last])

        plan.core(
            name("grads"), [],
            lambda pair=grads[2 * number : 2 * number + 2]: pair,
        )
        plan.send(name("core"), [name("grads")], lambda pair: exchange(pair[0], CORE))
        plan.core(
            name("near_sum"), both,
            lambda pair, arrived, total=total: add_low(*chip(pair, arrived, 0, 2 * total)),
        )
        plan.send(
            name("near"), [name("near_sum")], lambda t: lax.ppermute(t, "fsdp", near_pairs)
        )
        inside = 0
        for member, (size, parts) in enumerate(sets):

            def at(text, number=number, member=member):
                return "%s%d_%d" % (text, number, member)

            def far_sum(pair, arrived, r, inside=inside, size=size, total=total):
                first = 2 * total + inside
                return add_low(
                    *chip(pair, arrived, first, first + size), r[inside * B : (inside + size) * B]
                )

            plan.core(at("far_sum"), both + [name("near")], far_sum)
            plan.send(
                at("far"), [at("far_sum")], lambda t: lax.ppermute(t, "fsdp", far_pairs)
            )
            firsts = [size * p // parts for p in range(parts + 1)]

            def plane_sum(pair, arrived, r, q, inside=inside, total=total, firsts=firsts):
                sums = []
                for a, b in zip(firsts[:-1], firsts[1:]):
                    first, last = inside + a, inside + b
                    sums.append(
                        add_low(
                            *chip(pair, arrived, 3 * total + first, 3 * total + last),
                            r[(total + first) * B : (total + last) * B],
                            q[a * B : b * B],
                        )
                    )
                return sums

            plan.core(at("plane_sum"), both + [name("near"), at("far")], plane_sum)
            for part in range(parts):

                def of(text, part=part, at=at):
                    return at(text) + "abcd"[part]

                plan.send(
                    of("inward"), [at("plane_sum")],
                    lambda t, part=part: lax.ppermute(t[part], "rep", [(0, 1), (3, 2)]),
                )
                plan.core(
                    of("halfway"), [at("plane_sum"), of("inward")],
                    lambda t, r, part=part: add_low(t[part], r),
                )
                plan.send(
                    of("middle"), [of("halfway")],
                    lambda t: lax.ppermute(t, "rep", [(1, 2), (2, 1)]),
                )
                plan.core(of("whole"), [of("halfway"), of("middle")], add_low)
                plan.send(
                    of("outward"), [of("whole")],
                    lambda t: lax.ppermute(t, "rep", [(1, 0), (2, 3)]),
                )
                first, last = firsts[part : part + 2]

                def adam(whole, outward, first=start + inside + first, count=last - first):
                    nonlocal done
                    done = adam_blocks(whole, outward, inner, first, count, state, done)
                    return done

                plan.core(of("adam"), [of("whole"), of("outward")], adam)
            inside += size
        start += total

    old = None
    line = [[(i, i ^ bit) for i in range(4)] for bit in (1, 2)]
    for n, (text, axis, pairs) in enumerate(
        (("far", "fsdp", far_pairs), ("near", "fsdp", near_pairs),
         ("core", "fsdp", [(i, i ^ CORE) for i in range(owners)]),
         ("pair", "rep", line[0]), ("line", "rep", line[1]))
    ):
        plan.send(
            "gain_" + text, [old] if old else [],
            lambda gain=gain_grad, axis=axis, pairs=pairs: lax.ppermute(gain, axis, pairs),
        )
        new = "gain" + str(n + 1)
        if old:
            plan.core(new, [old, "gain_" + text], lambda a, b: a + b)
        else:
            plan.core(new, ["gain_" + text], lambda b: gain_grad + b)
        old = new
    values = plan.run(ORDER)
    return done, values[old]


def shards(
    tokens,
    cotangent,
    segment_ids,
    block_slot_index,
    weights,
    first_moment,
    second_moment,
    left_basis,
    right_basis,
    norm_gains,
    gain_first,
    gain_second,
):
    owners = lax.axis_size("fsdp")
    own = weights.shape[0]
    slots = own * owners
    me = lax.axis_index("fsdp")
    state = (weights, first_moment, second_moment, left_basis, right_basis)
    small = owners == 8 and lax.axis_size("rep") == 4 and own == sum(group_sizes())

    def make_tables(*others):
        segments, index = segment_ids, block_slot_index
        if others:
            segments, index, *_ = lax.optimization_barrier((segments, index, *others))
        return layer_tables(segments), slot_tables(index, slots)

    if small:
        pieces, piece_firsts, (tables, slot_factors) = gather_pieces(weights, me, make_tables)
    else:
        pieces = [lax.all_gather(weights.astype(BF16), "fsdp", axis=0, tiled=True)]
        piece_firsts = [jnp.int32(0)]
        tables, slot_factors = make_tables()
    if small:
        counts = group_sizes()
        slot_firsts = group_firsts(me, own)
    else:
        counts = [next(n for n in (8, 4, 2) if slots % (2 * n) == 0)]
        slot_firsts = [[jnp.int32(first) for first in range(0, slots, counts[0])]]
    block_out, token_grad, gain_grad, *grads = run_layer(
        tokens, cotangent, segment_ids, block_slot_index, norm_gains, tables, pieces, piece_firsts,
        slot_factors, slot_firsts, counts,
    )
    if small:
        done, gain_grads = reduce_and_step(me, own, grads, state, gain_grad)
    else:
        owner_sums = lax.psum_scatter(
            jnp.concatenate(grads), "fsdp", scatter_dimension=0, tiled=True
        )
        owner_grads = flat(lax.psum(owner_sums, "rep"))
        done = adam_blocks(owner_grads, owner_grads, jnp.int32(1), 0, own, state, ())
        gain_grads = sum_everywhere(sum_everywhere(gain_grad, "fsdp"), "rep")
    grads_wide, first_new, second_new, weights_new, weights_low = done
    gain_first_new, gain_second_new, gains_new = adam_plain(
        gain_grads, norm_gains, gain_first, gain_second
    )
    return (
        block_out,
        token_grad,
        grads_wide,
        first_new,
        second_new,
        weights_new,
        weights_low,
        gain_first_new,
        gain_second_new,
        gains_new,
    )


def solution(mesh):
    return jax.shard_map(
        shards,
        mesh=mesh,
        in_specs=(
            P(("fsdp", "rep"), None),
            P(("fsdp", "rep"), None),
            P(("fsdp", "rep"), None),
            P(),
            P("fsdp", None, None),
            P("fsdp", None, None),
            P("fsdp", None, None),
            P("fsdp", None, None),
            P("fsdp", None, None),
            P(),
            P(),
            P(),
        ),
        out_specs=(
            P(("fsdp", "rep"), None),
            P(("fsdp", "rep"), None),
            P("fsdp", None, None),
            P("fsdp", None, None),
            P("fsdp", None, None),
            P("fsdp", None, None),
            P("fsdp", None, None),
            P(),
            P(),
            P(),
        ),
        check_vma=False,
    )
```

```python
import functools
import math

import jax
import jax.numpy as jnp
import numpy as np
from jax import lax
from jax.experimental import pallas as pl
from jax.experimental.pallas import tpu as pltpu
from jax.sharding import PartitionSpec as P

D = 768
HEADS = 12
HEAD_DIM = 64
FF = 2048
BLOCK_ORDER = 256
STEP = 10


NORM_EPS = 1e-05
ROPE_BASE = 10000.0
BETA_ONE = 0.5
BETA_TWO = 0.5
ADAM_EPS = 1e-08
RATE = 0.03
GAIN_RATE = 0.4
DECAY = 0.01
MASKED = -1e30

B = BLOCK_ORDER
BF16 = jnp.bfloat16
F32 = jnp.float32
MIB = 1024 * 1024

LEFT_X, LEFT_A, LEFT_Y, LEFT_ACT = 0, D // B, 2 * D // B, 3 * D // B
LEFT_ROWS = 3 * D + FF
RIGHT_Q, RIGHT_K, RIGHT_V, RIGHT_O = 0, D, 2 * D, 3 * D
RIGHT_G, RIGHT_U, RIGHT_D = 4 * D, 4 * D + FF, 4 * D + 2 * FF
RIGHT_COLS = 5 * D + 2 * FF


def matrix_table():
    return [
        (D // B, D // B, LEFT_X, RIGHT_Q // B),
        (D // B, D // B, LEFT_X, RIGHT_K // B),
        (D // B, D // B, LEFT_X, RIGHT_V // B),
        (D // B, D // B, LEFT_A, RIGHT_O // B),
        (D // B, FF // B, LEFT_Y, RIGHT_G // B),
        (D // B, FF // B, LEFT_Y, RIGHT_U // B),
        (FF // B, D // B, LEFT_ACT, RIGHT_D // B),
    ]


def factor_tables():
    lefts, rights = [], []
    for grid_rows, grid_cols, left, right in matrix_table():
        for i in range(grid_rows):
            for j in range(grid_cols):
                lefts.append(left + i)
                rights.append(right + j)
    return np.array(lefts, np.int32), np.array(rights, np.int32)


def dot_nn(a, b):
    return jnp.dot(a, b, preferred_element_type=F32)


def dot_nt(a, b):
    return lax.dot_general(a, b, (((1,), (1,)), ((), ())), preferred_element_type=F32)


def half_swap(values, low_half):
    return jnp.where(low_half, pltpu.roll(values, 96, 1), pltpu.roll(values, 32, 1))


def list_factors(index_ref, block_left_ref, block_right_ref, left_ref, right_ref):
    def clear(g, carry):
        for n in range(4):
            left_ref[4 * g + n] = -1
            right_ref[4 * g + n] = 0
        return carry

    lax.fori_loop(0, left_ref.shape[0] // 4, clear, 0)

    def enter(g, carry):
        for n in range(4):
            slot = index_ref[4 * g + n]
            left_ref[slot] = block_left_ref[4 * g + n]
            right_ref[slot] = block_right_ref[4 * g + n]
        return carry

    lax.fori_loop(0, index_ref.shape[0] // 4, enter, 0)


WEIGH_COPY = 4


def weigh_slots(slot_ref, left_ref, right_ref, lefts, rights, outs, ring, sems):
    copies = [out.shape[0] // WEIGH_COPY for out in outs]
    total = sum(copies)
    assert total % 2 == 0

    def put(target, place):
        return pltpu.make_async_copy(ring.at[place], target, sems.at[place])

    def run(g, carry):
        first_place = 2 * lax.rem(g, 2)
        for half in range(2):

            @pl.when(g >= 2)
            def _(half=half):
                put(ring.at[first_place + half], first_place + half).wait()

        for n in range(2 * WEIGH_COPY):
            slot = slot_ref[2 * g * WEIGH_COPY + n]
            left = left_ref[slot]
            grad = dot_nn(
                lefts[pl.ds(pl.multiple_of(jnp.maximum(left, 0) * B, B), B), :],
                rights[:, pl.ds(pl.multiple_of(right_ref[slot] * B, B), B)],
            )
            keep = jnp.where(left >= 0, 1.0, 0.0)
            ring[first_place + n // WEIGH_COPY, n % WEIGH_COPY] = (grad * keep).astype(BF16)
        for half in range(2):
            copy = 2 * g + half
            first = 0
            for out, count in zip(outs, copies):

                @pl.when((copy >= first) & (copy < first + count))
                def _(out=out, first=first, half=half, copy=copy):
                    at = pl.ds((copy - first) * WEIGH_COPY, WEIGH_COPY)
                    put(out.at[at], first_place + half).start()

                first += count
        return carry

    assert total >= 4
    lax.fori_loop(0, total // 2, run, 0)
    for place in range(4):
        put(ring.at[place], place).wait()


def layer_kernel(
    micro,
    own,
    piece_slots,
    out_count,
    index_ref,
    base_ref,
    slot_ref,
    block_left_ref,
    block_right_ref,
    segments_ref,
    segments_t_ref,
    x_ref,
    dy_ref,
    gains_ref,
    *rest,
):
    pieces = rest[: len(piece_slots)]
    rest = rest[len(piece_slots) :]
    out_ref, token_grad_ref, gain_ref = rest[:3]
    grad_refs, rest = rest[3 : 3 + out_count], rest[3 + out_count :]
    (
        w_qkv,
        w_o,
        w_gu,
        w_d,
        lefts,
        rights,
        q_scr,
        k_scr,
        v_scr,
        p_scr,
        a_scr,
        act_scr,
        cg_scr,
        cu_scr,
        y1_scr,
        y1_low_scr,
        h1_scr,
        dh2_scr,
        r1_scr,
        w_sems,
        ring,
        ring_sems,
        left_ref,
        right_ref,
        bias_ref,
        cos_ref,
        sin_ref,
        cos_t_ref,
        sin_t_ref,
    ) = rest
    seq = segments_ref.shape[1]

    starts = [sum(piece_slots[:n]) for n in range(len(piece_slots) + 1)]
    reciprocal = (1 << 16) // own + 1
    assert all(slot * reciprocal >> 16 == slot // own for slot in range(starts[-1]))

    def fetch(block, target, row, col, sem):
        slot = index_ref[block]
        owner = lax.shift_right_logical(slot * reciprocal, 16)
        place = base_ref[owner] + slot - owner * own

        def among(low, high):
            if high - low > 1:
                middle = (low + high) // 2
                lax.cond(
                    place < starts[middle],
                    lambda: among(low, middle),
                    lambda: among(middle, high),
                )
            else:
                pltpu.make_async_copy(
                    pieces[low].at[place - starts[low]],
                    target.at[
                        pl.ds(pl.multiple_of(row * B, B), B), pl.ds(pl.multiple_of(col * B, B), B)
                    ],
                    sem,
                ).start()

        among(0, len(pieces))

    def fetch_matrix(first_block, grid_rows, grid_cols, target, col_offset, sem):
        def one(t, carry):
            i = t // grid_cols
            j = t - i * grid_cols
            fetch(first_block + t, target, i, j + col_offset, sem)
            return carry

        lax.fori_loop(0, grid_rows * grid_cols, one, 0)

    nd, nf = D // B, FF // B
    for m in range(3):
        fetch_matrix(m * nd * nd, nd, nd, w_qkv, m * nd, w_sems.at[0])

    list_factors(index_ref, block_left_ref, block_right_ref, left_ref, right_ref)
    half_dim = HEAD_DIM // 2
    step = lax.broadcasted_iota(jnp.int32, (half_dim, 1), 0).astype(F32)
    frequency = jnp.exp(step * (-2.0 / HEAD_DIM * math.log(ROPE_BASE)))
    keys = lax.broadcasted_iota(jnp.int32, (seq, seq), 0)
    queries = lax.broadcasted_iota(jnp.int32, (seq, seq), 1)
    for r in range(micro):
        rows = slice(r * seq, (r + 1) * seq)
        same = segments_t_ref[:, r : r + 1] == segments_ref[r : r + 1, :]
        bias_ref[r] = jnp.where(same & (keys <= queries), 0.0, MASKED)
        first = jnp.min(jnp.where(same, keys, seq), axis=0, keepdims=True)
        angles = frequency * (queries[0:1, :] - first).astype(F32)
        cosine_t, sine_t = jnp.cos(angles), jnp.sin(angles)
        cos_t_ref[:, rows] = cosine_t
        sin_t_ref[:, rows] = sine_t
        cosine, sine = cosine_t.T, sine_t.T
        cos_ref[rows, :] = jnp.concatenate([cosine] * 4, axis=1)
        sin_ref[rows, :] = jnp.concatenate([-sine, sine, -sine, sine], axis=1)

    fetch_matrix(3 * nd * nd, nd, nd, w_o, 0, w_sems.at[1])
    for m in range(2):
        fetch_matrix(4 * nd * nd + m * nd * nf, nd, nf, w_gu, m * nf, w_sems.at[2])
    fetch_matrix(4 * nd * nd + 2 * nd * nf, nf, nd, w_d, 0, w_sems.at[3])

    def wait_for(target, sem):
        pltpu.make_async_copy(target, target, sem).wait()

    lefts[0:D, :] = x_ref[...].T
    lane = lax.broadcasted_iota(jnp.int32, (1, 128), 1)
    low_half = lax.rem(lane, HEAD_DIM) < HEAD_DIM // 2
    head_lanes = [lane < HEAD_DIM, lane >= HEAD_DIM]

    def of_head(values, h):
        return jnp.where(head_lanes[h], values, jnp.zeros_like(values))

    wait_for(w_qkv, w_sems.at[0])

    def attend(jb, carry):
        def columns(offset):
            return pl.ds(pl.multiple_of(offset + jb * B, B), B)

        x = x_ref[...]
        q_raw = dot_nn(x, w_qkv[:, columns(0)])
        k_raw = dot_nn(x, w_qkv[:, columns(D)])
        v_raw = dot_nn(x, w_qkv[:, columns(2 * D)])
        cosine = cos_ref[...]
        sine = sin_ref[...]
        for sub in range(2):
            part = slice(sub * 128, sub * 128 + 128)
            slab = pl.ds(pl.multiple_of(jb * B + sub * 128, 128), 128)
            q = q_raw[:, part]
            k = k_raw[:, part]
            q = ((q * cosine + half_swap(q, low_half) * sine) * HEAD_DIM**-0.5).astype(BF16)
            k = (k * cosine + half_swap(k, low_half) * sine).astype(BF16)
            v = v_raw[:, part].astype(BF16)
            q_scr[:, slab] = q
            k_scr[:, slab] = k
            v_scr[:, slab] = v
            for r in range(micro):
                rows = slice(r * seq, (r + 1) * seq)
                v_t = v[rows].T
                outs = []
                for h in range(2):
                    scores = dot_nt(k[rows], of_head(q[rows], h)) + bias_ref[r]
                    top = jnp.max(scores, axis=0, keepdims=True)
                    exps = jnp.exp(scores - top)
                    total = jnp.sum(exps, axis=0, keepdims=True)
                    probs = (exps * (1.0 / total)).astype(BF16)
                    p_scr[(jb * 2 + sub) * 2 * micro + 2 * r + h] = probs
                    outs.append(dot_nn(v_t[h * HEAD_DIM : (h + 1) * HEAD_DIM], probs))
                a_t = jnp.concatenate(outs, axis=0).astype(BF16)
                lefts[pl.ds(pl.multiple_of(D + jb * B + sub * 128, 128), 128), rows] = a_t
                a_scr[rows, slab] = a_t.T
        return carry

    lax.fori_loop(0, nd, attend, 0)

    wait_for(w_o, w_sems.at[1])
    for r in range(micro):
        rows = slice(r * seq, (r + 1) * seq)
        h1 = x_ref[rows, :].astype(F32) + dot_nn(a_scr[rows, :], w_o[...])
        r1 = lax.rsqrt(jnp.mean(h1 * h1, axis=-1, keepdims=True) + NORM_EPS)
        y1 = h1 * r1 * gains_ref[0:1, :]
        y1_low = y1.astype(BF16)
        h1_scr[rows, :] = h1
        r1_scr[rows, :] = r1
        y1_scr[rows, :] = y1
        y1_low_scr[rows, :] = y1_low
        lefts[2 * D : 3 * D, rows] = y1_low.T

    wait_for(w_gu, w_sems.at[2])

    def feed(j, carry):
        y1_low = y1_low_scr[...]
        cols = pl.ds(pl.multiple_of(j * B, B), B)
        gate = dot_nn(y1_low, w_gu[:, cols])
        up = dot_nn(y1_low, w_gu[:, pl.ds(pl.multiple_of(FF + j * B, B), B)])
        sig = 1.0 / (1.0 + jnp.exp(-gate))
        silu = gate * sig
        act = (silu * up).astype(BF16)
        act_scr[:, cols] = act
        cu_scr[:, cols] = silu.astype(BF16)
        cg_scr[:, cols] = (up * sig * (1.0 + gate * (1.0 - sig))).astype(BF16)
        lefts[pl.ds(pl.multiple_of(3 * D + j * B, B), B), :] = act.T
        return carry

    lax.fori_loop(0, nf, feed, 0)

    wait_for(w_d, w_sems.at[3])
    gain_two = jnp.zeros((1, D), F32)
    for r in range(micro):
        rows = slice(r * seq, (r + 1) * seq)
        h2 = y1_scr[rows, :] + dot_nn(act_scr[rows, :], w_d[...])
        r2 = lax.rsqrt(jnp.mean(h2 * h2, axis=-1, keepdims=True) + NORM_EPS)
        scaled = h2 * r2
        gain = gains_ref[1:2, :]
        out_ref[rows, :] = (scaled * gain).astype(BF16)
        dy = dy_ref[rows, :].astype(F32)
        gain_two += jnp.sum(dy * scaled, axis=0, keepdims=True)
        dyg = dy * gain
        dh2 = r2 * (dyg - scaled * jnp.mean(scaled * dyg, axis=-1, keepdims=True))
        dh2_scr[rows, :] = dh2
        rights[rows, RIGHT_D:] = dh2.astype(BF16)
    gain_ref[1:2, :] = gain_two

    def feed_back(j, carry):
        cols = pl.ds(pl.multiple_of(j * B, B), B)
        dact = dot_nt(rights[:, RIGHT_D:], w_d[cols, :])
        rights[:, pl.ds(pl.multiple_of(RIGHT_G + j * B, B), B)] = (
            dact * cg_scr[:, cols].astype(F32)
        ).astype(BF16)
        rights[:, pl.ds(pl.multiple_of(RIGHT_U + j * B, B), B)] = (
            dact * cu_scr[:, cols].astype(F32)
        ).astype(BF16)
        return carry

    lax.fori_loop(0, nf, feed_back, 0)

    def feed_in(j, carry):
        cols = pl.ds(pl.multiple_of(j * B, B), B)
        dh2_scr[:, cols] += dot_nt(rights[:, RIGHT_G:RIGHT_D], w_gu[cols, :])
        return carry

    lax.fori_loop(0, nd, feed_in, 0)

    gain_one = jnp.zeros((1, D), F32)
    for r in range(micro):
        rows = slice(r * seq, (r + 1) * seq)
        dy1 = dh2_scr[rows, :]
        r1 = r1_scr[rows, :]
        scaled = h1_scr[rows, :] * r1
        gain_one += jnp.sum(dy1 * scaled, axis=0, keepdims=True)
        dyg = dy1 * gains_ref[0:1, :]
        dh1 = r1 * (dyg - scaled * jnp.mean(scaled * dyg, axis=-1, keepdims=True))
        h1_scr[rows, :] = dh1
        do = dh1.astype(BF16)
        rights[rows, RIGHT_O : RIGHT_O + D] = do
        a_scr[rows, :] = dot_nt(do, w_o[...]).astype(BF16)
    gain_ref[0:1, :] = gain_one

    def attend_back(jb, carry):
        for sub in range(2):
            slab = pl.ds(pl.multiple_of(jb * B + sub * 128, 128), 128)
            for r in range(micro):
                rows = slice(r * seq, (r + 1) * seq)
                q = q_scr[rows, slab]
                k = k_scr[rows, slab]
                v = v_scr[rows, slab]
                da = a_scr[rows, slab]
                k_t = k.T
                dv = jnp.zeros((seq, 128), F32)
                dk = jnp.zeros((seq, 128), F32)
                dq_t = []
                for h in range(2):
                    probs = p_scr[(jb * 2 + sub) * 2 * micro + 2 * r + h]
                    da_h = of_head(da, h)
                    probs_wide = probs.astype(F32)
                    dprobs = dot_nt(v, da_h)
                    weighted = probs_wide * dprobs
                    row_sum = jnp.sum(weighted, axis=0, keepdims=True)
                    ds = (weighted - probs_wide * row_sum).astype(BF16)
                    dv += dot_nn(probs, da_h)
                    dk += dot_nn(ds, of_head(q, h))
                    dq_h = dot_nn(k_t[h * HEAD_DIM : (h + 1) * HEAD_DIM], ds) * HEAD_DIM**-0.5
                    low, high = dq_h[: HEAD_DIM // 2], dq_h[HEAD_DIM // 2 :]
                    cosine = cos_t_ref[:, rows]
                    sine = sin_t_ref[:, rows]
                    dq_t.append(low * cosine + high * sine)
                    dq_t.append(high * cosine - low * sine)
                dq = jnp.concatenate(dq_t, axis=0).astype(BF16).T
                dk = dk * cos_ref[rows, :] - half_swap(dk, low_half) * sin_ref[rows, :]
                rights[rows, slab] = dq
                rights[rows, pl.ds(pl.multiple_of(RIGHT_K + jb * B + sub * 128, 128), 128)] = (
                    dk.astype(BF16)
                )
                rights[rows, pl.ds(pl.multiple_of(RIGHT_V + jb * B + sub * 128, 128), 128)] = (
                    dv.astype(BF16)
                )
        return carry

    lax.fori_loop(0, nd, attend_back, 0)

    def token_back(j, carry):
        cols = pl.ds(pl.multiple_of(j * B, B), B)
        token_grad_ref[:, cols] = (
            h1_scr[:, cols] + dot_nt(rights[:, : 3 * D], w_qkv[cols, :])
        ).astype(BF16)
        return carry

    lax.fori_loop(0, nd, token_back, 0)

    weigh_slots(slot_ref, left_ref, right_ref, lefts, rights, grad_refs, ring, ring_sems)


def run_layer(
    tokens, cotangent, segment_ids, block_slot_index, norm_gains, pieces, own, bases, slot_order,
    out_sizes,
):
    micro, seq = segment_ids.shape
    count = micro * seq
    slots = own * bases.shape[0]
    grads = [jax.ShapeDtypeStruct((size, B, B), BF16) for size in out_sizes]
    vmem = pl.BlockSpec(memory_space=pltpu.VMEM)
    smem = pl.BlockSpec(memory_space=pltpu.SMEM)
    hbm = pl.BlockSpec(memory_space=pl.ANY)
    return pl.pallas_call(
        functools.partial(layer_kernel, micro, own, [p.shape[0] for p in pieces], len(grads)),
        out_shape=(
            jax.ShapeDtypeStruct((count, D), BF16),
            jax.ShapeDtypeStruct((count, D), BF16),
            jax.ShapeDtypeStruct((2, D), F32),
            *grads,
        ),
        in_specs=[smem] * 5 + [vmem] * 5 + [hbm] * len(pieces),
        out_specs=(vmem,) * 3 + (hbm,) * len(grads),
        scratch_shapes=[
            pltpu.VMEM((D, 3 * D), BF16),
            pltpu.VMEM((D, D), BF16),
            pltpu.VMEM((D, 2 * FF), BF16),
            pltpu.VMEM((FF, D), BF16),
            pltpu.VMEM((LEFT_ROWS, count), BF16),
            pltpu.VMEM((count, RIGHT_COLS), BF16),
            pltpu.VMEM((count, D), BF16),
            pltpu.VMEM((count, D), BF16),
            pltpu.VMEM((count, D), BF16),
            pltpu.VMEM((HEADS * micro, seq, seq), BF16),
            pltpu.VMEM((count, D), BF16),
            pltpu.VMEM((count, FF), BF16),
            pltpu.VMEM((count, FF), BF16),
            pltpu.VMEM((count, FF), BF16),
            pltpu.VMEM((count, D), F32),
            pltpu.VMEM((count, D), BF16),
            pltpu.VMEM((count, D), F32),
            pltpu.VMEM((count, D), F32),
            pltpu.VMEM((count, 1), F32),
            pltpu.SemaphoreType.DMA((4,)),
            pltpu.VMEM((4, WEIGH_COPY, B, B), BF16),
            pltpu.SemaphoreType.DMA((4,)),
            pltpu.SMEM((slots,), jnp.int32),
            pltpu.SMEM((slots,), jnp.int32),
            pltpu.VMEM((micro, seq, seq), F32),
            pltpu.VMEM((count, 128), F32),
            pltpu.VMEM((count, 128), F32),
            pltpu.VMEM((HEAD_DIM // 2, count), F32),
            pltpu.VMEM((HEAD_DIM // 2, count), F32),
        ],
        compiler_params=pltpu.CompilerParams(vmem_limit_bytes=56 * MIB),
        cost_estimate=pl.CostEstimate(
            flops=23_000_000_000, bytes_accessed=32_000_000, transcendentals=3_000_000
        ),
        name="layer",
    )(
        block_slot_index,
        bases,
        slot_order,
        *(jnp.asarray(table) for table in factor_tables()),
        segment_ids,
        segment_ids.T,
        tokens,
        cotangent,
        norm_gains,
        *pieces,
    )


def split_two(values):
    high = values.astype(BF16)
    return high, (values - high.astype(F32)).astype(BF16)


def adam_kernel(steps, weight_ref, first_ref, second_ref, left_ref, right_ref, *rest):
    grad_refs = rest[: len(steps)]
    grad_out, first_out, second_out, weight_out, low_out, grads = rest[-6:]
    now, start = pl.program_id(0), 0
    for count, grad_ref in zip(steps, grad_refs):

        @pl.when((now >= start) & (now < start + count))
        def _(grad_ref=grad_ref):
            grads[...] = grad_ref[...]

        start += count
    for n in range(weight_ref.shape[0]):
        grad = grads[n * B : (n + 1) * B, :]
        left, left_rest = split_two(left_ref[n])
        right, right_rest = split_two(right_ref[n])
        grad_out[n] = grad.astype(F32)
        turned = (dot_nn(grad, right) + dot_nn(grad, right_rest)).astype(BF16)
        turned = dot_nn(left.T, turned) + dot_nn(left_rest.T, turned)
        first_new = BETA_ONE * first_ref[n] + (1.0 - BETA_ONE) * turned
        second_new = BETA_TWO * second_ref[n] + (1.0 - BETA_TWO) * turned * turned
        first_out[n] = first_new
        second_out[n] = second_new
        ratio = (
            first_new
            / (1.0 - BETA_ONE**STEP)
            / (jnp.sqrt(second_new / (1.0 - BETA_TWO**STEP)) + ADAM_EPS)
        )
        back = dot_nt(dot_nn(left, ratio.astype(BF16)).astype(BF16), right)
        weight = weight_ref[n]
        weight_new = weight - RATE * (back + DECAY * weight)
        weight_out[n] = weight_new
        low_out[n] = weight_new.astype(BF16)


def adam_blocks(grads, start, state, done):
    own = state[0].shape[0]
    step = math.gcd(2, start, *(part.shape[0] // B for part in grads))
    steps = [part.shape[0] // B // step for part in grads]
    local = []
    for number, count in enumerate(steps):
        local.append(
            pl.BlockSpec(
                (step * B, B),
                lambda s, first=sum(steps[:number]), count=count: (
                    jnp.clip(s - first, 0, count - 1),
                    0,
                ),
            )
        )
    spec = pl.BlockSpec((step, B, B), lambda s: (s + start // step, 0, 0))
    hbm = pl.BlockSpec(memory_space=pl.ANY)
    wide = jax.ShapeDtypeStruct((own, B, B), F32)
    return pl.pallas_call(
        functools.partial(adam_kernel, steps),
        grid=(sum(steps),),
        out_shape=(wide, wide, wide, wide, jax.ShapeDtypeStruct((own, B, B), BF16)),
        in_specs=[spec] * 5 + local + [hbm] * len(done),
        out_specs=(spec,) * 5,
        input_output_aliases={5 + len(local) + n: n for n in range(len(done))},
        scratch_shapes=[pltpu.VMEM((step * B, B), BF16)],
        compiler_params=pltpu.CompilerParams(vmem_limit_bytes=60 * MIB),
        cost_estimate=pl.CostEstimate(
            flops=sum(steps) * step * 12 * B**3,
            bytes_accessed=sum(steps) * step * B * B * 42,
            transcendentals=sum(steps) * step * B * B,
        ),
        name="adam",
    )(*state, *grads, *done)


def adam_plain(grads, values, first_moment, second_moment):
    first_new = BETA_ONE * first_moment + (1.0 - BETA_ONE) * grads
    second_new = BETA_TWO * second_moment + (1.0 - BETA_TWO) * grads * grads
    step_ratio = (
        first_new
        / (1.0 - BETA_ONE**STEP)
        / (jnp.sqrt(second_new / (1.0 - BETA_TWO**STEP)) + ADAM_EPS)
    )
    return (first_new, second_new, values - GAIN_RATE * step_ratio)


def sum_everywhere(values, axis):
    size = lax.axis_size(axis)
    if size & (size - 1):
        return lax.psum(values, axis)
    reach = 1
    while reach < size:
        values = values + lax.ppermute(values, axis, [(i, i ^ reach) for i in range(size)])
        reach *= 2
    return values


def add_low(*terms):
    return sum(term.astype(F32) for term in terms).astype(BF16)


CORE, ACROSS, ALONG = 1, 2, 4
DIAGONAL = ACROSS | ALONG


def exchange(values, bit):
    return lax.ppermute(values, "fsdp", [(i, i ^ bit) for i in range(lax.axis_size("fsdp"))])


def core_neighbours(me):
    near = jnp.where((me & CORE) == 0, ACROSS, ALONG)
    return near, DIAGONAL ^ near


def plane_pairs(owners):
    near = [(i, i ^ (ALONG if i & CORE else ACROSS)) for i in range(owners)]
    far = [(i, i ^ (ACROSS if i & CORE else ALONG)) for i in range(owners)]
    return near, far


def after(values, *others):
    return lax.optimization_barrier((values, *others))[0]


def gather_pieces(weights, me):
    own = weights.shape[0]
    half = own // 2
    near, far = core_neighbours(me)
    near_pairs, far_pairs = plane_pairs(lax.axis_size("fsdp"))
    mine = weights.astype(BF16)
    first_near = lax.ppermute(weights[:half].astype(BF16), "fsdp", near_pairs)
    last_near = lax.ppermute(weights[half:].astype(BF16), "fsdp", near_pairs)
    all_far = lax.ppermute(mine, "fsdp", far_pairs)
    first_diagonal = lax.ppermute(first_near, "fsdp", far_pairs)
    last_diagonal = lax.ppermute(last_near, "fsdp", far_pairs)
    pieces, relations = [], []
    for parts, relation, others in (
        ((mine,), 0, 0),
        ((first_near, last_near), near, far),
        ((all_far,), far, near),
        ((first_diagonal, last_diagonal), DIAGONAL, DIAGONAL),
    ):
        pieces += [*parts, *(exchange(part, CORE) for part in parts)]
        relations += [relation, others | CORE]
    owners = me ^ jnp.stack(relations).astype(jnp.int32)
    bases = jnp.sum(
        jnp.where(
            jnp.arange(len(relations), dtype=jnp.int32)[:, None] == owners[None, :],
            jnp.arange(len(relations), dtype=jnp.int32)[None, :] * own,
            0,
        ),
        axis=1,
    )
    return pieces, bases


class Plan:
    def __init__(self):
        self.tasks = {}

    def core(self, name, needs, run):
        self.tasks[name] = (True, needs, run)

    def send(self, name, needs, run):
        self.tasks[name] = (False, needs, run)

    def run(self, order):
        assert sorted(order) == sorted(self.tasks)
        values, last = {}, None
        for name in order:
            on_core, needs, run = self.tasks[name]
            inputs = [values[n] for n in needs]
            if last is not None:
                *inputs, _ = lax.optimization_barrier((*inputs, last))
            values[name] = run(*inputs)
            if on_core:
                last = jax.tree.leaves(values[name])[0]
        return values


GROUPS = (((4,),), ((6,), (2, 2)))
ORDER = (
    "grads0 grads1 core0 gain_far near_sum0 near0 core1 near_sum1 near1 gain1 far_sum0_0 far0_0 plane_sum0_0 "
    "inward0_0a halfway0_0a middle0_0a far_sum1_0 far1_0 far_sum1_1 far1_1 gain_near whole0_0a outward0_0a "
    "plane_sum1_0 inward1_0a plane_sum1_1 inward1_1a inward1_1b gain2 gain_core halfway1_0a middle1_0a "
    "final0_0a gain3 gain_pair halfway1_1a middle1_1a whole1_0a outward1_0a halfway1_1b middle1_1b step0 "
    "whole1_1a outward1_1a final1_0a whole1_1b outward1_1b gain4 gain_line final1_1a gain5 final1_1b step1"
).split()


def group_sizes():
    return [sum(sum(parts) for parts in sets) for sets in GROUPS]


def slot_order_of(me, own):
    near, far = core_neighbours(me)
    relations = [DIAGONAL | CORE, far | CORE, near | CORE, CORE, DIAGONAL, near, far, 0]
    slots, start = [], 0
    for size in group_sizes():
        for relation in relations:
            slots.append((me ^ relation) * own + start + jnp.arange(size, dtype=jnp.int32))
        start += size
    return jnp.concatenate(slots).astype(jnp.int32)


def flat(blocks):
    return blocks.reshape(-1, B)


def reduce_and_step(me, own, grads, state, gain_grad):
    plan = Plan()
    owners = lax.axis_size("fsdp")
    near_pairs, far_pairs = plane_pairs(owners)
    place = lax.axis_index("rep")
    inner = (place == 1) | (place == 2)
    done = ()
    start = 0

    for number, sets in enumerate(GROUPS):
        total = group_sizes()[number]

        def name(text, number=number):
            return text + str(number)

        both = [name("grads"), name("core")]
        finals = []

        def chip(pair, arrived, first, last):
            return flat(pair[1][first:last]), flat(arrived[first:last])

        plan.core(
            name("grads"), [],
            lambda pair=grads[2 * number : 2 * number + 2]: pair,
        )
        plan.send(name("core"), [name("grads")], lambda pair: exchange(pair[0], CORE))
        plan.core(
            name("near_sum"), both,
            lambda pair, arrived, total=total: add_low(*chip(pair, arrived, 0, 2 * total)),
        )
        plan.send(
            name("near"), [name("near_sum")], lambda t: lax.ppermute(t, "fsdp", near_pairs)
        )
        inside = 0
        for member, parts in enumerate(sets):
            size = sum(parts)

            def at(text, number=number, member=member):
                return "%s%d_%d" % (text, number, member)

            def far_sum(pair, arrived, r, inside=inside, size=size, total=total):
                first = 2 * total + inside
                return add_low(
                    *chip(pair, arrived, first, first + size), r[inside * B : (inside + size) * B]
                )

            plan.core(at("far_sum"), both + [name("near")], far_sum)
            plan.send(
                at("far"), [at("far_sum")], lambda t: lax.ppermute(t, "fsdp", far_pairs)
            )
            firsts = [sum(parts[:p]) for p in range(len(parts) + 1)]

            def plane_sum(pair, arrived, r, q, inside=inside, total=total, firsts=firsts):
                sums = []
                for a, b in zip(firsts[:-1], firsts[1:]):
                    first, last = inside + a, inside + b
                    sums.append(
                        add_low(
                            *chip(pair, arrived, 3 * total + first, 3 * total + last),
                            r[(total + first) * B : (total + last) * B],
                            q[a * B : b * B],
                        )
                    )
                return sums

            plan.core(at("plane_sum"), both + [name("near"), at("far")], plane_sum)
            for part in range(len(parts)):

                def of(text, part=part, at=at):
                    return at(text) + "abcd"[part]

                plan.send(
                    of("inward"), [at("plane_sum")],
                    lambda t, part=part: lax.ppermute(t[part], "rep", [(0, 1), (3, 2)]),
                )
                plan.core(
                    of("halfway"), [at("plane_sum"), of("inward")],
                    lambda t, r, part=part: add_low(t[part], r),
                )
                plan.send(
                    of("middle"), [of("halfway")],
                    lambda t: lax.ppermute(t, "rep", [(1, 2), (2, 1)]),
                )
                plan.core(of("whole"), [of("halfway"), of("middle")], add_low)
                plan.send(
                    of("outward"), [of("whole")],
                    lambda t: lax.ppermute(t, "rep", [(1, 0), (2, 3)]),
                )
                plan.core(
                    of("final"), [of("whole"), of("outward")],
                    lambda whole, outward: jnp.where(inner, whole, outward),
                )
                finals.append(of("final"))
            inside += size

        def step(*grads, start=start):
            nonlocal done
            done = adam_blocks(grads, start, state, done)
            return done

        plan.core(name("step"), finals, step)
        start += total

    old = None
    line = [[(i, i ^ bit) for i in range(4)] for bit in (1, 2)]
    for n, (text, axis, pairs) in enumerate(
        (("far", "fsdp", far_pairs), ("near", "fsdp", near_pairs),
         ("core", "fsdp", [(i, i ^ CORE) for i in range(owners)]),
         ("pair", "rep", line[0]), ("line", "rep", line[1]))
    ):
        plan.send(
            "gain_" + text, [old] if old else [],
            lambda gain=gain_grad, axis=axis, pairs=pairs: lax.ppermute(gain, axis, pairs),
        )
        new = "gain" + str(n + 1)
        if old:
            plan.core(new, [old, "gain_" + text], lambda a, b: a + b)
        else:
            plan.core(new, ["gain_" + text], lambda b: gain_grad + b)
        old = new
    values = plan.run(ORDER)
    return done, values[old]


def shards(
    tokens,
    cotangent,
    segment_ids,
    block_slot_index,
    weights,
    first_moment,
    second_moment,
    left_basis,
    right_basis,
    norm_gains,
    gain_first,
    gain_second,
):
    owners = lax.axis_size("fsdp")
    own = weights.shape[0]
    slots = own * owners
    me = lax.axis_index("fsdp")
    state = (weights, first_moment, second_moment, left_basis, right_basis)
    small = owners == 8 and lax.axis_size("rep") == 4 and own == sum(group_sizes())

    if small:
        pieces, bases = gather_pieces(weights, me)
        slot_order = slot_order_of(me, own)
        out_sizes = [4 * size for size in group_sizes() for _ in range(2)]
    else:
        pieces = [lax.all_gather(weights.astype(BF16), "fsdp", axis=0, tiled=True)]
        bases = jnp.arange(owners, dtype=jnp.int32) * own
        slot_order = jnp.arange(slots, dtype=jnp.int32)
        out_sizes = [slots]
    block_out, token_grad, gain_grad, *grads = run_layer(
        tokens, cotangent, segment_ids, block_slot_index, norm_gains, pieces, own, bases,
        slot_order, out_sizes,
    )
    if small:
        done, gain_grads = reduce_and_step(me, own, grads, state, gain_grad)
    else:
        owner_sums = lax.psum_scatter(
            grads[0], "fsdp", scatter_dimension=0, tiled=True
        )
        owner_grads = flat(lax.psum(owner_sums, "rep"))
        done = adam_blocks([owner_grads], 0, state, ())
        gain_grads = sum_everywhere(sum_everywhere(gain_grad, "fsdp"), "rep")
    grads_wide, first_new, second_new, weights_new, weights_low = done
    gain_first_new, gain_second_new, gains_new = adam_plain(
        gain_grads, norm_gains, gain_first, gain_second
    )
    return (
        block_out,
        token_grad,
        grads_wide,
        first_new,
        second_new,
        weights_new,
        weights_low,
        gain_first_new,
        gain_second_new,
        gains_new,
    )


def solution(mesh):
    return jax.shard_map(
        shards,
        mesh=mesh,
        in_specs=(
            P(("fsdp", "rep"), None),
            P(("fsdp", "rep"), None),
            P(("fsdp", "rep"), None),
            P(),
            P("fsdp", None, None),
            P("fsdp", None, None),
            P("fsdp", None, None),
            P("fsdp", None, None),
            P("fsdp", None, None),
            P(),
            P(),
            P(),
        ),
        out_specs=(
            P(("fsdp", "rep"), None),
            P(("fsdp", "rep"), None),
            P("fsdp", None, None),
            P("fsdp", None, None),
            P("fsdp", None, None),
            P("fsdp", None, None),
            P("fsdp", None, None),
            P(),
            P(),
            P(),
        ),
        check_vma=False,
    )
```

```python
import functools
import math

import jax
import jax.numpy as jnp
import numpy as np
from jax import lax
from jax.experimental import pallas as pl
from jax.experimental.pallas import tpu as pltpu
from jax.sharding import PartitionSpec as P

D = 768
HEADS = 12
HEAD_DIM = 64
FF = 2048
BLOCK_ORDER = 256
STEP = 10


NORM_EPS = 1e-05
ROPE_BASE = 10000.0
BETA_ONE = 0.5
BETA_TWO = 0.5
ADAM_EPS = 1e-08
RATE = 0.03
GAIN_RATE = 0.4
DECAY = 0.01
MASKED = -1e30

B = BLOCK_ORDER
BF16 = jnp.bfloat16
F32 = jnp.float32
MIB = 1024 * 1024

LEFT_X, LEFT_A, LEFT_Y, LEFT_ACT = 0, D // B, 2 * D // B, 3 * D // B
LEFT_ROWS = 3 * D + FF
RIGHT_Q, RIGHT_K, RIGHT_V, RIGHT_O = 0, D, 2 * D, 3 * D
RIGHT_G, RIGHT_U, RIGHT_D = 4 * D, 4 * D + FF, 4 * D + 2 * FF
RIGHT_COLS = 5 * D + 2 * FF


def matrix_table():
    return [
        (D // B, D // B, LEFT_X, RIGHT_Q // B),
        (D // B, D // B, LEFT_X, RIGHT_K // B),
        (D // B, D // B, LEFT_X, RIGHT_V // B),
        (D // B, D // B, LEFT_A, RIGHT_O // B),
        (D // B, FF // B, LEFT_Y, RIGHT_G // B),
        (D // B, FF // B, LEFT_Y, RIGHT_U // B),
        (FF // B, D // B, LEFT_ACT, RIGHT_D // B),
    ]


def factor_tables():
    lefts, rights = [], []
    for grid_rows, grid_cols, left, right in matrix_table():
        for i in range(grid_rows):
            for j in range(grid_cols):
                lefts.append(left + i)
                rights.append(right + j)
    return np.array(lefts, np.int32), np.array(rights, np.int32)


def dot_nn(a, b):
    return jnp.dot(a, b, preferred_element_type=F32)


def dot_nt(a, b):
    return lax.dot_general(a, b, (((1,), (1,)), ((), ())), preferred_element_type=F32)


def half_swap(values, low_half):
    return jnp.where(low_half, pltpu.roll(values, 96, 1), pltpu.roll(values, 32, 1))


def list_factors(index_ref, block_left_ref, block_right_ref, left_ref, right_ref):
    def clear(g, carry):
        for n in range(4):
            left_ref[4 * g + n] = -1
            right_ref[4 * g + n] = 0
        return carry

    lax.fori_loop(0, left_ref.shape[0] // 4, clear, 0)

    def enter(g, carry):
        for n in range(4):
            slot = index_ref[4 * g + n]
            left_ref[slot] = block_left_ref[4 * g + n]
            right_ref[slot] = block_right_ref[4 * g + n]
        return carry

    lax.fori_loop(0, index_ref.shape[0] // 4, enter, 0)


WEIGH_COPY = 4


def weigh_slots(slot_ref, left_ref, right_ref, lefts, rights, outs, ring, sems):
    copies = [out.shape[0] // WEIGH_COPY for out in outs]
    total = sum(copies)
    assert total % 2 == 0

    def put(target, place):
        return pltpu.make_async_copy(ring.at[place], target, sems.at[place])

    def run(g, carry):
        first_place = 2 * lax.rem(g, 2)
        for half in range(2):

            @pl.when(g >= 2)
            def _(half=half):
                put(ring.at[first_place + half], first_place + half).wait()

        for n in range(2 * WEIGH_COPY):
            slot = slot_ref[2 * g * WEIGH_COPY + n]
            left = left_ref[slot]
            grad = dot_nn(
                lefts[pl.ds(pl.multiple_of(jnp.maximum(left, 0) * B, B), B), :],
                rights[:, pl.ds(pl.multiple_of(right_ref[slot] * B, B), B)],
            )
            keep = jnp.where(left >= 0, 1.0, 0.0)
            ring[first_place + n // WEIGH_COPY, n % WEIGH_COPY] = (grad * keep).astype(BF16)
        for half in range(2):
            copy = 2 * g + half
            first = 0
            for out, count in zip(outs, copies):

                @pl.when((copy >= first) & (copy < first + count))
                def _(out=out, first=first, half=half, copy=copy):
                    at = pl.ds((copy - first) * WEIGH_COPY, WEIGH_COPY)
                    put(out.at[at], first_place + half).start()

                first += count
        return carry

    assert total >= 4
    lax.fori_loop(0, total // 2, run, 0)
    for place in range(4):
        put(ring.at[place], place).wait()


def layer_kernel(
    micro,
    own,
    piece_slots,
    out_count,
    index_ref,
    base_ref,
    slot_ref,
    block_left_ref,
    block_right_ref,
    segments_ref,
    segments_t_ref,
    x_ref,
    dy_ref,
    gains_ref,
    *rest,
):
    pieces = rest[: len(piece_slots)]
    rest = rest[len(piece_slots) :]
    out_ref, token_grad_ref, gain_ref = rest[:3]
    grad_refs, rest = rest[3 : 3 + out_count], rest[3 + out_count :]
    (
        w_qkv,
        w_o,
        w_gu,
        w_d,
        lefts,
        rights,
        q_scr,
        k_scr,
        v_scr,
        p_scr,
        a_scr,
        act_scr,
        cg_scr,
        cu_scr,
        y1_scr,
        y1_low_scr,
        h1_scr,
        dh2_scr,
        r1_scr,
        w_sems,
        ring,
        ring_sems,
        left_ref,
        right_ref,
        bias_ref,
        cos_ref,
        sin_ref,
        cos_t_ref,
        sin_t_ref,
    ) = rest
    seq = segments_ref.shape[1]

    starts = [sum(piece_slots[:n]) for n in range(len(piece_slots) + 1)]
    reciprocal = (1 << 16) // own + 1
    assert all(slot * reciprocal >> 16 == slot // own for slot in range(starts[-1]))

    def fetch(block, target, row, col, sem):
        slot = index_ref[block]
        owner = lax.shift_right_logical(slot * reciprocal, 16)
        place = base_ref[owner] + slot - owner * own

        def among(low, high):
            if high - low > 1:
                middle = (low + high) // 2
                lax.cond(
                    place < starts[middle],
                    lambda: among(low, middle),
                    lambda: among(middle, high),
                )
            else:
                pltpu.make_async_copy(
                    pieces[low].at[place - starts[low]],
                    target.at[
                        pl.ds(pl.multiple_of(row * B, B), B), pl.ds(pl.multiple_of(col * B, B), B)
                    ],
                    sem,
                ).start()

        among(0, len(pieces))

    def fetch_matrix(first_block, grid_rows, grid_cols, target, col_offset, sem):
        def one(t, carry):
            i = t // grid_cols
            j = t - i * grid_cols
            fetch(first_block + t, target, i, j + col_offset, sem)
            return carry

        lax.fori_loop(0, grid_rows * grid_cols, one, 0)

    nd, nf = D // B, FF // B
    for m in range(3):
        fetch_matrix(m * nd * nd, nd, nd, w_qkv, m * nd, w_sems.at[0])

    list_factors(index_ref, block_left_ref, block_right_ref, left_ref, right_ref)
    half_dim = HEAD_DIM // 2
    step = lax.broadcasted_iota(jnp.int32, (half_dim, 1), 0).astype(F32)
    frequency = jnp.exp(step * (-2.0 / HEAD_DIM * math.log(ROPE_BASE)))
    keys = lax.broadcasted_iota(jnp.int32, (seq, seq), 0)
    queries = lax.broadcasted_iota(jnp.int32, (seq, seq), 1)
    for r in range(micro):
        rows = slice(r * seq, (r + 1) * seq)
        same = segments_t_ref[:, r : r + 1] == segments_ref[r : r + 1, :]
        bias_ref[r] = jnp.where(same & (keys <= queries), 0.0, MASKED)
        first = jnp.min(jnp.where(same, keys, seq), axis=0, keepdims=True)
        angles = frequency * (queries[0:1, :] - first).astype(F32)
        cosine_t, sine_t = jnp.cos(angles), jnp.sin(angles)
        cos_t_ref[:, rows] = cosine_t
        sin_t_ref[:, rows] = sine_t
        cosine, sine = cosine_t.T, sine_t.T
        cos_ref[rows, :] = jnp.concatenate([cosine] * 4, axis=1)
        sin_ref[rows, :] = jnp.concatenate([-sine, sine, -sine, sine], axis=1)

    fetch_matrix(3 * nd * nd, nd, nd, w_o, 0, w_sems.at[1])
    for m in range(2):
        fetch_matrix(4 * nd * nd + m * nd * nf, nd, nf, w_gu, m * nf, w_sems.at[2])
    fetch_matrix(4 * nd * nd + 2 * nd * nf, nf, nd, w_d, 0, w_sems.at[3])

    def wait_for(target, sem):
        pltpu.make_async_copy(target, target, sem).wait()

    lefts[0:D, :] = x_ref[...].T
    lane = lax.broadcasted_iota(jnp.int32, (1, 128), 1)
    low_half = lax.rem(lane, HEAD_DIM) < HEAD_DIM // 2
    head_lanes = [lane < HEAD_DIM, lane >= HEAD_DIM]

    def of_head(values, h):
        return jnp.where(head_lanes[h], values, jnp.zeros_like(values))

    wait_for(w_qkv, w_sems.at[0])

    def attend(jb, carry):
        def columns(offset):
            return pl.ds(pl.multiple_of(offset + jb * B, B), B)

        x = x_ref[...]
        q_raw = dot_nn(x, w_qkv[:, columns(0)])
        k_raw = dot_nn(x, w_qkv[:, columns(D)])
        v_raw = dot_nn(x, w_qkv[:, columns(2 * D)])
        cosine = cos_ref[...]
        sine = sin_ref[...]
        for sub in range(2):
            part = slice(sub * 128, sub * 128 + 128)
            slab = pl.ds(pl.multiple_of(jb * B + sub * 128, 128), 128)
            q = q_raw[:, part]
            k = k_raw[:, part]
            q = ((q * cosine + half_swap(q, low_half) * sine) * HEAD_DIM**-0.5).astype(BF16)
            k = (k * cosine + half_swap(k, low_half) * sine).astype(BF16)
            v = v_raw[:, part].astype(BF16)
            q_scr[:, slab] = q
            k_scr[:, slab] = k
            v_scr[:, slab] = v
            for r in range(micro):
                rows = slice(r * seq, (r + 1) * seq)
                v_t = v[rows].T
                outs = []
                for h in range(2):
                    scores = dot_nt(k[rows], of_head(q[rows], h)) + bias_ref[r]
                    top = jnp.max(scores, axis=0, keepdims=True)
                    exps = jnp.exp(scores - top)
                    total = jnp.sum(exps, axis=0, keepdims=True)
                    probs = (exps * (1.0 / total)).astype(BF16)
                    p_scr[(jb * 2 + sub) * 2 * micro + 2 * r + h] = probs
                    outs.append(dot_nn(v_t[h * HEAD_DIM : (h + 1) * HEAD_DIM], probs))
                a_t = jnp.concatenate(outs, axis=0).astype(BF16)
                lefts[pl.ds(pl.multiple_of(D + jb * B + sub * 128, 128), 128), rows] = a_t
                a_scr[rows, slab] = a_t.T
        return carry

    lax.fori_loop(0, nd, attend, 0)

    wait_for(w_o, w_sems.at[1])
    for r in range(micro):
        rows = slice(r * seq, (r + 1) * seq)
        h1 = x_ref[rows, :].astype(F32) + dot_nn(a_scr[rows, :], w_o[...])
        r1 = lax.rsqrt(jnp.mean(h1 * h1, axis=-1, keepdims=True) + NORM_EPS)
        y1 = h1 * r1 * gains_ref[0:1, :]
        y1_low = y1.astype(BF16)
        h1_scr[rows, :] = h1
        r1_scr[rows, :] = r1
        y1_scr[rows, :] = y1
        y1_low_scr[rows, :] = y1_low
        lefts[2 * D : 3 * D, rows] = y1_low.T

    wait_for(w_gu, w_sems.at[2])

    def feed(j, carry):
        y1_low = y1_low_scr[...]
        cols = pl.ds(pl.multiple_of(j * B, B), B)
        gate = dot_nn(y1_low, w_gu[:, cols])
        up = dot_nn(y1_low, w_gu[:, pl.ds(pl.multiple_of(FF + j * B, B), B)])
        sig = 1.0 / (1.0 + jnp.exp(-gate))
        silu = gate * sig
        act = (silu * up).astype(BF16)
        act_scr[:, cols] = act
        cu_scr[:, cols] = silu.astype(BF16)
        cg_scr[:, cols] = (up * sig * (1.0 + gate * (1.0 - sig))).astype(BF16)
        lefts[pl.ds(pl.multiple_of(3 * D + j * B, B), B), :] = act.T
        return carry

    lax.fori_loop(0, nf, feed, 0)

    wait_for(w_d, w_sems.at[3])
    gain_two = jnp.zeros((1, D), F32)
    for r in range(micro):
        rows = slice(r * seq, (r + 1) * seq)
        h2 = y1_scr[rows, :] + dot_nn(act_scr[rows, :], w_d[...])
        r2 = lax.rsqrt(jnp.mean(h2 * h2, axis=-1, keepdims=True) + NORM_EPS)
        scaled = h2 * r2
        gain = gains_ref[1:2, :]
        out_ref[rows, :] = (scaled * gain).astype(BF16)
        dy = dy_ref[rows, :].astype(F32)
        gain_two += jnp.sum(dy * scaled, axis=0, keepdims=True)
        dyg = dy * gain
        dh2 = r2 * (dyg - scaled * jnp.mean(scaled * dyg, axis=-1, keepdims=True))
        dh2_scr[rows, :] = dh2
        rights[rows, RIGHT_D:] = dh2.astype(BF16)
    gain_ref[1:2, :] = gain_two

    def feed_back(j, carry):
        cols = pl.ds(pl.multiple_of(j * B, B), B)
        dact = dot_nt(rights[:, RIGHT_D:], w_d[cols, :])
        rights[:, pl.ds(pl.multiple_of(RIGHT_G + j * B, B), B)] = (
            dact * cg_scr[:, cols].astype(F32)
        ).astype(BF16)
        rights[:, pl.ds(pl.multiple_of(RIGHT_U + j * B, B), B)] = (
            dact * cu_scr[:, cols].astype(F32)
        ).astype(BF16)
        return carry

    lax.fori_loop(0, nf, feed_back, 0)

    def feed_in(j, carry):
        cols = pl.ds(pl.multiple_of(j * B, B), B)
        dh2_scr[:, cols] += dot_nt(rights[:, RIGHT_G:RIGHT_D], w_gu[cols, :])
        return carry

    lax.fori_loop(0, nd, feed_in, 0)

    gain_one = jnp.zeros((1, D), F32)
    for r in range(micro):
        rows = slice(r * seq, (r + 1) * seq)
        dy1 = dh2_scr[rows, :]
        r1 = r1_scr[rows, :]
        scaled = h1_scr[rows, :] * r1
        gain_one += jnp.sum(dy1 * scaled, axis=0, keepdims=True)
        dyg = dy1 * gains_ref[0:1, :]
        dh1 = r1 * (dyg - scaled * jnp.mean(scaled * dyg, axis=-1, keepdims=True))
        h1_scr[rows, :] = dh1
        do = dh1.astype(BF16)
        rights[rows, RIGHT_O : RIGHT_O + D] = do
        a_scr[rows, :] = dot_nt(do, w_o[...]).astype(BF16)
    gain_ref[0:1, :] = gain_one

    def attend_back(jb, carry):
        for sub in range(2):
            slab = pl.ds(pl.multiple_of(jb * B + sub * 128, 128), 128)
            for r in range(micro):
                rows = slice(r * seq, (r + 1) * seq)
                q = q_scr[rows, slab]
                k = k_scr[rows, slab]
                v = v_scr[rows, slab]
                da = a_scr[rows, slab]
                k_t = k.T
                dv = jnp.zeros((seq, 128), F32)
                dk = jnp.zeros((seq, 128), F32)
                dq_t = []
                for h in range(2):
                    probs = p_scr[(jb * 2 + sub) * 2 * micro + 2 * r + h]
                    da_h = of_head(da, h)
                    probs_wide = probs.astype(F32)
                    dprobs = dot_nt(v, da_h)
                    weighted = probs_wide * dprobs
                    row_sum = jnp.sum(weighted, axis=0, keepdims=True)
                    ds = (weighted - probs_wide * row_sum).astype(BF16)
                    dv += dot_nn(probs, da_h)
                    dk += dot_nn(ds, of_head(q, h))
                    dq_h = dot_nn(k_t[h * HEAD_DIM : (h + 1) * HEAD_DIM], ds) * HEAD_DIM**-0.5
                    low, high = dq_h[: HEAD_DIM // 2], dq_h[HEAD_DIM // 2 :]
                    cosine = cos_t_ref[:, rows]
                    sine = sin_t_ref[:, rows]
                    dq_t.append(low * cosine + high * sine)
                    dq_t.append(high * cosine - low * sine)
                dq = jnp.concatenate(dq_t, axis=0).astype(BF16).T
                dk = dk * cos_ref[rows, :] - half_swap(dk, low_half) * sin_ref[rows, :]
                rights[rows, slab] = dq
                rights[rows, pl.ds(pl.multiple_of(RIGHT_K + jb * B + sub * 128, 128), 128)] = (
                    dk.astype(BF16)
                )
                rights[rows, pl.ds(pl.multiple_of(RIGHT_V + jb * B + sub * 128, 128), 128)] = (
                    dv.astype(BF16)
                )
        return carry

    lax.fori_loop(0, nd, attend_back, 0)

    def token_back(j, carry):
        cols = pl.ds(pl.multiple_of(j * B, B), B)
        token_grad_ref[:, cols] = (
            h1_scr[:, cols] + dot_nt(rights[:, : 3 * D], w_qkv[cols, :])
        ).astype(BF16)
        return carry

    lax.fori_loop(0, nd, token_back, 0)

    weigh_slots(slot_ref, left_ref, right_ref, lefts, rights, grad_refs, ring, ring_sems)


def run_layer(
    tokens, cotangent, segment_ids, block_slot_index, norm_gains, pieces, own, bases, slot_order,
    out_sizes,
):
    micro, seq = segment_ids.shape
    count = micro * seq
    slots = own * bases.shape[0]
    grads = [jax.ShapeDtypeStruct((size, B, B), BF16) for size in out_sizes]
    vmem = pl.BlockSpec(memory_space=pltpu.VMEM)
    smem = pl.BlockSpec(memory_space=pltpu.SMEM)
    hbm = pl.BlockSpec(memory_space=pl.ANY)
    return pl.pallas_call(
        functools.partial(layer_kernel, micro, own, [p.shape[0] for p in pieces], len(grads)),
        out_shape=(
            jax.ShapeDtypeStruct((count, D), BF16),
            jax.ShapeDtypeStruct((count, D), BF16),
            jax.ShapeDtypeStruct((2, D), F32),
            *grads,
        ),
        in_specs=[smem] * 5 + [vmem] * 5 + [hbm] * len(pieces),
        out_specs=(vmem,) * 3 + (hbm,) * len(grads),
        scratch_shapes=[
            pltpu.VMEM((D, 3 * D), BF16),
            pltpu.VMEM((D, D), BF16),
            pltpu.VMEM((D, 2 * FF), BF16),
            pltpu.VMEM((FF, D), BF16),
            pltpu.VMEM((LEFT_ROWS, count), BF16),
            pltpu.VMEM((count, RIGHT_COLS), BF16),
            pltpu.VMEM((count, D), BF16),
            pltpu.VMEM((count, D), BF16),
            pltpu.VMEM((count, D), BF16),
            pltpu.VMEM((HEADS * micro, seq, seq), BF16),
            pltpu.VMEM((count, D), BF16),
            pltpu.VMEM((count, FF), BF16),
            pltpu.VMEM((count, FF), BF16),
            pltpu.VMEM((count, FF), BF16),
            pltpu.VMEM((count, D), F32),
            pltpu.VMEM((count, D), BF16),
            pltpu.VMEM((count, D), F32),
            pltpu.VMEM((count, D), F32),
            pltpu.VMEM((count, 1), F32),
            pltpu.SemaphoreType.DMA((4,)),
            pltpu.VMEM((4, WEIGH_COPY, B, B), BF16),
            pltpu.SemaphoreType.DMA((4,)),
            pltpu.SMEM((slots,), jnp.int32),
            pltpu.SMEM((slots,), jnp.int32),
            pltpu.VMEM((micro, seq, seq), F32),
            pltpu.VMEM((count, 128), F32),
            pltpu.VMEM((count, 128), F32),
            pltpu.VMEM((HEAD_DIM // 2, count), F32),
            pltpu.VMEM((HEAD_DIM // 2, count), F32),
        ],
        compiler_params=pltpu.CompilerParams(vmem_limit_bytes=56 * MIB),
        cost_estimate=pl.CostEstimate(
            flops=23_000_000_000, bytes_accessed=32_000_000, transcendentals=3_000_000
        ),
        name="layer",
    )(
        block_slot_index,
        bases,
        slot_order,
        *(jnp.asarray(table) for table in factor_tables()),
        segment_ids,
        segment_ids.T,
        tokens,
        cotangent,
        norm_gains,
        *pieces,
    )


def split_two(values):
    high = values.astype(BF16)
    return high, (values - high.astype(F32)).astype(BF16)


def adam_kernel(steps, weight_ref, first_ref, second_ref, left_ref, right_ref, *rest):
    grad_refs = rest[: len(steps)]
    grad_out, first_out, second_out, weight_out, low_out, grads = rest[-6:]
    now, start = pl.program_id(0), 0
    for count, grad_ref in zip(steps, grad_refs):

        @pl.when((now >= start) & (now < start + count))
        def _(grad_ref=grad_ref):
            grads[...] = grad_ref[...]

        start += count
    for n in range(weight_ref.shape[0]):
        grad = grads[n * B : (n + 1) * B, :]
        left, left_rest = split_two(left_ref[n])
        right, right_rest = split_two(right_ref[n])
        grad_out[n] = grad.astype(F32)
        turned = (dot_nn(grad, right) + dot_nn(grad, right_rest)).astype(BF16)
        turned = dot_nn(left.T, turned) + dot_nn(left_rest.T, turned)
        first_new = BETA_ONE * first_ref[n] + (1.0 - BETA_ONE) * turned
        second_new = BETA_TWO * second_ref[n] + (1.0 - BETA_TWO) * turned * turned
        first_out[n] = first_new
        second_out[n] = second_new
        ratio = (
            first_new
            / (1.0 - BETA_ONE**STEP)
            / (jnp.sqrt(second_new / (1.0 - BETA_TWO**STEP)) + ADAM_EPS)
        )
        back = dot_nt(dot_nn(left, ratio.astype(BF16)).astype(BF16), right)
        weight = weight_ref[n]
        weight_new = weight - RATE * (back + DECAY * weight)
        weight_out[n] = weight_new
        low_out[n] = weight_new.astype(BF16)


def adam_blocks(grads, start, state, done):
    own = state[0].shape[0]
    step = math.gcd(2, start, *(part.shape[0] // B for part in grads))
    steps = [part.shape[0] // B // step for part in grads]
    local = []
    for number, count in enumerate(steps):
        local.append(
            pl.BlockSpec(
                (step * B, B),
                lambda s, first=sum(steps[:number]), count=count: (
                    jnp.clip(s - first, 0, count - 1),
                    0,
                ),
            )
        )
    spec = pl.BlockSpec((step, B, B), lambda s: (s + start // step, 0, 0))
    hbm = pl.BlockSpec(memory_space=pl.ANY)
    wide = jax.ShapeDtypeStruct((own, B, B), F32)
    return pl.pallas_call(
        functools.partial(adam_kernel, steps),
        grid=(sum(steps),),
        out_shape=(wide, wide, wide, wide, jax.ShapeDtypeStruct((own, B, B), BF16)),
        in_specs=[spec] * 5 + local + [hbm] * len(done),
        out_specs=(spec,) * 5,
        input_output_aliases={5 + len(local) + n: n for n in range(len(done))},
        scratch_shapes=[pltpu.VMEM((step * B, B), BF16)],
        compiler_params=pltpu.CompilerParams(vmem_limit_bytes=60 * MIB),
        cost_estimate=pl.CostEstimate(
            flops=sum(steps) * step * 12 * B**3,
            bytes_accessed=sum(steps) * step * B * B * 42,
            transcendentals=sum(steps) * step * B * B,
        ),
        name="adam",
    )(*state, *grads, *done)


def adam_plain(grads, values, first_moment, second_moment):
    first_new = BETA_ONE * first_moment + (1.0 - BETA_ONE) * grads
    second_new = BETA_TWO * second_moment + (1.0 - BETA_TWO) * grads * grads
    step_ratio = (
        first_new
        / (1.0 - BETA_ONE**STEP)
        / (jnp.sqrt(second_new / (1.0 - BETA_TWO**STEP)) + ADAM_EPS)
    )
    return (first_new, second_new, values - GAIN_RATE * step_ratio)


def sum_everywhere(values, axis):
    size = lax.axis_size(axis)
    if size & (size - 1):
        return lax.psum(values, axis)
    reach = 1
    while reach < size:
        values = values + lax.ppermute(values, axis, [(i, i ^ reach) for i in range(size)])
        reach *= 2
    return values


def add_low(*terms):
    return sum(term.astype(F32) for term in terms).astype(BF16)


CORE, ACROSS, ALONG = 1, 2, 4
DIAGONAL = ACROSS | ALONG


def exchange(values, bit):
    return lax.ppermute(values, "fsdp", [(i, i ^ bit) for i in range(lax.axis_size("fsdp"))])


def core_neighbours(me):
    near = jnp.where((me & CORE) == 0, ACROSS, ALONG)
    return near, DIAGONAL ^ near


def plane_pairs(owners):
    near = [(i, i ^ (ALONG if i & CORE else ACROSS)) for i in range(owners)]
    far = [(i, i ^ (ACROSS if i & CORE else ALONG)) for i in range(owners)]
    return near, far


def after(values, *others):
    return lax.optimization_barrier((values, *others))[0]


def gather_pieces(weights, me):
    own = weights.shape[0]
    half = own // 2
    near, far = core_neighbours(me)
    near_pairs, far_pairs = plane_pairs(lax.axis_size("fsdp"))
    mine = weights.astype(BF16)
    first_near = lax.ppermute(weights[:half].astype(BF16), "fsdp", near_pairs)
    last_near = lax.ppermute(weights[half:].astype(BF16), "fsdp", near_pairs)
    all_far = lax.ppermute(mine, "fsdp", far_pairs)
    first_diagonal = lax.ppermute(first_near, "fsdp", far_pairs)
    last_diagonal = lax.ppermute(last_near, "fsdp", far_pairs)
    pieces, relations = [], []
    for parts, relation, others in (
        ((mine,), 0, 0),
        ((first_near, last_near), near, far),
        ((all_far,), far, near),
        ((first_diagonal, last_diagonal), DIAGONAL, DIAGONAL),
    ):
        pieces += [*parts, *(exchange(part, CORE) for part in parts)]
        relations += [relation, others | CORE]
    owners = me ^ jnp.stack(relations).astype(jnp.int32)
    bases = jnp.sum(
        jnp.where(
            jnp.arange(len(relations), dtype=jnp.int32)[:, None] == owners[None, :],
            jnp.arange(len(relations), dtype=jnp.int32)[None, :] * own,
            0,
        ),
        axis=1,
    )
    return pieces, bases


class Plan:
    def __init__(self):
        self.tasks = {}

    def core(self, name, needs, run):
        self.tasks[name] = (True, needs, run)

    def send(self, name, needs, run):
        self.tasks[name] = (False, needs, run)

    def run(self, order):
        assert sorted(order) == sorted(self.tasks)
        values, last = {}, None
        for name in order:
            on_core, needs, run = self.tasks[name]
            inputs = [values[n] for n in needs]
            if last is not None:
                *inputs, _ = lax.optimization_barrier((*inputs, last))
            values[name] = run(*inputs)
            if on_core:
                last = jax.tree.leaves(values[name])[0]
        return values


GROUPS = (((4,),), ((6,), (4,)))
ORDER = (
    "grads0 grads1 core0 gain_far near_sum0 near0 core1 near_sum1 near1 gain1 far_sum0_0 far0_0 plane_sum0_0 "
    "inward0_0a halfway0_0a middle0_0a far_sum1_0 far1_0 far_sum1_1 far1_1 gain_near whole0_0a outward0_0a "
    "plane_sum1_0 inward1_0a plane_sum1_1 inward1_1a gain2 gain_core halfway1_0a middle1_0a final0_0a gain3 "
    "gain_pair halfway1_1a middle1_1a whole1_0a outward1_0a step0_0 whole1_1a outward1_1a final1_0a gain4 "
    "gain_line step1_0 gain5 final1_1a step1_1"
).split()


def group_sizes():
    return [sum(sum(parts) for parts in sets) for sets in GROUPS]


def slot_order_of(me, own):
    near, far = core_neighbours(me)
    relations = [DIAGONAL | CORE, far | CORE, near | CORE, CORE, DIAGONAL, near, far, 0]
    slots, start = [], 0
    for size in group_sizes():
        for relation in relations:
            slots.append((me ^ relation) * own + start + jnp.arange(size, dtype=jnp.int32))
        start += size
    return jnp.concatenate(slots).astype(jnp.int32)


def flat(blocks):
    return blocks.reshape(-1, B)


def reduce_and_step(me, own, grads, state, gain_grad):
    plan = Plan()
    owners = lax.axis_size("fsdp")
    near_pairs, far_pairs = plane_pairs(owners)
    place = lax.axis_index("rep")
    inner = (place == 1) | (place == 2)
    done = ()
    start = 0

    for number, sets in enumerate(GROUPS):
        total = group_sizes()[number]

        def name(text, number=number):
            return text + str(number)

        both = [name("grads"), name("core")]

        def chip(pair, arrived, first, last):
            return flat(pair[1][first:last]), flat(arrived[first:last])

        plan.core(
            name("grads"), [],
            lambda pair=grads[2 * number : 2 * number + 2]: pair,
        )
        plan.send(name("core"), [name("grads")], lambda pair: exchange(pair[0], CORE))
        plan.core(
            name("near_sum"), both,
            lambda pair, arrived, total=total: add_low(*chip(pair, arrived, 0, 2 * total)),
        )
        plan.send(
            name("near"), [name("near_sum")], lambda t: lax.ppermute(t, "fsdp", near_pairs)
        )
        inside = 0
        for member, parts in enumerate(sets):
            size = sum(parts)
            finals = []

            def at(text, number=number, member=member):
                return "%s%d_%d" % (text, number, member)

            def far_sum(pair, arrived, r, inside=inside, size=size, total=total):
                first = 2 * total + inside
                return add_low(
                    *chip(pair, arrived, first, first + size), r[inside * B : (inside + size) * B]
                )

            plan.core(at("far_sum"), both + [name("near")], far_sum)
            plan.send(
                at("far"), [at("far_sum")], lambda t: lax.ppermute(t, "fsdp", far_pairs)
            )
            firsts = [sum(parts[:p]) for p in range(len(parts) + 1)]

            def plane_sum(pair, arrived, r, q, inside=inside, total=total, firsts=firsts):
                sums = []
                for a, b in zip(firsts[:-1], firsts[1:]):
                    first, last = inside + a, inside + b
                    sums.append(
                        add_low(
                            *chip(pair, arrived, 3 * total + first, 3 * total + last),
                            r[(total + first) * B : (total + last) * B],
                            q[a * B : b * B],
                        )
                    )
                return sums

            plan.core(at("plane_sum"), both + [name("near"), at("far")], plane_sum)
            for part in range(len(parts)):

                def of(text, part=part, at=at):
                    return at(text) + "abcd"[part]

                plan.send(
                    of("inward"), [at("plane_sum")],
                    lambda t, part=part: lax.ppermute(t[part], "rep", [(0, 1), (3, 2)]),
                )
                plan.core(
                    of("halfway"), [at("plane_sum"), of("inward")],
                    lambda t, r, part=part: add_low(t[part], r),
                )
                plan.send(
                    of("middle"), [of("halfway")],
                    lambda t: lax.ppermute(t, "rep", [(1, 2), (2, 1)]),
                )
                plan.core(of("whole"), [of("halfway"), of("middle")], add_low)
                plan.send(
                    of("outward"), [of("whole")],
                    lambda t: lax.ppermute(t, "rep", [(1, 0), (2, 3)]),
                )
                plan.core(
                    of("final"), [of("whole"), of("outward")],
                    lambda whole, outward: jnp.where(inner, whole, outward),
                )
                finals.append(of("final"))
            inside += size

            def step(*grads, start=start):
                nonlocal done
                done = adam_blocks(grads, start, state, done)
                return done

            plan.core(at("step"), finals, step)
            start += size

    old = None
    line = [[(i, i ^ bit) for i in range(4)] for bit in (1, 2)]
    for n, (text, axis, pairs) in enumerate(
        (("far", "fsdp", far_pairs), ("near", "fsdp", near_pairs),
         ("core", "fsdp", [(i, i ^ CORE) for i in range(owners)]),
         ("pair", "rep", line[0]), ("line", "rep", line[1]))
    ):
        plan.send(
            "gain_" + text, [old] if old else [],
            lambda gain=gain_grad, axis=axis, pairs=pairs: lax.ppermute(gain, axis, pairs),
        )
        new = "gain" + str(n + 1)
        if old:
            plan.core(new, [old, "gain_" + text], lambda a, b: a + b)
        else:
            plan.core(new, ["gain_" + text], lambda b: gain_grad + b)
        old = new
    values = plan.run(ORDER)
    return done, values[old]


def shards(
    tokens,
    cotangent,
    segment_ids,
    block_slot_index,
    weights,
    first_moment,
    second_moment,
    left_basis,
    right_basis,
    norm_gains,
    gain_first,
    gain_second,
):
    owners = lax.axis_size("fsdp")
    own = weights.shape[0]
    slots = own * owners
    me = lax.axis_index("fsdp")
    state = (weights, first_moment, second_moment, left_basis, right_basis)
    small = owners == 8 and lax.axis_size("rep") == 4 and own == sum(group_sizes())

    if small:
        pieces, bases = gather_pieces(weights, me)
        slot_order = slot_order_of(me, own)
        out_sizes = [4 * size for size in group_sizes() for _ in range(2)]
    else:
        pieces = [lax.all_gather(weights.astype(BF16), "fsdp", axis=0, tiled=True)]
        bases = jnp.arange(owners, dtype=jnp.int32) * own
        slot_order = jnp.arange(slots, dtype=jnp.int32)
        out_sizes = [slots]
    block_out, token_grad, gain_grad, *grads = run_layer(
        tokens, cotangent, segment_ids, block_slot_index, norm_gains, pieces, own, bases,
        slot_order, out_sizes,
    )
    if small:
        done, gain_grads = reduce_and_step(me, own, grads, state, gain_grad)
    else:
        owner_sums = lax.psum_scatter(
            grads[0], "fsdp", scatter_dimension=0, tiled=True
        )
        owner_grads = flat(lax.psum(owner_sums, "rep"))
        done = adam_blocks([owner_grads], 0, state, ())
        gain_grads = sum_everywhere(sum_everywhere(gain_grad, "fsdp"), "rep")
    grads_wide, first_new, second_new, weights_new, weights_low = done
    gain_first_new, gain_second_new, gains_new = adam_plain(
        gain_grads, norm_gains, gain_first, gain_second
    )
    return (
        block_out,
        token_grad,
        grads_wide,
        first_new,
        second_new,
        weights_new,
        weights_low,
        gain_first_new,
        gain_second_new,
        gains_new,
    )


def solution(mesh):
    return jax.shard_map(
        shards,
        mesh=mesh,
        in_specs=(
            P(("fsdp", "rep"), None),
            P(("fsdp", "rep"), None),
            P(("fsdp", "rep"), None),
            P(),
            P("fsdp", None, None),
            P("fsdp", None, None),
            P("fsdp", None, None),
            P("fsdp", None, None),
            P("fsdp", None, None),
            P(),
            P(),
            P(),
        ),
        out_specs=(
            P(("fsdp", "rep"), None),
            P(("fsdp", "rep"), None),
            P("fsdp", None, None),
            P("fsdp", None, None),
            P("fsdp", None, None),
            P("fsdp", None, None),
            P("fsdp", None, None),
            P(),
            P(),
            P(),
        ),
        check_vma=False,
    )
```

```python
import functools
import math

import jax
import jax.numpy as jnp
import numpy as np
from jax import lax
from jax.experimental import pallas as pl
from jax.experimental.pallas import tpu as pltpu
from jax.sharding import PartitionSpec as P

D = 768
HEADS = 12
HEAD_DIM = 64
FF = 2048
BLOCK_ORDER = 256
STEP = 10


NORM_EPS = 1e-05
ROPE_BASE = 10000.0
BETA_ONE = 0.5
BETA_TWO = 0.5
ADAM_EPS = 1e-08
RATE = 0.03
GAIN_RATE = 0.4
DECAY = 0.01
MASKED = -1e30

B = BLOCK_ORDER
BF16 = jnp.bfloat16
F32 = jnp.float32
MIB = 1024 * 1024

LEFT_X, LEFT_A, LEFT_Y, LEFT_ACT = 0, D // B, 2 * D // B, 3 * D // B
LEFT_ROWS = 3 * D + FF
RIGHT_Q, RIGHT_K, RIGHT_V, RIGHT_O = 0, D, 2 * D, 3 * D
RIGHT_G, RIGHT_U, RIGHT_D = 4 * D, 4 * D + FF, 4 * D + 2 * FF
RIGHT_COLS = 5 * D + 2 * FF


def matrix_table():
    return [
        (D // B, D // B, LEFT_X, RIGHT_Q // B),
        (D // B, D // B, LEFT_X, RIGHT_K // B),
        (D // B, D // B, LEFT_X, RIGHT_V // B),
        (D // B, D // B, LEFT_A, RIGHT_O // B),
        (D // B, FF // B, LEFT_Y, RIGHT_G // B),
        (D // B, FF // B, LEFT_Y, RIGHT_U // B),
        (FF // B, D // B, LEFT_ACT, RIGHT_D // B),
    ]


def factor_tables():
    lefts, rights = [], []
    for grid_rows, grid_cols, left, right in matrix_table():
        for i in range(grid_rows):
            for j in range(grid_cols):
                lefts.append(left + i)
                rights.append(right + j)
    return np.array(lefts, np.int32), np.array(rights, np.int32)


def dot_nn(a, b):
    return jnp.dot(a, b, preferred_element_type=F32)


def dot_nt(a, b):
    return lax.dot_general(a, b, (((1,), (1,)), ((), ())), preferred_element_type=F32)


def half_swap(values, low_half):
    return jnp.where(low_half, pltpu.roll(values, 96, 1), pltpu.roll(values, 32, 1))


def list_factors(index_ref, block_left_ref, block_right_ref, left_ref, right_ref):
    def clear(g, carry):
        for n in range(4):
            left_ref[4 * g + n] = -1
            right_ref[4 * g + n] = 0
        return carry

    lax.fori_loop(0, left_ref.shape[0] // 4, clear, 0)

    def enter(g, carry):
        for n in range(4):
            slot = index_ref[4 * g + n]
            left_ref[slot] = block_left_ref[4 * g + n]
            right_ref[slot] = block_right_ref[4 * g + n]
        return carry

    lax.fori_loop(0, index_ref.shape[0] // 4, enter, 0)


WEIGH_COPY = 4


def weigh_slots(slot_ref, left_ref, right_ref, lefts, rights, outs, ring, sems):
    copies = [out.shape[0] // WEIGH_COPY for out in outs]
    total = sum(copies)
    assert total % 2 == 0

    def put(target, place):
        return pltpu.make_async_copy(ring.at[place], target, sems.at[place])

    def run(g, carry):
        first_place = 2 * lax.rem(g, 2)
        for half in range(2):

            @pl.when(g >= 2)
            def _(half=half):
                put(ring.at[first_place + half], first_place + half).wait()

        for n in range(2 * WEIGH_COPY):
            slot = slot_ref[2 * g * WEIGH_COPY + n]
            left = left_ref[slot]
            grad = dot_nn(
                lefts[pl.ds(pl.multiple_of(jnp.maximum(left, 0) * B, B), B), :],
                rights[:, pl.ds(pl.multiple_of(right_ref[slot] * B, B), B)],
            )
            keep = jnp.where(left >= 0, 1.0, 0.0)
            ring[first_place + n // WEIGH_COPY, n % WEIGH_COPY] = (grad * keep).astype(BF16)
        for half in range(2):
            copy = 2 * g + half
            first = 0
            for out, count in zip(outs, copies):

                @pl.when((copy >= first) & (copy < first + count))
                def _(out=out, first=first, half=half, copy=copy):
                    at = pl.ds((copy - first) * WEIGH_COPY, WEIGH_COPY)
                    put(out.at[at], first_place + half).start()

                first += count
        return carry

    assert total >= 4
    lax.fori_loop(0, total // 2, run, 0)
    for place in range(4):
        put(ring.at[place], place).wait()


def layer_kernel(
    micro,
    own,
    piece_slots,
    out_count,
    index_ref,
    base_ref,
    slot_ref,
    block_left_ref,
    block_right_ref,
    segments_ref,
    segments_t_ref,
    x_hbm,
    dy_hbm,
    gains_ref,
    *rest,
):
    pieces = rest[: len(piece_slots)]
    rest = rest[len(piece_slots) :]
    out_hbm, token_grad_hbm, gain_ref = rest[:3]
    grad_refs, rest = rest[3 : 3 + out_count], rest[3 + out_count :]
    (
        w_qkv,
        w_o,
        w_gu,
        w_d,
        lefts,
        rights,
        q_scr,
        k_scr,
        v_scr,
        p_scr,
        a_scr,
        act_scr,
        cg_scr,
        cu_scr,
        y1_scr,
        y1_low_scr,
        h1_scr,
        dh2_scr,
        r1_scr,
        w_sems,
        ring,
        ring_sems,
        left_ref,
        right_ref,
        bias_ref,
        cos_ref,
        sin_ref,
        cos_t_ref,
        sin_t_ref,
        x_ref,
        dy_ref,
        out_ref,
        token_grad_ref,
        row_sems,
    ) = rest
    seq = segments_ref.shape[1]
    bring_x = pltpu.make_async_copy(x_hbm, x_ref, row_sems.at[0])
    bring_dy = pltpu.make_async_copy(dy_hbm, dy_ref, row_sems.at[1])
    take_out = pltpu.make_async_copy(out_ref, out_hbm, row_sems.at[2])
    take_token_grad = pltpu.make_async_copy(token_grad_ref, token_grad_hbm, row_sems.at[3])
    bring_x.start()
    bring_dy.start()

    starts = [sum(piece_slots[:n]) for n in range(len(piece_slots) + 1)]
    reciprocal = (1 << 16) // own + 1
    assert all(slot * reciprocal >> 16 == slot // own for slot in range(starts[-1]))

    def fetch(block, target, row, col, sem):
        slot = index_ref[block]
        owner = lax.shift_right_logical(slot * reciprocal, 16)
        place = base_ref[owner] + slot - owner * own

        def among(low, high):
            if high - low > 1:
                middle = (low + high) // 2
                lax.cond(
                    place < starts[middle],
                    lambda: among(low, middle),
                    lambda: among(middle, high),
                )
            else:
                pltpu.make_async_copy(
                    pieces[low].at[place - starts[low]],
                    target.at[
                        pl.ds(pl.multiple_of(row * B, B), B), pl.ds(pl.multiple_of(col * B, B), B)
                    ],
                    sem,
                ).start()

        among(0, len(pieces))

    def fetch_matrix(first_block, grid_rows, grid_cols, target, col_offset, sem):
        def one(t, carry):
            i = t // grid_cols
            j = t - i * grid_cols
            fetch(first_block + t, target, i, j + col_offset, sem)
            return carry

        lax.fori_loop(0, grid_rows * grid_cols, one, 0)

    nd, nf = D // B, FF // B
    for m in range(3):
        fetch_matrix(m * nd * nd, nd, nd, w_qkv, m * nd, w_sems.at[0])

    list_factors(index_ref, block_left_ref, block_right_ref, left_ref, right_ref)
    half_dim = HEAD_DIM // 2
    step = lax.broadcasted_iota(jnp.int32, (half_dim, 1), 0).astype(F32)
    frequency = jnp.exp(step * (-2.0 / HEAD_DIM * math.log(ROPE_BASE)))
    keys = lax.broadcasted_iota(jnp.int32, (seq, seq), 0)
    queries = lax.broadcasted_iota(jnp.int32, (seq, seq), 1)
    for r in range(micro):
        rows = slice(r * seq, (r + 1) * seq)
        same = segments_t_ref[:, r : r + 1] == segments_ref[r : r + 1, :]
        bias_ref[r] = jnp.where(same & (keys <= queries), 0.0, MASKED)
        first = jnp.min(jnp.where(same, keys, seq), axis=0, keepdims=True)
        angles = frequency * (queries[0:1, :] - first).astype(F32)
        cosine_t, sine_t = jnp.cos(angles), jnp.sin(angles)
        cos_t_ref[:, rows] = cosine_t
        sin_t_ref[:, rows] = sine_t
        cosine, sine = cosine_t.T, sine_t.T
        cos_ref[rows, :] = jnp.concatenate([cosine] * 4, axis=1)
        sin_ref[rows, :] = jnp.concatenate([-sine, sine, -sine, sine], axis=1)

    fetch_matrix(3 * nd * nd, nd, nd, w_o, 0, w_sems.at[1])
    for m in range(2):
        fetch_matrix(4 * nd * nd + m * nd * nf, nd, nf, w_gu, m * nf, w_sems.at[2])
    fetch_matrix(4 * nd * nd + 2 * nd * nf, nf, nd, w_d, 0, w_sems.at[3])

    def wait_for(target, sem):
        pltpu.make_async_copy(target, target, sem).wait()

    bring_x.wait()
    lefts[0:D, :] = x_ref[...].T
    lane = lax.broadcasted_iota(jnp.int32, (1, 128), 1)
    low_half = lax.rem(lane, HEAD_DIM) < HEAD_DIM // 2
    head_lanes = [lane < HEAD_DIM, lane >= HEAD_DIM]

    def of_head(values, h):
        return jnp.where(head_lanes[h], values, jnp.zeros_like(values))

    wait_for(w_qkv, w_sems.at[0])

    def attend(jb, carry):
        def columns(offset):
            return pl.ds(pl.multiple_of(offset + jb * B, B), B)

        x = x_ref[...]
        q_raw = dot_nn(x, w_qkv[:, columns(0)])
        k_raw = dot_nn(x, w_qkv[:, columns(D)])
        v_raw = dot_nn(x, w_qkv[:, columns(2 * D)])
        cosine = cos_ref[...]
        sine = sin_ref[...]
        for sub in range(2):
            part = slice(sub * 128, sub * 128 + 128)
            slab = pl.ds(pl.multiple_of(jb * B + sub * 128, 128), 128)
            q = q_raw[:, part]
            k = k_raw[:, part]
            q = ((q * cosine + half_swap(q, low_half) * sine) * HEAD_DIM**-0.5).astype(BF16)
            k = (k * cosine + half_swap(k, low_half) * sine).astype(BF16)
            v = v_raw[:, part].astype(BF16)
            q_scr[:, slab] = q
            k_scr[:, slab] = k
            v_scr[:, slab] = v
            for r in range(micro):
                rows = slice(r * seq, (r + 1) * seq)
                v_t = v[rows].T
                outs = []
                for h in range(2):
                    scores = dot_nt(k[rows], of_head(q[rows], h)) + bias_ref[r]
                    top = jnp.max(scores, axis=0, keepdims=True)
                    exps = jnp.exp(scores - top)
                    total = jnp.sum(exps, axis=0, keepdims=True)
                    probs = (exps * (1.0 / total)).astype(BF16)
                    p_scr[(jb * 2 + sub) * 2 * micro + 2 * r + h] = probs
                    outs.append(dot_nn(v_t[h * HEAD_DIM : (h + 1) * HEAD_DIM], probs))
                a_t = jnp.concatenate(outs, axis=0).astype(BF16)
                lefts[pl.ds(pl.multiple_of(D + jb * B + sub * 128, 128), 128), rows] = a_t
                a_scr[rows, slab] = a_t.T
        return carry

    lax.fori_loop(0, nd, attend, 0)

    wait_for(w_o, w_sems.at[1])
    for r in range(micro):
        rows = slice(r * seq, (r + 1) * seq)
        h1 = x_ref[rows, :].astype(F32) + dot_nn(a_scr[rows, :], w_o[...])
        r1 = lax.rsqrt(jnp.mean(h1 * h1, axis=-1, keepdims=True) + NORM_EPS)
        y1 = h1 * r1 * gains_ref[0:1, :]
        y1_low = y1.astype(BF16)
        h1_scr[rows, :] = h1
        r1_scr[rows, :] = r1
        y1_scr[rows, :] = y1
        y1_low_scr[rows, :] = y1_low
        lefts[2 * D : 3 * D, rows] = y1_low.T

    wait_for(w_gu, w_sems.at[2])

    def feed(j, carry):
        y1_low = y1_low_scr[...]
        cols = pl.ds(pl.multiple_of(j * B, B), B)
        gate = dot_nn(y1_low, w_gu[:, cols])
        up = dot_nn(y1_low, w_gu[:, pl.ds(pl.multiple_of(FF + j * B, B), B)])
        sig = 1.0 / (1.0 + jnp.exp(-gate))
        silu = gate * sig
        act = (silu * up).astype(BF16)
        act_scr[:, cols] = act
        cu_scr[:, cols] = silu.astype(BF16)
        cg_scr[:, cols] = (up * sig * (1.0 + gate * (1.0 - sig))).astype(BF16)
        lefts[pl.ds(pl.multiple_of(3 * D + j * B, B), B), :] = act.T
        return carry

    lax.fori_loop(0, nf, feed, 0, unroll=2)

    wait_for(w_d, w_sems.at[3])
    bring_dy.wait()
    gain_two = jnp.zeros((1, D), F32)
    for r in range(micro):
        rows = slice(r * seq, (r + 1) * seq)
        h2 = y1_scr[rows, :] + dot_nn(act_scr[rows, :], w_d[...])
        r2 = lax.rsqrt(jnp.mean(h2 * h2, axis=-1, keepdims=True) + NORM_EPS)
        scaled = h2 * r2
        gain = gains_ref[1:2, :]
        out_ref[rows, :] = (scaled * gain).astype(BF16)
        dy = dy_ref[rows, :].astype(F32)
        gain_two += jnp.sum(dy * scaled, axis=0, keepdims=True)
        dyg = dy * gain
        dh2 = r2 * (dyg - scaled * jnp.mean(scaled * dyg, axis=-1, keepdims=True))
        dh2_scr[rows, :] = dh2
        rights[rows, RIGHT_D:] = dh2.astype(BF16)
    gain_ref[1:2, :] = gain_two
    take_out.start()

    def feed_back(j, carry):
        cols = pl.ds(pl.multiple_of(j * B, B), B)
        dact = dot_nt(rights[:, RIGHT_D:], w_d[cols, :])
        rights[:, pl.ds(pl.multiple_of(RIGHT_G + j * B, B), B)] = (
            dact * cg_scr[:, cols].astype(F32)
        ).astype(BF16)
        rights[:, pl.ds(pl.multiple_of(RIGHT_U + j * B, B), B)] = (
            dact * cu_scr[:, cols].astype(F32)
        ).astype(BF16)
        return carry

    lax.fori_loop(0, nf, feed_back, 0)

    def feed_in(j, carry):
        cols = pl.ds(pl.multiple_of(j * B, B), B)
        dh2_scr[:, cols] += dot_nt(rights[:, RIGHT_G:RIGHT_D], w_gu[cols, :])
        return carry

    lax.fori_loop(0, nd, feed_in, 0)

    gain_one = jnp.zeros((1, D), F32)
    for r in range(micro):
        rows = slice(r * seq, (r + 1) * seq)
        dy1 = dh2_scr[rows, :]
        r1 = r1_scr[rows, :]
        scaled = h1_scr[rows, :] * r1
        gain_one += jnp.sum(dy1 * scaled, axis=0, keepdims=True)
        dyg = dy1 * gains_ref[0:1, :]
        dh1 = r1 * (dyg - scaled * jnp.mean(scaled * dyg, axis=-1, keepdims=True))
        h1_scr[rows, :] = dh1
        do = dh1.astype(BF16)
        rights[rows, RIGHT_O : RIGHT_O + D] = do
        a_scr[rows, :] = dot_nt(do, w_o[...]).astype(BF16)
    gain_ref[0:1, :] = gain_one

    def attend_back(jb, carry):
        for sub in range(2):
            slab = pl.ds(pl.multiple_of(jb * B + sub * 128, 128), 128)
            for r in range(micro):
                rows = slice(r * seq, (r + 1) * seq)
                q = q_scr[rows, slab]
                k = k_scr[rows, slab]
                v = v_scr[rows, slab]
                da = a_scr[rows, slab]
                k_t = k.T
                dv = jnp.zeros((seq, 128), F32)
                dk = jnp.zeros((seq, 128), F32)
                dq_t = []
                for h in range(2):
                    probs = p_scr[(jb * 2 + sub) * 2 * micro + 2 * r + h]
                    da_h = of_head(da, h)
                    probs_wide = probs.astype(F32)
                    dprobs = dot_nt(v, da_h)
                    weighted = probs_wide * dprobs
                    row_sum = jnp.sum(weighted, axis=0, keepdims=True)
                    ds = (weighted - probs_wide * row_sum).astype(BF16)
                    dv += dot_nn(probs, da_h)
                    dk += dot_nn(ds, of_head(q, h))
                    dq_h = dot_nn(k_t[h * HEAD_DIM : (h + 1) * HEAD_DIM], ds) * HEAD_DIM**-0.5
                    low, high = dq_h[: HEAD_DIM // 2], dq_h[HEAD_DIM // 2 :]
                    cosine = cos_t_ref[:, rows]
                    sine = sin_t_ref[:, rows]
                    dq_t.append(low * cosine + high * sine)
                    dq_t.append(high * cosine - low * sine)
                dq = jnp.concatenate(dq_t, axis=0).astype(BF16).T
                dk = dk * cos_ref[rows, :] - half_swap(dk, low_half) * sin_ref[rows, :]
                rights[rows, slab] = dq
                rights[rows, pl.ds(pl.multiple_of(RIGHT_K + jb * B + sub * 128, 128), 128)] = (
                    dk.astype(BF16)
                )
                rights[rows, pl.ds(pl.multiple_of(RIGHT_V + jb * B + sub * 128, 128), 128)] = (
                    dv.astype(BF16)
                )
        return carry

    lax.fori_loop(0, nd, attend_back, 0)

    def token_back(j, carry):
        cols = pl.ds(pl.multiple_of(j * B, B), B)
        token_grad_ref[:, cols] = (
            h1_scr[:, cols] + dot_nt(rights[:, : 3 * D], w_qkv[cols, :])
        ).astype(BF16)
        return carry

    lax.fori_loop(0, nd, token_back, 0)
    take_token_grad.start()

    weigh_slots(slot_ref, left_ref, right_ref, lefts, rights, grad_refs, ring, ring_sems)
    take_out.wait()
    take_token_grad.wait()


def run_layer(
    tokens, cotangent, segment_ids, block_slot_index, norm_gains, pieces, own, bases, slot_order,
    out_sizes,
):
    micro, seq = segment_ids.shape
    count = micro * seq
    slots = own * bases.shape[0]
    grads = [jax.ShapeDtypeStruct((size, B, B), BF16) for size in out_sizes]
    vmem = pl.BlockSpec(memory_space=pltpu.VMEM)
    smem = pl.BlockSpec(memory_space=pltpu.SMEM)
    hbm = pl.BlockSpec(memory_space=pl.ANY)
    return pl.pallas_call(
        functools.partial(layer_kernel, micro, own, [p.shape[0] for p in pieces], len(grads)),
        out_shape=(
            jax.ShapeDtypeStruct((count, D), BF16),
            jax.ShapeDtypeStruct((count, D), BF16),
            jax.ShapeDtypeStruct((2, D), F32),
            *grads,
        ),
        in_specs=[smem] * 5 + [vmem] * 2 + [hbm] * 2 + [vmem] + [hbm] * len(pieces),
        out_specs=(hbm, hbm, vmem) + (hbm,) * len(grads),
        scratch_shapes=[
            pltpu.VMEM((D, 3 * D), BF16),
            pltpu.VMEM((D, D), BF16),
            pltpu.VMEM((D, 2 * FF), BF16),
            pltpu.VMEM((FF, D), BF16),
            pltpu.VMEM((LEFT_ROWS, count), BF16),
            pltpu.VMEM((count, RIGHT_COLS), BF16),
            pltpu.VMEM((count, D), BF16),
            pltpu.VMEM((count, D), BF16),
            pltpu.VMEM((count, D), BF16),
            pltpu.VMEM((HEADS * micro, seq, seq), BF16),
            pltpu.VMEM((count, D), BF16),
            pltpu.VMEM((count, FF), BF16),
            pltpu.VMEM((count, FF), BF16),
            pltpu.VMEM((count, FF), BF16),
            pltpu.VMEM((count, D), F32),
            pltpu.VMEM((count, D), BF16),
            pltpu.VMEM((count, D), F32),
            pltpu.VMEM((count, D), F32),
            pltpu.VMEM((count, 1), F32),
            pltpu.SemaphoreType.DMA((4,)),
            pltpu.VMEM((4, WEIGH_COPY, B, B), BF16),
            pltpu.SemaphoreType.DMA((4,)),
            pltpu.SMEM((slots,), jnp.int32),
            pltpu.SMEM((slots,), jnp.int32),
            pltpu.VMEM((micro, seq, seq), F32),
            pltpu.VMEM((count, 128), F32),
            pltpu.VMEM((count, 128), F32),
            pltpu.VMEM((HEAD_DIM // 2, count), F32),
            pltpu.VMEM((HEAD_DIM // 2, count), F32),
            *(pltpu.VMEM((count, D), BF16) for _ in range(4)),
            pltpu.SemaphoreType.DMA((4,)),
        ],
        compiler_params=pltpu.CompilerParams(vmem_limit_bytes=56 * MIB),
        cost_estimate=pl.CostEstimate(
            flops=23_000_000_000, bytes_accessed=32_000_000, transcendentals=3_000_000
        ),
        name="layer",
    )(
        block_slot_index,
        bases,
        slot_order,
        *(jnp.asarray(table) for table in factor_tables()),
        segment_ids,
        segment_ids.T,
        tokens,
        cotangent,
        norm_gains,
        *pieces,
    )


def split_two(values):
    high = values.astype(BF16)
    return high, (values - high.astype(F32)).astype(BF16)


def adam_kernel(steps, weight_ref, first_ref, second_ref, left_ref, right_ref, *rest):
    grad_refs = rest[: len(steps)]
    grad_out, first_out, second_out, weight_out, low_out, grads = rest[-6:]
    now, start = pl.program_id(0), 0
    for count, grad_ref in zip(steps, grad_refs):

        @pl.when((now >= start) & (now < start + count))
        def _(grad_ref=grad_ref):
            grads[...] = grad_ref[...]

        start += count
    for n in range(weight_ref.shape[0]):
        grad = grads[n * B : (n + 1) * B, :]
        left, left_rest = split_two(left_ref[n])
        right, right_rest = split_two(right_ref[n])
        grad_out[n] = grad.astype(F32)
        turned = (dot_nn(grad, right) + dot_nn(grad, right_rest)).astype(BF16)
        turned = dot_nn(left.T, turned) + dot_nn(left_rest.T, turned)
        first_new = BETA_ONE * first_ref[n] + (1.0 - BETA_ONE) * turned
        second_new = BETA_TWO * second_ref[n] + (1.0 - BETA_TWO) * turned * turned
        first_out[n] = first_new
        second_out[n] = second_new
        ratio = (
            first_new
            / (1.0 - BETA_ONE**STEP)
            / (jnp.sqrt(second_new / (1.0 - BETA_TWO**STEP)) + ADAM_EPS)
        )
        back = dot_nt(dot_nn(left, ratio.astype(BF16)).astype(BF16), right)
        weight = weight_ref[n]
        weight_new = weight - RATE * (back + DECAY * weight)
        weight_out[n] = weight_new
        low_out[n] = weight_new.astype(BF16)


def adam_blocks(grads, start, state, done):
    own = state[0].shape[0]
    step = math.gcd(2, start, *(part.shape[0] // B for part in grads))
    steps = [part.shape[0] // B // step for part in grads]
    local = []
    for number, count in enumerate(steps):
        local.append(
            pl.BlockSpec(
                (step * B, B),
                lambda s, first=sum(steps[:number]), count=count: (
                    jnp.clip(s - first, 0, count - 1),
                    0,
                ),
            )
        )
    spec = pl.BlockSpec((step, B, B), lambda s: (s + start // step, 0, 0))
    hbm = pl.BlockSpec(memory_space=pl.ANY)
    wide = jax.ShapeDtypeStruct((own, B, B), F32)
    return pl.pallas_call(
        functools.partial(adam_kernel, steps),
        grid=(sum(steps),),
        out_shape=(wide, wide, wide, wide, jax.ShapeDtypeStruct((own, B, B), BF16)),
        in_specs=[spec] * 5 + local + [hbm] * len(done),
        out_specs=(spec,) * 5,
        input_output_aliases={5 + len(local) + n: n for n in range(len(done))},
        scratch_shapes=[pltpu.VMEM((step * B, B), BF16)],
        compiler_params=pltpu.CompilerParams(vmem_limit_bytes=60 * MIB),
        cost_estimate=pl.CostEstimate(
            flops=sum(steps) * step * 12 * B**3,
            bytes_accessed=sum(steps) * step * B * B * 42,
            transcendentals=sum(steps) * step * B * B,
        ),
        name="adam",
    )(*state, *grads, *done)


def adam_plain(grads, values, first_moment, second_moment):
    first_new = BETA_ONE * first_moment + (1.0 - BETA_ONE) * grads
    second_new = BETA_TWO * second_moment + (1.0 - BETA_TWO) * grads * grads
    step_ratio = (
        first_new
        / (1.0 - BETA_ONE**STEP)
        / (jnp.sqrt(second_new / (1.0 - BETA_TWO**STEP)) + ADAM_EPS)
    )
    return (first_new, second_new, values - GAIN_RATE * step_ratio)


def sum_everywhere(values, axis):
    size = lax.axis_size(axis)
    if size & (size - 1):
        return lax.psum(values, axis)
    reach = 1
    while reach < size:
        values = values + lax.ppermute(values, axis, [(i, i ^ reach) for i in range(size)])
        reach *= 2
    return values


def add_low(*terms):
    return sum(term.astype(F32) for term in terms).astype(BF16)


CORE, ACROSS, ALONG = 1, 2, 4
DIAGONAL = ACROSS | ALONG


def exchange(values, bit):
    return lax.ppermute(values, "fsdp", [(i, i ^ bit) for i in range(lax.axis_size("fsdp"))])


def core_neighbours(me):
    near = jnp.where((me & CORE) == 0, ACROSS, ALONG)
    return near, DIAGONAL ^ near


def plane_pairs(owners):
    near = [(i, i ^ (ALONG if i & CORE else ACROSS)) for i in range(owners)]
    far = [(i, i ^ (ACROSS if i & CORE else ALONG)) for i in range(owners)]
    return near, far


def after(values, *others):
    return lax.optimization_barrier((values, *others))[0]


def gather_pieces(weights, me):
    own = weights.shape[0]
    half = own // 2
    near, far = core_neighbours(me)
    near_pairs, far_pairs = plane_pairs(lax.axis_size("fsdp"))
    mine = weights.astype(BF16)
    first_near = lax.ppermute(weights[:half].astype(BF16), "fsdp", near_pairs)
    last_near = lax.ppermute(weights[half:].astype(BF16), "fsdp", near_pairs)
    all_far = lax.ppermute(mine, "fsdp", far_pairs)
    first_diagonal = lax.ppermute(first_near, "fsdp", far_pairs)
    last_diagonal = lax.ppermute(last_near, "fsdp", far_pairs)
    pieces, relations = [], []
    for parts, relation, others in (
        ((mine,), 0, 0),
        ((first_near, last_near), near, far),
        ((all_far,), far, near),
        ((first_diagonal, last_diagonal), DIAGONAL, DIAGONAL),
    ):
        pieces += [*parts, *(exchange(part, CORE) for part in parts)]
        relations += [relation, others | CORE]
    owners = me ^ jnp.stack(relations).astype(jnp.int32)
    bases = jnp.sum(
        jnp.where(
            jnp.arange(len(relations), dtype=jnp.int32)[:, None] == owners[None, :],
            jnp.arange(len(relations), dtype=jnp.int32)[None, :] * own,
            0,
        ),
        axis=1,
    )
    return pieces, bases


class Plan:
    def __init__(self):
        self.tasks = {}

    def core(self, name, needs, run):
        self.tasks[name] = (True, needs, run)

    def send(self, name, needs, run):
        self.tasks[name] = (False, needs, run)

    def run(self, order):
        assert sorted(order) == sorted(self.tasks)
        values, last = {}, None
        for name in order:
            on_core, needs, run = self.tasks[name]
            inputs = [values[n] for n in needs]
            if last is not None:
                *inputs, _ = lax.optimization_barrier((*inputs, last))
            values[name] = run(*inputs)
            if on_core:
                last = jax.tree.leaves(values[name])[0]
        return values


GROUPS = (((4,),), ((6,), (4,)))
ORDER = (
    "grads0 grads1 core0 gain_far near_sum0 near0 core1 near_sum1 near1 gain1 far_sum0_0 far0_0 plane_sum0_0 "
    "inward0_0a halfway0_0a middle0_0a far_sum1_0 far1_0 far_sum1_1 far1_1 gain_near whole0_0a outward0_0a "
    "plane_sum1_0 inward1_0a plane_sum1_1 inward1_1a gain2 gain_core halfway1_0a middle1_0a final0_0a gain3 "
    "gain_pair halfway1_1a middle1_1a whole1_0a outward1_0a step0_0 whole1_1a outward1_1a final1_0a gain4 "
    "gain_line step1_0 gain5 final1_1a step1_1"
).split()


def group_sizes():
    return [sum(sum(parts) for parts in sets) for sets in GROUPS]


def slot_order_of(me, own):
    near, far = core_neighbours(me)
    relations = [DIAGONAL | CORE, far | CORE, near | CORE, CORE, DIAGONAL, near, far, 0]
    slots, start = [], 0
    for size in group_sizes():
        for relation in relations:
            slots.append((me ^ relation) * own + start + jnp.arange(size, dtype=jnp.int32))
        start += size
    return jnp.concatenate(slots).astype(jnp.int32)


def flat(blocks):
    return blocks.reshape(-1, B)


def reduce_and_step(me, own, grads, state, gain_grad):
    plan = Plan()
    owners = lax.axis_size("fsdp")
    near_pairs, far_pairs = plane_pairs(owners)
    place = lax.axis_index("rep")
    inner = (place == 1) | (place == 2)
    done = ()
    start = 0

    for number, sets in enumerate(GROUPS):
        total = group_sizes()[number]

        def name(text, number=number):
            return text + str(number)

        both = [name("grads"), name("core")]

        def chip(pair, arrived, first, last):
            return flat(pair[1][first:last]), flat(arrived[first:last])

        plan.core(
            name("grads"), [],
            lambda pair=grads[2 * number : 2 * number + 2]: pair,
        )
        plan.send(name("core"), [name("grads")], lambda pair: exchange(pair[0], CORE))
        plan.core(
            name("near_sum"), both,
            lambda pair, arrived, total=total: add_low(*chip(pair, arrived, 0, 2 * total)),
        )
        plan.send(
            name("near"), [name("near_sum")], lambda t: lax.ppermute(t, "fsdp", near_pairs)
        )
        inside = 0
        for member, parts in enumerate(sets):
            size = sum(parts)
            finals = []

            def at(text, number=number, member=member):
                return "%s%d_%d" % (text, number, member)

            def far_sum(pair, arrived, r, inside=inside, size=size, total=total):
                first = 2 * total + inside
                return add_low(
                    *chip(pair, arrived, first, first + size), r[inside * B : (inside + size) * B]
                )

            plan.core(at("far_sum"), both + [name("near")], far_sum)
            plan.send(
                at("far"), [at("far_sum")], lambda t: lax.ppermute(t, "fsdp", far_pairs)
            )
            firsts = [sum(parts[:p]) for p in range(len(parts) + 1)]

            def plane_sum(pair, arrived, r, q, inside=inside, total=total, firsts=firsts):
                sums = []
                for a, b in zip(firsts[:-1], firsts[1:]):
                    first, last = inside + a, inside + b
                    sums.append(
                        add_low(
                            *chip(pair, arrived, 3 * total + first, 3 * total + last),
                            r[(total + first) * B : (total + last) * B],
                            q[a * B : b * B],
                        )
                    )
                return sums

            plan.core(at("plane_sum"), both + [name("near"), at("far")], plane_sum)
            for part in range(len(parts)):

                def of(text, part=part, at=at):
                    return at(text) + "abcd"[part]

                plan.send(
                    of("inward"), [at("plane_sum")],
                    lambda t, part=part: lax.ppermute(t[part], "rep", [(0, 1), (3, 2)]),
                )
                plan.core(
                    of("halfway"), [at("plane_sum"), of("inward")],
                    lambda t, r, part=part: add_low(t[part], r),
                )
                plan.send(
                    of("middle"), [of("halfway")],
                    lambda t: lax.ppermute(t, "rep", [(1, 2), (2, 1)]),
                )
                plan.core(of("whole"), [of("halfway"), of("middle")], add_low)
                plan.send(
                    of("outward"), [of("whole")],
                    lambda t: lax.ppermute(t, "rep", [(1, 0), (2, 3)]),
                )
                plan.core(
                    of("final"), [of("whole"), of("outward")],
                    lambda whole, outward: jnp.where(inner, whole, outward),
                )
                finals.append(of("final"))
            inside += size

            def step(*grads, start=start):
                nonlocal done
                done = adam_blocks(grads, start, state, done)
                return done

            plan.core(at("step"), finals, step)
            start += size

    old = None
    line = [[(i, i ^ bit) for i in range(4)] for bit in (1, 2)]
    for n, (text, axis, pairs) in enumerate(
        (("far", "fsdp", far_pairs), ("near", "fsdp", near_pairs),
         ("core", "fsdp", [(i, i ^ CORE) for i in range(owners)]),
         ("pair", "rep", line[0]), ("line", "rep", line[1]))
    ):
        plan.send(
            "gain_" + text, [old] if old else [],
            lambda gain=gain_grad, axis=axis, pairs=pairs: lax.ppermute(gain, axis, pairs),
        )
        new = "gain" + str(n + 1)
        if old:
            plan.core(new, [old, "gain_" + text], lambda a, b: a + b)
        else:
            plan.core(new, ["gain_" + text], lambda b: gain_grad + b)
        old = new
    values = plan.run(ORDER)
    return done, values[old]


def shards(
    tokens,
    cotangent,
    segment_ids,
    block_slot_index,
    weights,
    first_moment,
    second_moment,
    left_basis,
    right_basis,
    norm_gains,
    gain_first,
    gain_second,
):
    owners = lax.axis_size("fsdp")
    own = weights.shape[0]
    slots = own * owners
    me = lax.axis_index("fsdp")
    state = (weights, first_moment, second_moment, left_basis, right_basis)
    small = owners == 8 and lax.axis_size("rep") == 4 and own == sum(group_sizes())

    if small:
        pieces, bases = gather_pieces(weights, me)
        slot_order = slot_order_of(me, own)
        out_sizes = [4 * size for size in group_sizes() for _ in range(2)]
    else:
        pieces = [lax.all_gather(weights.astype(BF16), "fsdp", axis=0, tiled=True)]
        bases = jnp.arange(owners, dtype=jnp.int32) * own
        slot_order = jnp.arange(slots, dtype=jnp.int32)
        out_sizes = [slots]
    block_out, token_grad, gain_grad, *grads = run_layer(
        tokens, cotangent, segment_ids, block_slot_index, norm_gains, pieces, own, bases,
        slot_order, out_sizes,
    )
    if small:
        done, gain_grads = reduce_and_step(me, own, grads, state, gain_grad)
    else:
        owner_sums = lax.psum_scatter(
            grads[0], "fsdp", scatter_dimension=0, tiled=True
        )
        owner_grads = flat(lax.psum(owner_sums, "rep"))
        done = adam_blocks([owner_grads], 0, state, ())
        gain_grads = sum_everywhere(sum_everywhere(gain_grad, "fsdp"), "rep")
    grads_wide, first_new, second_new, weights_new, weights_low = done
    gain_first_new, gain_second_new, gains_new = adam_plain(
        gain_grads, norm_gains, gain_first, gain_second
    )
    return (
        block_out,
        token_grad,
        grads_wide,
        first_new,
        second_new,
        weights_new,
        weights_low,
        gain_first_new,
        gain_second_new,
        gains_new,
    )


def solution(mesh):
    return jax.shard_map(
        shards,
        mesh=mesh,
        in_specs=(
            P(("fsdp", "rep"), None),
            P(("fsdp", "rep"), None),
            P(("fsdp", "rep"), None),
            P(),
            P("fsdp", None, None),
            P("fsdp", None, None),
            P("fsdp", None, None),
            P("fsdp", None, None),
            P("fsdp", None, None),
            P(),
            P(),
            P(),
        ),
        out_specs=(
            P(("fsdp", "rep"), None),
            P(("fsdp", "rep"), None),
            P("fsdp", None, None),
            P("fsdp", None, None),
            P("fsdp", None, None),
            P("fsdp", None, None),
            P("fsdp", None, None),
            P(),
            P(),
            P(),
        ),
        check_vma=False,
    )
```

```python
import functools
import math

import jax
import jax.numpy as jnp
import numpy as np
from jax import lax
from jax.experimental import pallas as pl
from jax.experimental.pallas import tpu as pltpu
from jax.sharding import PartitionSpec as P

D = 768
HEADS = 12
HEAD_DIM = 64
FF = 2048
BLOCK_ORDER = 256
STEP = 10


NORM_EPS = 1e-05
ROPE_BASE = 10000.0
BETA_ONE = 0.5
BETA_TWO = 0.5
ADAM_EPS = 1e-08
RATE = 0.03
GAIN_RATE = 0.4
DECAY = 0.01
MASKED = -1e30

B = BLOCK_ORDER
BF16 = jnp.bfloat16
F32 = jnp.float32
MIB = 1024 * 1024

LEFT_X, LEFT_A, LEFT_Y, LEFT_ACT = 0, D // B, 2 * D // B, 3 * D // B
LEFT_ROWS = 3 * D + FF
RIGHT_Q, RIGHT_K, RIGHT_V, RIGHT_O = 0, D, 2 * D, 3 * D
RIGHT_G, RIGHT_U, RIGHT_D = 4 * D, 4 * D + FF, 4 * D + 2 * FF
RIGHT_COLS = 5 * D + 2 * FF


def matrix_table():
    return [
        (D // B, D // B, LEFT_X, RIGHT_Q // B),
        (D // B, D // B, LEFT_X, RIGHT_K // B),
        (D // B, D // B, LEFT_X, RIGHT_V // B),
        (D // B, D // B, LEFT_A, RIGHT_O // B),
        (D // B, FF // B, LEFT_Y, RIGHT_G // B),
        (D // B, FF // B, LEFT_Y, RIGHT_U // B),
        (FF // B, D // B, LEFT_ACT, RIGHT_D // B),
    ]


def factor_tables():
    lefts, rights = [], []
    for grid_rows, grid_cols, left, right in matrix_table():
        for i in range(grid_rows):
            for j in range(grid_cols):
                lefts.append(left + i)
                rights.append(right + j)
    return np.array(lefts, np.int32), np.array(rights, np.int32)


def dot_nn(a, b):
    return jnp.dot(a, b, preferred_element_type=F32)


def dot_nt(a, b):
    return lax.dot_general(a, b, (((1,), (1,)), ((), ())), preferred_element_type=F32)


def half_swap(values, low_half):
    return jnp.where(low_half, pltpu.roll(values, 96, 1), pltpu.roll(values, 32, 1))


def list_factors(index_ref, block_left_ref, block_right_ref, left_ref, right_ref):
    def clear(g, carry):
        for n in range(4):
            left_ref[4 * g + n] = -1
            right_ref[4 * g + n] = 0
        return carry

    lax.fori_loop(0, left_ref.shape[0] // 4, clear, 0)

    def enter(g, carry):
        for n in range(4):
            slot = index_ref[4 * g + n]
            left_ref[slot] = block_left_ref[4 * g + n]
            right_ref[slot] = block_right_ref[4 * g + n]
        return carry

    lax.fori_loop(0, index_ref.shape[0] // 4, enter, 0)


WEIGH_COPY = 4


def weigh_slots(slot_ref, left_ref, right_ref, lefts, rights, outs, ring, sems):
    copies = [out.shape[0] // WEIGH_COPY for out in outs]
    total = sum(copies)
    assert total % 2 == 0

    def put(target, place):
        return pltpu.make_async_copy(ring.at[place], target, sems.at[place])

    def run(g, carry):
        first_place = 2 * lax.rem(g, 2)
        for half in range(2):

            @pl.when(g >= 2)
            def _(half=half):
                put(ring.at[first_place + half], first_place + half).wait()

        for n in range(2 * WEIGH_COPY):
            slot = slot_ref[2 * g * WEIGH_COPY + n]
            left = left_ref[slot]
            grad = dot_nn(
                lefts[pl.ds(pl.multiple_of(jnp.maximum(left, 0) * B, B), B), :],
                rights[:, pl.ds(pl.multiple_of(right_ref[slot] * B, B), B)],
            )
            keep = jnp.where(left >= 0, 1.0, 0.0)
            ring[first_place + n // WEIGH_COPY, n % WEIGH_COPY] = (grad * keep).astype(BF16)
        for half in range(2):
            copy = 2 * g + half
            first = 0
            for out, count in zip(outs, copies):

                @pl.when((copy >= first) & (copy < first + count))
                def _(out=out, first=first, half=half, copy=copy):
                    at = pl.ds((copy - first) * WEIGH_COPY, WEIGH_COPY)
                    put(out.at[at], first_place + half).start()

                first += count
        return carry

    assert total >= 4
    lax.fori_loop(0, total // 2, run, 0)
    for place in range(4):
        put(ring.at[place], place).wait()


def layer_kernel(
    micro,
    own,
    piece_slots,
    out_count,
    index_ref,
    base_ref,
    slot_ref,
    block_left_ref,
    block_right_ref,
    segments_ref,
    segments_t_ref,
    x_hbm,
    dy_hbm,
    gains_ref,
    *rest,
):
    pieces = rest[: len(piece_slots)]
    rest = rest[len(piece_slots) :]
    out_hbm, token_grad_hbm, gain_ref = rest[:3]
    grad_refs, rest = rest[3 : 3 + out_count], rest[3 + out_count :]
    (
        w_qkv,
        w_o,
        w_gu,
        w_d,
        lefts,
        rights,
        q_scr,
        k_scr,
        v_scr,
        p_scr,
        a_scr,
        act_scr,
        cg_scr,
        cu_scr,
        y1_scr,
        y1_low_scr,
        h1_scr,
        dh2_scr,
        r1_scr,
        w_sems,
        ring,
        ring_sems,
        left_ref,
        right_ref,
        bias_ref,
        cos_ref,
        sin_ref,
        cos_t_ref,
        sin_t_ref,
        x_ref,
        dy_ref,
        out_ref,
        token_grad_ref,
        row_sems,
    ) = rest
    seq = segments_ref.shape[1]
    bring_x = pltpu.make_async_copy(x_hbm, x_ref, row_sems.at[0])
    bring_dy = pltpu.make_async_copy(dy_hbm, dy_ref, row_sems.at[1])
    take_out = pltpu.make_async_copy(out_ref, out_hbm, row_sems.at[2])
    take_token_grad = pltpu.make_async_copy(token_grad_ref, token_grad_hbm, row_sems.at[3])
    bring_x.start()
    bring_dy.start()

    starts = [sum(piece_slots[:n]) for n in range(len(piece_slots) + 1)]
    reciprocal = (1 << 16) // own + 1
    assert all(slot * reciprocal >> 16 == slot // own for slot in range(starts[-1]))

    def fetch(block, target, row, col, sem):
        slot = index_ref[block]
        owner = lax.shift_right_logical(slot * reciprocal, 16)
        place = base_ref[owner] + slot - owner * own

        def among(low, high):
            if high - low > 1:
                middle = (low + high) // 2
                lax.cond(
                    place < starts[middle],
                    lambda: among(low, middle),
                    lambda: among(middle, high),
                )
            else:
                pltpu.make_async_copy(
                    pieces[low].at[place - starts[low]],
                    target.at[
                        pl.ds(pl.multiple_of(row * B, B), B), pl.ds(pl.multiple_of(col * B, B), B)
                    ],
                    sem,
                ).start()

        among(0, len(pieces))

    def fetch_matrix(first_block, grid_rows, grid_cols, target, col_offset, sem):
        def one(t, carry):
            i = t // grid_cols
            j = t - i * grid_cols
            fetch(first_block + t, target, i, j + col_offset, sem)
            return carry

        lax.fori_loop(0, grid_rows * grid_cols, one, 0)

    nd, nf = D // B, FF // B
    for m in range(3):
        fetch_matrix(m * nd * nd, nd, nd, w_qkv, m * nd, w_sems.at[0])

    list_factors(index_ref, block_left_ref, block_right_ref, left_ref, right_ref)
    half_dim = HEAD_DIM // 2
    step = lax.broadcasted_iota(jnp.int32, (half_dim, 1), 0).astype(F32)
    frequency = jnp.exp(step * (-2.0 / HEAD_DIM * math.log(ROPE_BASE)))
    keys = lax.broadcasted_iota(jnp.int32, (seq, seq), 0)
    queries = lax.broadcasted_iota(jnp.int32, (seq, seq), 1)
    for r in range(micro):
        rows = slice(r * seq, (r + 1) * seq)
        same = segments_t_ref[:, r : r + 1] == segments_ref[r : r + 1, :]
        bias_ref[r] = jnp.where(same & (keys <= queries), 0.0, MASKED)
        first = jnp.min(jnp.where(same, keys, seq), axis=0, keepdims=True)
        angles = frequency * (queries[0:1, :] - first).astype(F32)
        cosine_t, sine_t = jnp.cos(angles), jnp.sin(angles)
        cos_t_ref[:, rows] = cosine_t
        sin_t_ref[:, rows] = sine_t
        cosine, sine = cosine_t.T, sine_t.T
        cos_ref[rows, :] = jnp.concatenate([cosine] * 4, axis=1)
        sin_ref[rows, :] = jnp.concatenate([-sine, sine, -sine, sine], axis=1)

    fetch_matrix(3 * nd * nd, nd, nd, w_o, 0, w_sems.at[1])
    for m in range(2):
        fetch_matrix(4 * nd * nd + m * nd * nf, nd, nf, w_gu, m * nf, w_sems.at[2])
    fetch_matrix(4 * nd * nd + 2 * nd * nf, nf, nd, w_d, 0, w_sems.at[3])

    def wait_for(target, sem):
        pltpu.make_async_copy(target, target, sem).wait()

    bring_x.wait()
    lefts[0:D, :] = x_ref[...].T
    lane = lax.broadcasted_iota(jnp.int32, (1, 128), 1)
    low_half = lax.rem(lane, HEAD_DIM) < HEAD_DIM // 2
    head_lanes = [lane < HEAD_DIM, lane >= HEAD_DIM]

    def of_head(values, h):
        return jnp.where(head_lanes[h], values, jnp.zeros_like(values))

    wait_for(w_qkv, w_sems.at[0])

    def attend(jb, carry):
        def columns(offset):
            return pl.ds(pl.multiple_of(offset + jb * B, B), B)

        x = x_ref[...]
        q_raw = dot_nn(x, w_qkv[:, columns(0)])
        k_raw = dot_nn(x, w_qkv[:, columns(D)])
        v_raw = dot_nn(x, w_qkv[:, columns(2 * D)])
        cosine = cos_ref[...]
        sine = sin_ref[...]
        for sub in range(2):
            part = slice(sub * 128, sub * 128 + 128)
            slab = pl.ds(pl.multiple_of(jb * B + sub * 128, 128), 128)
            q = q_raw[:, part]
            k = k_raw[:, part]
            q = ((q * cosine + half_swap(q, low_half) * sine) * HEAD_DIM**-0.5).astype(BF16)
            k = (k * cosine + half_swap(k, low_half) * sine).astype(BF16)
            v = v_raw[:, part].astype(BF16)
            q_scr[:, slab] = q
            k_scr[:, slab] = k
            v_scr[:, slab] = v
            for r in range(micro):
                rows = slice(r * seq, (r + 1) * seq)
                v_t = v[rows].T
                outs = []
                for h in range(2):
                    scores = dot_nt(k[rows], of_head(q[rows], h)) + bias_ref[r]
                    top = jnp.max(scores, axis=0, keepdims=True)
                    exps = jnp.exp(scores - top)
                    total = jnp.sum(exps, axis=0, keepdims=True)
                    probs = (exps * (1.0 / total)).astype(BF16)
                    p_scr[(jb * 2 + sub) * 2 * micro + 2 * r + h] = probs
                    outs.append(dot_nn(v_t[h * HEAD_DIM : (h + 1) * HEAD_DIM], probs))
                a_t = jnp.concatenate(outs, axis=0).astype(BF16)
                lefts[pl.ds(pl.multiple_of(D + jb * B + sub * 128, 128), 128), rows] = a_t
                a_scr[rows, slab] = a_t.T
        return carry

    lax.fori_loop(0, nd, attend, 0, unroll=True)

    wait_for(w_o, w_sems.at[1])
    for r in range(micro):
        rows = slice(r * seq, (r + 1) * seq)
        h1 = x_ref[rows, :].astype(F32) + dot_nn(a_scr[rows, :], w_o[...])
        r1 = lax.rsqrt(jnp.mean(h1 * h1, axis=-1, keepdims=True) + NORM_EPS)
        y1 = h1 * r1 * gains_ref[0:1, :]
        y1_low = y1.astype(BF16)
        h1_scr[rows, :] = h1
        r1_scr[rows, :] = r1
        y1_scr[rows, :] = y1
        y1_low_scr[rows, :] = y1_low
        lefts[2 * D : 3 * D, rows] = y1_low.T

    wait_for(w_gu, w_sems.at[2])

    def feed(j, carry):
        y1_low = y1_low_scr[...]
        cols = pl.ds(pl.multiple_of(j * B, B), B)
        gate = dot_nn(y1_low, w_gu[:, cols])
        up = dot_nn(y1_low, w_gu[:, pl.ds(pl.multiple_of(FF + j * B, B), B)])
        sig = 1.0 / (1.0 + jnp.exp(-gate))
        silu = gate * sig
        act = (silu * up).astype(BF16)
        act_scr[:, cols] = act
        cu_scr[:, cols] = silu.astype(BF16)
        cg_scr[:, cols] = (up * sig * (1.0 + gate * (1.0 - sig))).astype(BF16)
        lefts[pl.ds(pl.multiple_of(3 * D + j * B, B), B), :] = act.T
        return carry

    lax.fori_loop(0, nf, feed, 0, unroll=2)

    wait_for(w_d, w_sems.at[3])
    bring_dy.wait()
    gain_two = jnp.zeros((1, D), F32)
    for r in range(micro):
        rows = slice(r * seq, (r + 1) * seq)
        h2 = y1_scr[rows, :] + dot_nn(act_scr[rows, :], w_d[...])
        r2 = lax.rsqrt(jnp.mean(h2 * h2, axis=-1, keepdims=True) + NORM_EPS)
        scaled = h2 * r2
        gain = gains_ref[1:2, :]
        out_ref[rows, :] = (scaled * gain).astype(BF16)
        dy = dy_ref[rows, :].astype(F32)
        gain_two += jnp.sum(dy * scaled, axis=0, keepdims=True)
        dyg = dy * gain
        dh2 = r2 * (dyg - scaled * jnp.mean(scaled * dyg, axis=-1, keepdims=True))
        dh2_scr[rows, :] = dh2
        rights[rows, RIGHT_D:] = dh2.astype(BF16)
    gain_ref[1:2, :] = gain_two
    take_out.start()

    def feed_back(j, carry):
        cols = pl.ds(pl.multiple_of(j * B, B), B)
        dact = dot_nt(rights[:, RIGHT_D:], w_d[cols, :])
        rights[:, pl.ds(pl.multiple_of(RIGHT_G + j * B, B), B)] = (
            dact * cg_scr[:, cols].astype(F32)
        ).astype(BF16)
        rights[:, pl.ds(pl.multiple_of(RIGHT_U + j * B, B), B)] = (
            dact * cu_scr[:, cols].astype(F32)
        ).astype(BF16)
        return carry

    lax.fori_loop(0, nf, feed_back, 0)

    def feed_in(j, carry):
        cols = pl.ds(pl.multiple_of(j * B, B), B)
        dh2_scr[:, cols] += dot_nt(rights[:, RIGHT_G:RIGHT_D], w_gu[cols, :])
        return carry

    lax.fori_loop(0, nd, feed_in, 0)

    gain_one = jnp.zeros((1, D), F32)
    for r in range(micro):
        rows = slice(r * seq, (r + 1) * seq)
        dy1 = dh2_scr[rows, :]
        r1 = r1_scr[rows, :]
        scaled = h1_scr[rows, :] * r1
        gain_one += jnp.sum(dy1 * scaled, axis=0, keepdims=True)
        dyg = dy1 * gains_ref[0:1, :]
        dh1 = r1 * (dyg - scaled * jnp.mean(scaled * dyg, axis=-1, keepdims=True))
        h1_scr[rows, :] = dh1
        do = dh1.astype(BF16)
        rights[rows, RIGHT_O : RIGHT_O + D] = do
        a_scr[rows, :] = dot_nt(do, w_o[...]).astype(BF16)
    gain_ref[0:1, :] = gain_one

    def attend_back(jb, carry):
        for sub in range(2):
            slab = pl.ds(pl.multiple_of(jb * B + sub * 128, 128), 128)
            for r in range(micro):
                rows = slice(r * seq, (r + 1) * seq)
                q = q_scr[rows, slab]
                k = k_scr[rows, slab]
                v = v_scr[rows, slab]
                da = a_scr[rows, slab]
                k_t = k.T
                dv = jnp.zeros((seq, 128), F32)
                dk = jnp.zeros((seq, 128), F32)
                dq_t = []
                for h in range(2):
                    probs = p_scr[(jb * 2 + sub) * 2 * micro + 2 * r + h]
                    da_h = of_head(da, h)
                    probs_wide = probs.astype(F32)
                    dprobs = dot_nt(v, da_h)
                    weighted = probs_wide * dprobs
                    row_sum = jnp.sum(weighted, axis=0, keepdims=True)
                    ds = (weighted - probs_wide * row_sum).astype(BF16)
                    dv += dot_nn(probs, da_h)
                    dk += dot_nn(ds, of_head(q, h))
                    dq_h = dot_nn(k_t[h * HEAD_DIM : (h + 1) * HEAD_DIM], ds) * HEAD_DIM**-0.5
                    low, high = dq_h[: HEAD_DIM // 2], dq_h[HEAD_DIM // 2 :]
                    cosine = cos_t_ref[:, rows]
                    sine = sin_t_ref[:, rows]
                    dq_t.append(low * cosine + high * sine)
                    dq_t.append(high * cosine - low * sine)
                dq = jnp.concatenate(dq_t, axis=0).astype(BF16).T
                dk = dk * cos_ref[rows, :] - half_swap(dk, low_half) * sin_ref[rows, :]
                rights[rows, slab] = dq
                rights[rows, pl.ds(pl.multiple_of(RIGHT_K + jb * B + sub * 128, 128), 128)] = (
                    dk.astype(BF16)
                )
                rights[rows, pl.ds(pl.multiple_of(RIGHT_V + jb * B + sub * 128, 128), 128)] = (
                    dv.astype(BF16)
                )
        return carry

    lax.fori_loop(0, nd, attend_back, 0, unroll=True)

    def token_back(j, carry):
        cols = pl.ds(pl.multiple_of(j * B, B), B)
        token_grad_ref[:, cols] = (
            h1_scr[:, cols] + dot_nt(rights[:, : 3 * D], w_qkv[cols, :])
        ).astype(BF16)
        return carry

    lax.fori_loop(0, nd, token_back, 0)
    take_token_grad.start()

    weigh_slots(slot_ref, left_ref, right_ref, lefts, rights, grad_refs, ring, ring_sems)
    take_out.wait()
    take_token_grad.wait()


def run_layer(
    tokens, cotangent, segment_ids, block_slot_index, norm_gains, pieces, own, bases, slot_order,
    out_sizes,
):
    micro, seq = segment_ids.shape
    count = micro * seq
    slots = own * bases.shape[0]
    grads = [jax.ShapeDtypeStruct((size, B, B), BF16) for size in out_sizes]
    vmem = pl.BlockSpec(memory_space=pltpu.VMEM)
    smem = pl.BlockSpec(memory_space=pltpu.SMEM)
    hbm = pl.BlockSpec(memory_space=pl.ANY)
    return pl.pallas_call(
        functools.partial(layer_kernel, micro, own, [p.shape[0] for p in pieces], len(grads)),
        out_shape=(
            jax.ShapeDtypeStruct((count, D), BF16),
            jax.ShapeDtypeStruct((count, D), BF16),
            jax.ShapeDtypeStruct((2, D), F32),
            *grads,
        ),
        in_specs=[smem] * 5 + [vmem] * 2 + [hbm] * 2 + [vmem] + [hbm] * len(pieces),
        out_specs=(hbm, hbm, vmem) + (hbm,) * len(grads),
        scratch_shapes=[
            pltpu.VMEM((D, 3 * D), BF16),
            pltpu.VMEM((D, D), BF16),
            pltpu.VMEM((D, 2 * FF), BF16),
            pltpu.VMEM((FF, D), BF16),
            pltpu.VMEM((LEFT_ROWS, count), BF16),
            pltpu.VMEM((count, RIGHT_COLS), BF16),
            pltpu.VMEM((count, D), BF16),
            pltpu.VMEM((count, D), BF16),
            pltpu.VMEM((count, D), BF16),
            pltpu.VMEM((HEADS * micro, seq, seq), BF16),
            pltpu.VMEM((count, D), BF16),
            pltpu.VMEM((count, FF), BF16),
            pltpu.VMEM((count, FF), BF16),
            pltpu.VMEM((count, FF), BF16),
            pltpu.VMEM((count, D), F32),
            pltpu.VMEM((count, D), BF16),
            pltpu.VMEM((count, D), F32),
            pltpu.VMEM((count, D), F32),
            pltpu.VMEM((count, 1), F32),
            pltpu.SemaphoreType.DMA((4,)),
            pltpu.VMEM((4, WEIGH_COPY, B, B), BF16),
            pltpu.SemaphoreType.DMA((4,)),
            pltpu.SMEM((slots,), jnp.int32),
            pltpu.SMEM((slots,), jnp.int32),
            pltpu.VMEM((micro, seq, seq), F32),
            pltpu.VMEM((count, 128), F32),
            pltpu.VMEM((count, 128), F32),
            pltpu.VMEM((HEAD_DIM // 2, count), F32),
            pltpu.VMEM((HEAD_DIM // 2, count), F32),
            *(pltpu.VMEM((count, D), BF16) for _ in range(4)),
            pltpu.SemaphoreType.DMA((4,)),
        ],
        compiler_params=pltpu.CompilerParams(vmem_limit_bytes=56 * MIB),
        cost_estimate=pl.CostEstimate(
            flops=23_000_000_000, bytes_accessed=32_000_000, transcendentals=3_000_000
        ),
        name="layer",
    )(
        block_slot_index,
        bases,
        slot_order,
        *(jnp.asarray(table) for table in factor_tables()),
        segment_ids,
        segment_ids.T,
        tokens,
        cotangent,
        norm_gains,
        *pieces,
    )


def split_two(values):
    high = values.astype(BF16)
    return high, (values - high.astype(F32)).astype(BF16)


def adam_kernel(steps, weight_ref, first_ref, second_ref, left_ref, right_ref, *rest):
    grad_refs = rest[: len(steps)]
    grad_out, first_out, second_out, weight_out, low_out, grads = rest[-6:]
    now, start = pl.program_id(0), 0
    for count, grad_ref in zip(steps, grad_refs):

        @pl.when((now >= start) & (now < start + count))
        def _(grad_ref=grad_ref):
            grads[...] = grad_ref[...]

        start += count
    for n in range(weight_ref.shape[0]):
        grad = grads[n * B : (n + 1) * B, :]
        left, left_rest = split_two(left_ref[n])
        right, right_rest = split_two(right_ref[n])
        grad_out[n] = grad.astype(F32)
        turned = (dot_nn(grad, right) + dot_nn(grad, right_rest)).astype(BF16)
        turned = dot_nn(left.T, turned) + dot_nn(left_rest.T, turned)
        first_new = BETA_ONE * first_ref[n] + (1.0 - BETA_ONE) * turned
        second_new = BETA_TWO * second_ref[n] + (1.0 - BETA_TWO) * turned * turned
        first_out[n] = first_new
        second_out[n] = second_new
        ratio = (
            first_new
            / (1.0 - BETA_ONE**STEP)
            / (jnp.sqrt(second_new / (1.0 - BETA_TWO**STEP)) + ADAM_EPS)
        )
        back = dot_nt(dot_nn(left, ratio.astype(BF16)).astype(BF16), right)
        weight = weight_ref[n]
        weight_new = weight - RATE * (back + DECAY * weight)
        weight_out[n] = weight_new
        low_out[n] = weight_new.astype(BF16)


def adam_blocks(grads, start, state, done):
    own = state[0].shape[0]
    step = math.gcd(2, start, *(part.shape[0] // B for part in grads))
    steps = [part.shape[0] // B // step for part in grads]
    local = []
    for number, count in enumerate(steps):
        local.append(
            pl.BlockSpec(
                (step * B, B),
                lambda s, first=sum(steps[:number]), count=count: (
                    jnp.clip(s - first, 0, count - 1),
                    0,
                ),
            )
        )
    spec = pl.BlockSpec((step, B, B), lambda s: (s + start // step, 0, 0))
    hbm = pl.BlockSpec(memory_space=pl.ANY)
    wide = jax.ShapeDtypeStruct((own, B, B), F32)
    return pl.pallas_call(
        functools.partial(adam_kernel, steps),
        grid=(sum(steps),),
        out_shape=(wide, wide, wide, wide, jax.ShapeDtypeStruct((own, B, B), BF16)),
        in_specs=[spec] * 5 + local + [hbm] * len(done),
        out_specs=(spec,) * 5,
        input_output_aliases={5 + len(local) + n: n for n in range(len(done))},
        scratch_shapes=[pltpu.VMEM((step * B, B), BF16)],
        compiler_params=pltpu.CompilerParams(vmem_limit_bytes=60 * MIB),
        cost_estimate=pl.CostEstimate(
            flops=sum(steps) * step * 12 * B**3,
            bytes_accessed=sum(steps) * step * B * B * 42,
            transcendentals=sum(steps) * step * B * B,
        ),
        name="adam",
    )(*state, *grads, *done)


def adam_plain(grads, values, first_moment, second_moment):
    first_new = BETA_ONE * first_moment + (1.0 - BETA_ONE) * grads
    second_new = BETA_TWO * second_moment + (1.0 - BETA_TWO) * grads * grads
    step_ratio = (
        first_new
        / (1.0 - BETA_ONE**STEP)
        / (jnp.sqrt(second_new / (1.0 - BETA_TWO**STEP)) + ADAM_EPS)
    )
    return (first_new, second_new, values - GAIN_RATE * step_ratio)


def sum_everywhere(values, axis):
    size = lax.axis_size(axis)
    if size & (size - 1):
        return lax.psum(values, axis)
    reach = 1
    while reach < size:
        values = values + lax.ppermute(values, axis, [(i, i ^ reach) for i in range(size)])
        reach *= 2
    return values


def add_low(*terms):
    return sum(term.astype(F32) for term in terms).astype(BF16)


CORE, ACROSS, ALONG = 1, 2, 4
DIAGONAL = ACROSS | ALONG


def exchange(values, bit):
    return lax.ppermute(values, "fsdp", [(i, i ^ bit) for i in range(lax.axis_size("fsdp"))])


def core_neighbours(me):
    near = jnp.where((me & CORE) == 0, ACROSS, ALONG)
    return near, DIAGONAL ^ near


def plane_pairs(owners):
    near = [(i, i ^ (ALONG if i & CORE else ACROSS)) for i in range(owners)]
    far = [(i, i ^ (ACROSS if i & CORE else ALONG)) for i in range(owners)]
    return near, far


def after(values, *others):
    return lax.optimization_barrier((values, *others))[0]


def gather_pieces(weights, me):
    own = weights.shape[0]
    half = own // 2
    near, far = core_neighbours(me)
    near_pairs, far_pairs = plane_pairs(lax.axis_size("fsdp"))
    mine = weights.astype(BF16)
    first_near = lax.ppermute(weights[:half].astype(BF16), "fsdp", near_pairs)
    last_near = lax.ppermute(weights[half:].astype(BF16), "fsdp", near_pairs)
    all_far = lax.ppermute(mine, "fsdp", far_pairs)
    first_diagonal = lax.ppermute(first_near, "fsdp", far_pairs)
    last_diagonal = lax.ppermute(last_near, "fsdp", far_pairs)
    pieces, relations = [], []
    for parts, relation, others in (
        ((mine,), 0, 0),
        ((first_near, last_near), near, far),
        ((all_far,), far, near),
        ((first_diagonal, last_diagonal), DIAGONAL, DIAGONAL),
    ):
        pieces += [*parts, *(exchange(part, CORE) for part in parts)]
        relations += [relation, others | CORE]
    owners = me ^ jnp.stack(relations).astype(jnp.int32)
    bases = jnp.sum(
        jnp.where(
            jnp.arange(len(relations), dtype=jnp.int32)[:, None] == owners[None, :],
            jnp.arange(len(relations), dtype=jnp.int32)[None, :] * own,
            0,
        ),
        axis=1,
    )
    return pieces, bases


class Plan:
    def __init__(self):
        self.tasks = {}

    def core(self, name, needs, run):
        self.tasks[name] = (True, needs, run)

    def send(self, name, needs, run):
        self.tasks[name] = (False, needs, run)

    def run(self, order):
        assert sorted(order) == sorted(self.tasks)
        values, last = {}, None
        for name in order:
            on_core, needs, run = self.tasks[name]
            inputs = [values[n] for n in needs]
            if last is not None:
                *inputs, _ = lax.optimization_barrier((*inputs, last))
            values[name] = run(*inputs)
            if on_core:
                last = jax.tree.leaves(values[name])[0]
        return values


GROUPS = (((4,),), ((6,), (4,)))
ORDER = (
    "grads0 grads1 core0 gain_far near_sum0 near0 core1 near_sum1 near1 gain1 far_sum0_0 far0_0 plane_sum0_0 "
    "inward0_0a halfway0_0a middle0_0a far_sum1_0 far1_0 far_sum1_1 far1_1 gain_near whole0_0a outward0_0a "
    "plane_sum1_0 inward1_0a plane_sum1_1 inward1_1a gain2 gain_core halfway1_0a middle1_0a final0_0a gain3 "
    "gain_pair halfway1_1a middle1_1a whole1_0a outward1_0a step0_0 whole1_1a outward1_1a final1_0a gain4 "
    "gain_line step1_0 gain5 final1_1a step1_1"
).split()


def group_sizes():
    return [sum(sum(parts) for parts in sets) for sets in GROUPS]


def slot_order_of(me, own):
    near, far = core_neighbours(me)
    relations = [DIAGONAL | CORE, far | CORE, near | CORE, CORE, DIAGONAL, near, far, 0]
    slots, start = [], 0
    for size in group_sizes():
        for relation in relations:
            slots.append((me ^ relation) * own + start + jnp.arange(size, dtype=jnp.int32))
        start += size
    return jnp.concatenate(slots).astype(jnp.int32)


def flat(blocks):
    return blocks.reshape(-1, B)


def reduce_and_step(me, own, grads, state, gain_grad):
    plan = Plan()
    owners = lax.axis_size("fsdp")
    near_pairs, far_pairs = plane_pairs(owners)
    place = lax.axis_index("rep")
    inner = (place == 1) | (place == 2)
    done = ()
    start = 0

    for number, sets in enumerate(GROUPS):
        total = group_sizes()[number]

        def name(text, number=number):
            return text + str(number)

        both = [name("grads"), name("core")]

        def chip(pair, arrived, first, last):
            return flat(pair[1][first:last]), flat(arrived[first:last])

        plan.core(
            name("grads"), [],
            lambda pair=grads[2 * number : 2 * number + 2]: pair,
        )
        plan.send(name("core"), [name("grads")], lambda pair: exchange(pair[0], CORE))
        plan.core(
            name("near_sum"), both,
            lambda pair, arrived, total=total: add_low(*chip(pair, arrived, 0, 2 * total)),
        )
        plan.send(
            name("near"), [name("near_sum")], lambda t: lax.ppermute(t, "fsdp", near_pairs)
        )
        inside = 0
        for member, parts in enumerate(sets):
            size = sum(parts)
            finals = []

            def at(text, number=number, member=member):
                return "%s%d_%d" % (text, number, member)

            def far_sum(pair, arrived, r, inside=inside, size=size, total=total):
                first = 2 * total + inside
                return add_low(
                    *chip(pair, arrived, first, first + size), r[inside * B : (inside + size) * B]
                )

            plan.core(at("far_sum"), both + [name("near")], far_sum)
            plan.send(
                at("far"), [at("far_sum")], lambda t: lax.ppermute(t, "fsdp", far_pairs)
            )
            firsts = [sum(parts[:p]) for p in range(len(parts) + 1)]

            def plane_sum(pair, arrived, r, q, inside=inside, total=total, firsts=firsts):
                sums = []
                for a, b in zip(firsts[:-1], firsts[1:]):
                    first, last = inside + a, inside + b
                    sums.append(
                        add_low(
                            *chip(pair, arrived, 3 * total + first, 3 * total + last),
                            r[(total + first) * B : (total + last) * B],
                            q[a * B : b * B],
                        )
                    )
                return sums

            plan.core(at("plane_sum"), both + [name("near"), at("far")], plane_sum)
            for part in range(len(parts)):

                def of(text, part=part, at=at):
                    return at(text) + "abcd"[part]

                plan.send(
                    of("inward"), [at("plane_sum")],
                    lambda t, part=part: lax.ppermute(t[part], "rep", [(0, 1), (3, 2)]),
                )
                plan.core(
                    of("halfway"), [at("plane_sum"), of("inward")],
                    lambda t, r, part=part: add_low(t[part], r),
                )
                plan.send(
                    of("middle"), [of("halfway")],
                    lambda t: lax.ppermute(t, "rep", [(1, 2), (2, 1)]),
                )
                plan.core(of("whole"), [of("halfway"), of("middle")], add_low)
                plan.send(
                    of("outward"), [of("whole")],
                    lambda t: lax.ppermute(t, "rep", [(1, 0), (2, 3)]),
                )
                plan.core(
                    of("final"), [of("whole"), of("outward")],
                    lambda whole, outward: jnp.where(inner, whole, outward),
                )
                finals.append(of("final"))
            inside += size

            def step(*grads, start=start):
                nonlocal done
                done = adam_blocks(grads, start, state, done)
                return done

            plan.core(at("step"), finals, step)
            start += size

    old = None
    line = [[(i, i ^ bit) for i in range(4)] for bit in (1, 2)]
    for n, (text, axis, pairs) in enumerate(
        (("far", "fsdp", far_pairs), ("near", "fsdp", near_pairs),
         ("core", "fsdp", [(i, i ^ CORE) for i in range(owners)]),
         ("pair", "rep", line[0]), ("line", "rep", line[1]))
    ):
        plan.send(
            "gain_" + text, [old] if old else [],
            lambda gain=gain_grad, axis=axis, pairs=pairs: lax.ppermute(gain, axis, pairs),
        )
        new = "gain" + str(n + 1)
        if old:
            plan.core(new, [old, "gain_" + text], lambda a, b: a + b)
        else:
            plan.core(new, ["gain_" + text], lambda b: gain_grad + b)
        old = new
    values = plan.run(ORDER)
    return done, values[old]


def shards(
    tokens,
    cotangent,
    segment_ids,
    block_slot_index,
    weights,
    first_moment,
    second_moment,
    left_basis,
    right_basis,
    norm_gains,
    gain_first,
    gain_second,
):
    owners = lax.axis_size("fsdp")
    own = weights.shape[0]
    slots = own * owners
    me = lax.axis_index("fsdp")
    state = (weights, first_moment, second_moment, left_basis, right_basis)
    small = owners == 8 and lax.axis_size("rep") == 4 and own == sum(group_sizes())

    if small:
        pieces, bases = gather_pieces(weights, me)
        slot_order = slot_order_of(me, own)
        out_sizes = [4 * size for size in group_sizes() for _ in range(2)]
    else:
        pieces = [lax.all_gather(weights.astype(BF16), "fsdp", axis=0, tiled=True)]
        bases = jnp.arange(owners, dtype=jnp.int32) * own
        slot_order = jnp.arange(slots, dtype=jnp.int32)
        out_sizes = [slots]
    block_out, token_grad, gain_grad, *grads = run_layer(
        tokens, cotangent, segment_ids, block_slot_index, norm_gains, pieces, own, bases,
        slot_order, out_sizes,
    )
    if small:
        done, gain_grads = reduce_and_step(me, own, grads, state, gain_grad)
    else:
        owner_sums = lax.psum_scatter(
            grads[0], "fsdp", scatter_dimension=0, tiled=True
        )
        owner_grads = flat(lax.psum(owner_sums, "rep"))
        done = adam_blocks([owner_grads], 0, state, ())
        gain_grads = sum_everywhere(sum_everywhere(gain_grad, "fsdp"), "rep")
    grads_wide, first_new, second_new, weights_new, weights_low = done
    gain_first_new, gain_second_new, gains_new = adam_plain(
        gain_grads, norm_gains, gain_first, gain_second
    )
    return (
        block_out,
        token_grad,
        grads_wide,
        first_new,
        second_new,
        weights_new,
        weights_low,
        gain_first_new,
        gain_second_new,
        gains_new,
    )


def solution(mesh):
    return jax.shard_map(
        shards,
        mesh=mesh,
        in_specs=(
            P(("fsdp", "rep"), None),
            P(("fsdp", "rep"), None),
            P(("fsdp", "rep"), None),
            P(),
            P("fsdp", None, None),
            P("fsdp", None, None),
            P("fsdp", None, None),
            P("fsdp", None, None),
            P("fsdp", None, None),
            P(),
            P(),
            P(),
        ),
        out_specs=(
            P(("fsdp", "rep"), None),
            P(("fsdp", "rep"), None),
            P("fsdp", None, None),
            P("fsdp", None, None),
            P("fsdp", None, None),
            P("fsdp", None, None),
            P("fsdp", None, None),
            P(),
            P(),
            P(),
        ),
        check_vma=False,
    )
```

```python
import functools
import math

import jax
import jax.numpy as jnp
import numpy as np
from jax import lax
from jax.experimental import pallas as pl
from jax.experimental.pallas import tpu as pltpu
from jax.sharding import PartitionSpec as P

D = 768
HEADS = 12
HEAD_DIM = 64
FF = 2048
BLOCK_ORDER = 256
STEP = 10


NORM_EPS = 1e-05
ROPE_BASE = 10000.0
BETA_ONE = 0.5
BETA_TWO = 0.5
ADAM_EPS = 1e-08
RATE = 0.03
GAIN_RATE = 0.4
DECAY = 0.01
MASKED = -1e30

B = BLOCK_ORDER
BF16 = jnp.bfloat16
F32 = jnp.float32
MIB = 1024 * 1024

LEFT_X, LEFT_A, LEFT_Y, LEFT_ACT = 0, D // B, 2 * D // B, 3 * D // B
LEFT_ROWS = 3 * D + FF
RIGHT_Q, RIGHT_K, RIGHT_V, RIGHT_O = 0, D, 2 * D, 3 * D
RIGHT_G, RIGHT_U, RIGHT_D = 4 * D, 4 * D + FF, 4 * D + 2 * FF
RIGHT_COLS = 5 * D + 2 * FF


def matrix_table():
    return [
        (D // B, D // B, LEFT_X, RIGHT_Q // B),
        (D // B, D // B, LEFT_X, RIGHT_K // B),
        (D // B, D // B, LEFT_X, RIGHT_V // B),
        (D // B, D // B, LEFT_A, RIGHT_O // B),
        (D // B, FF // B, LEFT_Y, RIGHT_G // B),
        (D // B, FF // B, LEFT_Y, RIGHT_U // B),
        (FF // B, D // B, LEFT_ACT, RIGHT_D // B),
    ]


def factor_tables():
    lefts, rights = [], []
    for grid_rows, grid_cols, left, right in matrix_table():
        for i in range(grid_rows):
            for j in range(grid_cols):
                lefts.append(left + i)
                rights.append(right + j)
    return np.array(lefts, np.int32), np.array(rights, np.int32)


def dot_nn(a, b):
    return jnp.dot(a, b, preferred_element_type=F32)


def dot_nt(a, b):
    return lax.dot_general(a, b, (((1,), (1,)), ((), ())), preferred_element_type=F32)


def half_swap(values, low_half):
    return jnp.where(low_half, pltpu.roll(values, 96, 1), pltpu.roll(values, 32, 1))


def list_factors(index_ref, block_left_ref, block_right_ref, left_ref, right_ref):
    def clear(g, carry):
        for n in range(4):
            left_ref[4 * g + n] = -1
            right_ref[4 * g + n] = 0
        return carry

    lax.fori_loop(0, left_ref.shape[0] // 4, clear, 0)

    def enter(g, carry):
        for n in range(4):
            slot = index_ref[4 * g + n]
            left_ref[slot] = block_left_ref[4 * g + n]
            right_ref[slot] = block_right_ref[4 * g + n]
        return carry

    lax.fori_loop(0, index_ref.shape[0] // 4, enter, 0)


WEIGH_COPY = 4


def weigh_slots(slot_ref, left_ref, right_ref, lefts, rights, outs, ring, sems):
    copies = [out.shape[0] // WEIGH_COPY for out in outs]
    total = sum(copies)
    assert total % 2 == 0

    def put(target, place):
        return pltpu.make_async_copy(ring.at[place], target, sems.at[place])

    def run(g, carry):
        first_place = 2 * lax.rem(g, 2)
        for half in range(2):

            @pl.when(g >= 2)
            def _(half=half):
                put(ring.at[first_place + half], first_place + half).wait()

        for n in range(2 * WEIGH_COPY):
            slot = slot_ref[2 * g * WEIGH_COPY + n]
            left = left_ref[slot]
            grad = dot_nn(
                lefts[pl.ds(pl.multiple_of(jnp.maximum(left, 0) * B, B), B), :],
                rights[:, pl.ds(pl.multiple_of(right_ref[slot] * B, B), B)],
            )
            keep = jnp.where(left >= 0, 1.0, 0.0)
            ring[first_place + n // WEIGH_COPY, n % WEIGH_COPY] = (grad * keep).astype(BF16)
        for half in range(2):
            copy = 2 * g + half
            first = 0
            for out, count in zip(outs, copies):

                @pl.when((copy >= first) & (copy < first + count))
                def _(out=out, first=first, half=half, copy=copy):
                    at = pl.ds((copy - first) * WEIGH_COPY, WEIGH_COPY)
                    put(out.at[at], first_place + half).start()

                first += count
        return carry

    assert total >= 4
    lax.fori_loop(0, total // 2, run, 0)
    for place in range(4):
        put(ring.at[place], place).wait()


def layer_kernel(
    micro,
    own,
    piece_slots,
    out_count,
    index_ref,
    base_ref,
    slot_ref,
    block_left_ref,
    block_right_ref,
    segments_ref,
    segments_t_ref,
    x_hbm,
    dy_hbm,
    gains_ref,
    *rest,
):
    pieces = rest[: len(piece_slots)]
    rest = rest[len(piece_slots) :]
    out_hbm, token_grad_hbm, gain_ref = rest[:3]
    grad_refs, rest = rest[3 : 3 + out_count], rest[3 + out_count :]
    (
        w_qkv,
        w_o,
        w_gu,
        w_d,
        lefts,
        rights,
        q_scr,
        k_scr,
        v_scr,
        p_scr,
        a_scr,
        act_scr,
        cg_scr,
        cu_scr,
        y1_scr,
        y1_low_scr,
        h1_scr,
        dh2_scr,
        r1_scr,
        w_sems,
        ring,
        ring_sems,
        left_ref,
        right_ref,
        bias_ref,
        cos_ref,
        sin_ref,
        cos_t_ref,
        sin_t_ref,
        x_ref,
        dy_ref,
        out_ref,
        token_grad_ref,
        row_sems,
    ) = rest
    seq = segments_ref.shape[1]
    bring_x = pltpu.make_async_copy(x_hbm, x_ref, row_sems.at[0])
    bring_dy = pltpu.make_async_copy(dy_hbm, dy_ref, row_sems.at[1])
    take_out = pltpu.make_async_copy(out_ref, out_hbm, row_sems.at[2])
    take_token_grad = pltpu.make_async_copy(token_grad_ref, token_grad_hbm, row_sems.at[3])
    bring_x.start()
    bring_dy.start()

    starts = [sum(piece_slots[:n]) for n in range(len(piece_slots) + 1)]
    reciprocal = (1 << 16) // own + 1
    assert all(slot * reciprocal >> 16 == slot // own for slot in range(starts[-1]))

    def fetch(block, target, row, col, sem):
        slot = index_ref[block]
        owner = lax.shift_right_logical(slot * reciprocal, 16)
        place = base_ref[owner] + slot - owner * own

        def among(low, high):
            if high - low > 1:
                middle = (low + high) // 2
                lax.cond(
                    place < starts[middle],
                    lambda: among(low, middle),
                    lambda: among(middle, high),
                )
            else:
                pltpu.make_async_copy(
                    pieces[low].at[place - starts[low]],
                    target.at[
                        pl.ds(pl.multiple_of(row * B, B), B), pl.ds(pl.multiple_of(col * B, B), B)
                    ],
                    sem,
                ).start()

        among(0, len(pieces))

    def fetch_matrix(first_block, grid_rows, grid_cols, target, col_offset, sem):
        def one(t, carry):
            i = t // grid_cols
            j = t - i * grid_cols
            fetch(first_block + t, target, i, j + col_offset, sem)
            return carry

        lax.fori_loop(0, grid_rows * grid_cols, one, 0)

    nd, nf = D // B, FF // B
    for m in range(3):
        fetch_matrix(m * nd * nd, nd, nd, w_qkv, m * nd, w_sems.at[0])

    list_factors(index_ref, block_left_ref, block_right_ref, left_ref, right_ref)
    half_dim = HEAD_DIM // 2
    step = lax.broadcasted_iota(jnp.int32, (half_dim, 1), 0).astype(F32)
    frequency = jnp.exp(step * (-2.0 / HEAD_DIM * math.log(ROPE_BASE)))
    keys = lax.broadcasted_iota(jnp.int32, (seq, seq), 0)
    queries = lax.broadcasted_iota(jnp.int32, (seq, seq), 1)
    for r in range(micro):
        rows = slice(r * seq, (r + 1) * seq)
        same = segments_t_ref[:, r : r + 1] == segments_ref[r : r + 1, :]
        bias_ref[r] = jnp.where(same & (keys <= queries), 0.0, MASKED)
        first = jnp.min(jnp.where(same, keys, seq), axis=0, keepdims=True)
        angles = frequency * (queries[0:1, :] - first).astype(F32)
        cosine_t, sine_t = jnp.cos(angles), jnp.sin(angles)
        cos_t_ref[:, rows] = cosine_t
        sin_t_ref[:, rows] = sine_t
        cosine, sine = cosine_t.T, sine_t.T
        cos_ref[rows, :] = jnp.concatenate([cosine] * 4, axis=1)
        sin_ref[rows, :] = jnp.concatenate([-sine, sine, -sine, sine], axis=1)

    fetch_matrix(3 * nd * nd, nd, nd, w_o, 0, w_sems.at[1])
    for m in range(2):
        fetch_matrix(4 * nd * nd + m * nd * nf, nd, nf, w_gu, m * nf, w_sems.at[2])
    fetch_matrix(4 * nd * nd + 2 * nd * nf, nf, nd, w_d, 0, w_sems.at[3])

    def wait_for(target, sem):
        pltpu.make_async_copy(target, target, sem).wait()

    bring_x.wait()
    lefts[0:D, :] = x_ref[...].T
    lane = lax.broadcasted_iota(jnp.int32, (1, 128), 1)
    low_half = lax.rem(lane, HEAD_DIM) < HEAD_DIM // 2
    head_lanes = [lane < HEAD_DIM, lane >= HEAD_DIM]

    def of_head(values, h):
        return jnp.where(head_lanes[h], values, jnp.zeros_like(values))

    wait_for(w_qkv, w_sems.at[0])

    def attend(jb, carry):
        def columns(offset):
            return pl.ds(pl.multiple_of(offset + jb * B, B), B)

        x = x_ref[...]
        q_raw = dot_nn(x, w_qkv[:, columns(0)])
        k_raw = dot_nn(x, w_qkv[:, columns(D)])
        v_raw = dot_nn(x, w_qkv[:, columns(2 * D)])
        cosine = cos_ref[...]
        sine = sin_ref[...]
        for sub in range(2):
            part = slice(sub * 128, sub * 128 + 128)
            slab = pl.ds(pl.multiple_of(jb * B + sub * 128, 128), 128)
            q = q_raw[:, part]
            k = k_raw[:, part]
            q = ((q * cosine + half_swap(q, low_half) * sine) * HEAD_DIM**-0.5).astype(BF16)
            k = (k * cosine + half_swap(k, low_half) * sine).astype(BF16)
            v = v_raw[:, part].astype(BF16)
            q_scr[:, slab] = q
            k_scr[:, slab] = k
            v_scr[:, slab] = v
            for r in range(micro):
                rows = slice(r * seq, (r + 1) * seq)
                v_t = v[rows].T
                outs = []
                for h in range(2):
                    scores = dot_nt(k[rows], of_head(q[rows], h)) + bias_ref[r]
                    top = jnp.max(scores, axis=0, keepdims=True)
                    exps = jnp.exp(scores - top)
                    total = jnp.sum(exps, axis=0, keepdims=True)
                    probs = (exps * (1.0 / total)).astype(BF16)
                    p_scr[(jb * 2 + sub) * 2 * micro + 2 * r + h] = probs
                    outs.append(dot_nn(v_t[h * HEAD_DIM : (h + 1) * HEAD_DIM], probs))
                a_t = jnp.concatenate(outs, axis=0).astype(BF16)
                lefts[pl.ds(pl.multiple_of(D + jb * B + sub * 128, 128), 128), rows] = a_t
                a_scr[rows, slab] = a_t.T
        return carry

    lax.fori_loop(0, nd, attend, 0, unroll=True)

    wait_for(w_o, w_sems.at[1])
    for r in range(micro):
        rows = slice(r * seq, (r + 1) * seq)
        h1 = x_ref[rows, :].astype(F32) + dot_nn(a_scr[rows, :], w_o[...])
        r1 = lax.rsqrt(jnp.mean(h1 * h1, axis=-1, keepdims=True) + NORM_EPS)
        y1 = h1 * r1 * gains_ref[0:1, :]
        y1_low = y1.astype(BF16)
        h1_scr[rows, :] = h1
        r1_scr[rows, :] = r1
        y1_scr[rows, :] = y1
        y1_low_scr[rows, :] = y1_low
        lefts[2 * D : 3 * D, rows] = y1_low.T

    wait_for(w_gu, w_sems.at[2])

    def feed(j, carry):
        y1_low = y1_low_scr[...]
        cols = pl.ds(pl.multiple_of(j * B, B), B)
        gate = dot_nn(y1_low, w_gu[:, cols])
        up = dot_nn(y1_low, w_gu[:, pl.ds(pl.multiple_of(FF + j * B, B), B)])
        sig = 1.0 / (1.0 + jnp.exp(-gate))
        silu = gate * sig
        act = (silu * up).astype(BF16)
        act_scr[:, cols] = act
        cu_scr[:, cols] = silu.astype(BF16)
        cg_scr[:, cols] = (up * sig * (1.0 + gate * (1.0 - sig))).astype(BF16)
        lefts[pl.ds(pl.multiple_of(3 * D + j * B, B), B), :] = act.T
        return carry

    lax.fori_loop(0, nf, feed, 0, unroll=2)

    wait_for(w_d, w_sems.at[3])
    bring_dy.wait()
    gain_two = jnp.zeros((1, D), F32)
    for r in range(micro):
        rows = slice(r * seq, (r + 1) * seq)
        h2 = y1_scr[rows, :] + dot_nn(act_scr[rows, :], w_d[...])
        r2 = lax.rsqrt(jnp.mean(h2 * h2, axis=-1, keepdims=True) + NORM_EPS)
        scaled = h2 * r2
        gain = gains_ref[1:2, :]
        out_ref[rows, :] = (scaled * gain).astype(BF16)
        dy = dy_ref[rows, :].astype(F32)
        gain_two += jnp.sum(dy * scaled, axis=0, keepdims=True)
        dyg = dy * gain
        dh2 = r2 * (dyg - scaled * jnp.mean(scaled * dyg, axis=-1, keepdims=True))
        dh2_scr[rows, :] = dh2
        rights[rows, RIGHT_D:] = dh2.astype(BF16)
    gain_ref[1:2, :] = gain_two
    take_out.start()

    def feed_back(j, carry):
        cols = pl.ds(pl.multiple_of(j * B, B), B)
        dact = dot_nt(rights[:, RIGHT_D:], w_d[cols, :])
        rights[:, pl.ds(pl.multiple_of(RIGHT_G + j * B, B), B)] = (
            dact * cg_scr[:, cols].astype(F32)
        ).astype(BF16)
        rights[:, pl.ds(pl.multiple_of(RIGHT_U + j * B, B), B)] = (
            dact * cu_scr[:, cols].astype(F32)
        ).astype(BF16)
        return carry

    lax.fori_loop(0, nf, feed_back, 0)

    def feed_in(j, carry):
        cols = pl.ds(pl.multiple_of(j * B, B), B)
        dh2_scr[:, cols] += dot_nt(rights[:, RIGHT_G:RIGHT_D], w_gu[cols, :])
        return carry

    lax.fori_loop(0, nd, feed_in, 0)

    gain_one = jnp.zeros((1, D), F32)
    for r in range(micro):
        rows = slice(r * seq, (r + 1) * seq)
        dy1 = dh2_scr[rows, :]
        r1 = r1_scr[rows, :]
        scaled = h1_scr[rows, :] * r1
        gain_one += jnp.sum(dy1 * scaled, axis=0, keepdims=True)
        dyg = dy1 * gains_ref[0:1, :]
        dh1 = r1 * (dyg - scaled * jnp.mean(scaled * dyg, axis=-1, keepdims=True))
        h1_scr[rows, :] = dh1
        do = dh1.astype(BF16)
        rights[rows, RIGHT_O : RIGHT_O + D] = do
        a_scr[rows, :] = dot_nt(do, w_o[...]).astype(BF16)
    gain_ref[0:1, :] = gain_one

    def attend_back(jb, carry):
        for sub in range(2):
            slab = pl.ds(pl.multiple_of(jb * B + sub * 128, 128), 128)
            for r in range(micro):
                rows = slice(r * seq, (r + 1) * seq)
                q = q_scr[rows, slab]
                k = k_scr[rows, slab]
                v = v_scr[rows, slab]
                da = a_scr[rows, slab]
                k_t = k.T
                dv = jnp.zeros((seq, 128), F32)
                dk = jnp.zeros((seq, 128), F32)
                dq_t = []
                for h in range(2):
                    probs = p_scr[(jb * 2 + sub) * 2 * micro + 2 * r + h]
                    da_h = of_head(da, h)
                    probs_wide = probs.astype(F32)
                    dprobs = dot_nt(v, da_h)
                    weighted = probs_wide * dprobs
                    row_sum = jnp.sum(weighted, axis=0, keepdims=True)
                    ds = (weighted - probs_wide * row_sum).astype(BF16)
                    dv += dot_nn(probs, da_h)
                    dk += dot_nn(ds, of_head(q, h))
                    dq_h = dot_nn(k_t[h * HEAD_DIM : (h + 1) * HEAD_DIM], ds) * HEAD_DIM**-0.5
                    low, high = dq_h[: HEAD_DIM // 2], dq_h[HEAD_DIM // 2 :]
                    cosine = cos_t_ref[:, rows]
                    sine = sin_t_ref[:, rows]
                    dq_t.append(low * cosine + high * sine)
                    dq_t.append(high * cosine - low * sine)
                dq = jnp.concatenate(dq_t, axis=0).astype(BF16).T
                dk = dk * cos_ref[rows, :] - half_swap(dk, low_half) * sin_ref[rows, :]
                rights[rows, slab] = dq
                rights[rows, pl.ds(pl.multiple_of(RIGHT_K + jb * B + sub * 128, 128), 128)] = (
                    dk.astype(BF16)
                )
                rights[rows, pl.ds(pl.multiple_of(RIGHT_V + jb * B + sub * 128, 128), 128)] = (
                    dv.astype(BF16)
                )
        return carry

    lax.fori_loop(0, nd, attend_back, 0, unroll=True)

    def token_back(j, carry):
        cols = pl.ds(pl.multiple_of(j * B, B), B)
        token_grad_ref[:, cols] = (
            h1_scr[:, cols] + dot_nt(rights[:, : 3 * D], w_qkv[cols, :])
        ).astype(BF16)
        return carry

    lax.fori_loop(0, nd, token_back, 0)
    take_token_grad.start()

    weigh_slots(slot_ref, left_ref, right_ref, lefts, rights, grad_refs, ring, ring_sems)
    take_out.wait()
    take_token_grad.wait()


def run_layer(
    tokens, cotangent, segment_ids, block_slot_index, norm_gains, pieces, own, bases, slot_order,
    out_sizes,
):
    micro, seq = segment_ids.shape
    count = micro * seq
    slots = own * bases.shape[0]
    grads = [jax.ShapeDtypeStruct((size, B, B), BF16) for size in out_sizes]
    vmem = pl.BlockSpec(memory_space=pltpu.VMEM)
    smem = pl.BlockSpec(memory_space=pltpu.SMEM)
    hbm = pl.BlockSpec(memory_space=pl.ANY)
    return pl.pallas_call(
        functools.partial(layer_kernel, micro, own, [p.shape[0] for p in pieces], len(grads)),
        out_shape=(
            jax.ShapeDtypeStruct((count, D), BF16),
            jax.ShapeDtypeStruct((count, D), BF16),
            jax.ShapeDtypeStruct((2, D), F32),
            *grads,
        ),
        in_specs=[smem] * 5 + [vmem] * 2 + [hbm] * 2 + [vmem] + [hbm] * len(pieces),
        out_specs=(hbm, hbm, vmem) + (hbm,) * len(grads),
        scratch_shapes=[
            pltpu.VMEM((D, 3 * D), BF16),
            pltpu.VMEM((D, D), BF16),
            pltpu.VMEM((D, 2 * FF), BF16),
            pltpu.VMEM((FF, D), BF16),
            pltpu.VMEM((LEFT_ROWS, count), BF16),
            pltpu.VMEM((count, RIGHT_COLS), BF16),
            pltpu.VMEM((count, D), BF16),
            pltpu.VMEM((count, D), BF16),
            pltpu.VMEM((count, D), BF16),
            pltpu.VMEM((HEADS * micro, seq, seq), BF16),
            pltpu.VMEM((count, D), BF16),
            pltpu.VMEM((count, FF), BF16),
            pltpu.VMEM((count, FF), BF16),
            pltpu.VMEM((count, FF), BF16),
            pltpu.VMEM((count, D), F32),
            pltpu.VMEM((count, D), BF16),
            pltpu.VMEM((count, D), F32),
            pltpu.VMEM((count, D), F32),
            pltpu.VMEM((count, 1), F32),
            pltpu.SemaphoreType.DMA((4,)),
            pltpu.VMEM((4, WEIGH_COPY, B, B), BF16),
            pltpu.SemaphoreType.DMA((4,)),
            pltpu.SMEM((slots,), jnp.int32),
            pltpu.SMEM((slots,), jnp.int32),
            pltpu.VMEM((micro, seq, seq), F32),
            pltpu.VMEM((count, 128), F32),
            pltpu.VMEM((count, 128), F32),
            pltpu.VMEM((HEAD_DIM // 2, count), F32),
            pltpu.VMEM((HEAD_DIM // 2, count), F32),
            *(pltpu.VMEM((count, D), BF16) for _ in range(4)),
            pltpu.SemaphoreType.DMA((4,)),
        ],
        compiler_params=pltpu.CompilerParams(vmem_limit_bytes=56 * MIB),
        cost_estimate=pl.CostEstimate(
            flops=23_000_000_000, bytes_accessed=32_000_000, transcendentals=3_000_000
        ),
        name="layer",
    )(
        block_slot_index,
        bases,
        slot_order,
        *(jnp.asarray(table) for table in factor_tables()),
        segment_ids,
        segment_ids.T,
        tokens,
        cotangent,
        norm_gains,
        *pieces,
    )


def split_two(values):
    high = values.astype(BF16)
    return high, (values - high.astype(F32)).astype(BF16)


def adam_kernel(steps, weight_ref, first_ref, second_ref, left_ref, right_ref, *rest):
    grad_refs = rest[: len(steps)]
    grad_out, first_out, second_out, weight_out, low_out, grads = rest[-6:]
    now, start = pl.program_id(0), 0
    for count, grad_ref in zip(steps, grad_refs):

        @pl.when((now >= start) & (now < start + count))
        def _(grad_ref=grad_ref):
            grads[...] = grad_ref[...]

        start += count
    for n in range(weight_ref.shape[0]):
        grad = grads[n * B : (n + 1) * B, :]
        left, left_rest = split_two(left_ref[n])
        right, right_rest = split_two(right_ref[n])
        grad_out[n] = grad.astype(F32)
        turned = (dot_nn(grad, right) + dot_nn(grad, right_rest)).astype(BF16)
        turned = dot_nn(left.T, turned) + dot_nn(left_rest.T, turned)
        first_new = BETA_ONE * first_ref[n] + (1.0 - BETA_ONE) * turned
        second_new = BETA_TWO * second_ref[n] + (1.0 - BETA_TWO) * turned * turned
        first_out[n] = first_new
        second_out[n] = second_new
        ratio = (
            first_new
            / (1.0 - BETA_ONE**STEP)
            / (jnp.sqrt(second_new / (1.0 - BETA_TWO**STEP)) + ADAM_EPS)
        )
        back = dot_nt(dot_nn(left, ratio.astype(BF16)).astype(BF16), right)
        weight = weight_ref[n]
        weight_new = weight - RATE * (back + DECAY * weight)
        weight_out[n] = weight_new
        low_out[n] = weight_new.astype(BF16)


def adam_blocks(grads, start, state, done):
    own = state[0].shape[0]
    step = math.gcd(2, start, *(part.shape[0] // B for part in grads))
    steps = [part.shape[0] // B // step for part in grads]
    local = []
    for number, count in enumerate(steps):
        local.append(
            pl.BlockSpec(
                (step * B, B),
                lambda s, first=sum(steps[:number]), count=count: (
                    jnp.clip(s - first, 0, count - 1),
                    0,
                ),
            )
        )
    spec = pl.BlockSpec((step, B, B), lambda s: (s + start // step, 0, 0))
    hbm = pl.BlockSpec(memory_space=pl.ANY)
    wide = jax.ShapeDtypeStruct((own, B, B), F32)
    return pl.pallas_call(
        functools.partial(adam_kernel, steps),
        grid=(sum(steps),),
        out_shape=(wide, wide, wide, wide, jax.ShapeDtypeStruct((own, B, B), BF16)),
        in_specs=[spec] * 5 + local + [hbm] * len(done),
        out_specs=(spec,) * 5,
        input_output_aliases={5 + len(local) + n: n for n in range(len(done))},
        scratch_shapes=[pltpu.VMEM((step * B, B), BF16)],
        compiler_params=pltpu.CompilerParams(vmem_limit_bytes=60 * MIB),
        cost_estimate=pl.CostEstimate(
            flops=sum(steps) * step * 12 * B**3,
            bytes_accessed=sum(steps) * step * B * B * 42,
            transcendentals=sum(steps) * step * B * B,
        ),
        name="adam",
    )(*state, *grads, *done)


def adam_plain(grads, values, first_moment, second_moment):
    first_new = BETA_ONE * first_moment + (1.0 - BETA_ONE) * grads
    second_new = BETA_TWO * second_moment + (1.0 - BETA_TWO) * grads * grads
    step_ratio = (
        first_new
        / (1.0 - BETA_ONE**STEP)
        / (jnp.sqrt(second_new / (1.0 - BETA_TWO**STEP)) + ADAM_EPS)
    )
    return (first_new, second_new, values - GAIN_RATE * step_ratio)


def sum_everywhere(values, axis):
    size = lax.axis_size(axis)
    if size & (size - 1):
        return lax.psum(values, axis)
    reach = 1
    while reach < size:
        values = values + lax.ppermute(values, axis, [(i, i ^ reach) for i in range(size)])
        reach *= 2
    return values


def add_low(*terms):
    return sum(term.astype(F32) for term in terms).astype(BF16)


CORE, ACROSS, ALONG = 1, 2, 4
DIAGONAL = ACROSS | ALONG


def exchange(values, bit):
    return lax.ppermute(values, "fsdp", [(i, i ^ bit) for i in range(lax.axis_size("fsdp"))])


def core_neighbours(me):
    near = jnp.where((me & CORE) == 0, ACROSS, ALONG)
    return near, DIAGONAL ^ near


def plane_pairs(owners):
    near = [(i, i ^ (ALONG if i & CORE else ACROSS)) for i in range(owners)]
    far = [(i, i ^ (ACROSS if i & CORE else ALONG)) for i in range(owners)]
    return near, far


def after(values, *others):
    return lax.optimization_barrier((values, *others))[0]


def gather_pieces(weights, me):
    own = weights.shape[0]
    half = own // 2
    near, far = core_neighbours(me)
    near_pairs, far_pairs = plane_pairs(lax.axis_size("fsdp"))
    mine = weights.astype(BF16)
    first_near = lax.ppermute(weights[:half].astype(BF16), "fsdp", near_pairs)
    last_near = lax.ppermute(weights[half:].astype(BF16), "fsdp", near_pairs)
    all_far = lax.ppermute(mine, "fsdp", far_pairs)
    first_diagonal = lax.ppermute(first_near, "fsdp", far_pairs)
    last_diagonal = lax.ppermute(last_near, "fsdp", far_pairs)
    pieces, relations = [], []
    for parts, relation, others in (
        ((mine,), 0, 0),
        ((first_near, last_near), near, far),
        ((all_far,), far, near),
        ((first_diagonal, last_diagonal), DIAGONAL, DIAGONAL),
    ):
        pieces += [*parts, *(exchange(part, CORE) for part in parts)]
        relations += [relation, others | CORE]
    owners = me ^ jnp.stack(relations).astype(jnp.int32)
    bases = jnp.sum(
        jnp.where(
            jnp.arange(len(relations), dtype=jnp.int32)[:, None] == owners[None, :],
            jnp.arange(len(relations), dtype=jnp.int32)[None, :] * own,
            0,
        ),
        axis=1,
    )
    return pieces, bases


class Plan:
    def __init__(self):
        self.tasks = {}

    def core(self, name, needs, run):
        self.tasks[name] = (True, needs, run)

    def send(self, name, needs, run):
        self.tasks[name] = (False, needs, run)

    def run(self, order):
        assert sorted(order) == sorted(self.tasks)
        values, last = {}, None
        for name in order:
            on_core, needs, run = self.tasks[name]
            inputs = [values[n] for n in needs]
            if last is not None:
                *inputs, _ = lax.optimization_barrier((*inputs, last))
            values[name] = run(*inputs)
            if on_core:
                last = jax.tree.leaves(values[name])[0]
        return values


GROUPS = (((4,),), ((6,), (4,)))
ORDER = (
    "grads0", "grads1", "core0", "gain_far", "near_sum0", "near0", "core1", "near_sum1", "near1",
    "gain1", "far_sum0_0", "far0_0", "plane_sum0_0", "inward0_0a", "halfway0_0a", "middle0_0a",
    "far_sum1_0", "far1_0", "far_sum1_1", "far1_1", "gain_near", "whole0_0a", "outward0_0a",
    "plane_sum1_0", "inward1_0a", "plane_sum1_1", "inward1_1a", "gain2", "gain_core", "halfway1_0a",
    "middle1_0a", "final0_0a", "gain3", "gain_pair", "halfway1_1a", "middle1_1a", "whole1_0a",
    "outward1_0a", "step0_0", "whole1_1a", "outward1_1a", "final1_0a", "gain4", "gain_line",
    "step1_0", "gain5", "final1_1a", "step1_1",
)


def group_sizes():
    return [sum(sum(parts) for parts in sets) for sets in GROUPS]


def slot_order_of(me, own):
    near, far = core_neighbours(me)
    relations = [DIAGONAL | CORE, far | CORE, near | CORE, CORE, DIAGONAL, near, far, 0]
    slots, start = [], 0
    for size in group_sizes():
        for relation in relations:
            slots.append((me ^ relation) * own + start + jnp.arange(size, dtype=jnp.int32))
        start += size
    return jnp.concatenate(slots).astype(jnp.int32)


def flat(blocks):
    return blocks.reshape(-1, B)


def reduce_and_step(me, own, grads, state, gain_grad):
    plan = Plan()
    owners = lax.axis_size("fsdp")
    near_pairs, far_pairs = plane_pairs(owners)
    place = lax.axis_index("rep")
    inner = (place == 1) | (place == 2)
    done = ()
    start = 0

    for number, sets in enumerate(GROUPS):
        total = group_sizes()[number]

        def name(text, number=number):
            return text + str(number)

        both = [name("grads"), name("core")]

        def chip(pair, arrived, first, last):
            return flat(pair[1][first:last]), flat(arrived[first:last])

        plan.core(
            name("grads"), [],
            lambda pair=grads[2 * number : 2 * number + 2]: pair,
        )
        plan.send(name("core"), [name("grads")], lambda pair: exchange(pair[0], CORE))
        plan.core(
            name("near_sum"), both,
            lambda pair, arrived, total=total: add_low(*chip(pair, arrived, 0, 2 * total)),
        )
        plan.send(
            name("near"), [name("near_sum")], lambda t: lax.ppermute(t, "fsdp", near_pairs)
        )
        inside = 0
        for member, parts in enumerate(sets):
            size = sum(parts)
            finals = []

            def at(text, number=number, member=member):
                return "%s%d_%d" % (text, number, member)

            def far_sum(pair, arrived, r, inside=inside, size=size, total=total):
                first = 2 * total + inside
                return add_low(
                    *chip(pair, arrived, first, first + size), r[inside * B : (inside + size) * B]
                )

            plan.core(at("far_sum"), both + [name("near")], far_sum)
            plan.send(
                at("far"), [at("far_sum")], lambda t: lax.ppermute(t, "fsdp", far_pairs)
            )
            firsts = [sum(parts[:p]) for p in range(len(parts) + 1)]

            def plane_sum(pair, arrived, r, q, inside=inside, total=total, firsts=firsts):
                sums = []
                for a, b in zip(firsts[:-1], firsts[1:]):
                    first, last = inside + a, inside + b
                    sums.append(
                        add_low(
                            *chip(pair, arrived, 3 * total + first, 3 * total + last),
                            r[(total + first) * B : (total + last) * B],
                            q[a * B : b * B],
                        )
                    )
                return sums

            plan.core(at("plane_sum"), both + [name("near"), at("far")], plane_sum)
            for part in range(len(parts)):

                def of(text, part=part, at=at):
                    return at(text) + "abcd"[part]

                plan.send(
                    of("inward"), [at("plane_sum")],
                    lambda t, part=part: lax.ppermute(t[part], "rep", [(0, 1), (3, 2)]),
                )
                plan.core(
                    of("halfway"), [at("plane_sum"), of("inward")],
                    lambda t, r, part=part: add_low(t[part], r),
                )
                plan.send(
                    of("middle"), [of("halfway")],
                    lambda t: lax.ppermute(t, "rep", [(1, 2), (2, 1)]),
                )
                plan.core(of("whole"), [of("halfway"), of("middle")], add_low)
                plan.send(
                    of("outward"), [of("whole")],
                    lambda t: lax.ppermute(t, "rep", [(1, 0), (2, 3)]),
                )
                plan.core(
                    of("final"), [of("whole"), of("outward")],
                    lambda whole, outward: jnp.where(inner, whole, outward),
                )
                finals.append(of("final"))
            inside += size

            def step(*grads, start=start):
                nonlocal done
                done = adam_blocks(grads, start, state, done)
                return done

            plan.core(at("step"), finals, step)
            start += size

    old = None
    line = [[(i, i ^ bit) for i in range(4)] for bit in (1, 2)]
    for n, (text, axis, pairs) in enumerate(
        (("far", "fsdp", far_pairs), ("near", "fsdp", near_pairs),
         ("core", "fsdp", [(i, i ^ CORE) for i in range(owners)]),
         ("pair", "rep", line[0]), ("line", "rep", line[1]))
    ):
        plan.send(
            "gain_" + text, [old] if old else [],
            lambda gain=gain_grad, axis=axis, pairs=pairs: lax.ppermute(gain, axis, pairs),
        )
        new = "gain" + str(n + 1)
        if old:
            plan.core(new, [old, "gain_" + text], lambda a, b: a + b)
        else:
            plan.core(new, ["gain_" + text], lambda b: gain_grad + b)
        old = new
    values = plan.run(ORDER)
    return done, values[old]


def shards(
    tokens,
    cotangent,
    segment_ids,
    block_slot_index,
    weights,
    first_moment,
    second_moment,
    left_basis,
    right_basis,
    norm_gains,
    gain_first,
    gain_second,
):
    owners = lax.axis_size("fsdp")
    own = weights.shape[0]
    slots = own * owners
    me = lax.axis_index("fsdp")
    state = (weights, first_moment, second_moment, left_basis, right_basis)
    small = owners == 8 and lax.axis_size("rep") == 4 and own == sum(group_sizes())

    if small:
        pieces, bases = gather_pieces(weights, me)
        slot_order = slot_order_of(me, own)
        out_sizes = [4 * size for size in group_sizes() for _ in range(2)]
    else:
        pieces = [lax.all_gather(weights.astype(BF16), "fsdp", axis=0, tiled=True)]
        bases = jnp.arange(owners, dtype=jnp.int32) * own
        slot_order = jnp.arange(slots, dtype=jnp.int32)
        out_sizes = [slots]
    block_out, token_grad, gain_grad, *grads = run_layer(
        tokens, cotangent, segment_ids, block_slot_index, norm_gains, pieces, own, bases,
        slot_order, out_sizes,
    )
    if small:
        done, gain_grads = reduce_and_step(me, own, grads, state, gain_grad)
    else:
        owner_sums = lax.psum_scatter(
            grads[0], "fsdp", scatter_dimension=0, tiled=True
        )
        owner_grads = flat(lax.psum(owner_sums, "rep"))
        done = adam_blocks([owner_grads], 0, state, ())
        gain_grads = sum_everywhere(sum_everywhere(gain_grad, "fsdp"), "rep")
    grads_wide, first_new, second_new, weights_new, weights_low = done
    gain_first_new, gain_second_new, gains_new = adam_plain(
        gain_grads, norm_gains, gain_first, gain_second
    )
    return (
        block_out,
        token_grad,
        grads_wide,
        first_new,
        second_new,
        weights_new,
        weights_low,
        gain_first_new,
        gain_second_new,
        gains_new,
    )


def solution(mesh):
    return jax.shard_map(
        shards,
        mesh=mesh,
        in_specs=(
            P(("fsdp", "rep"), None),
            P(("fsdp", "rep"), None),
            P(("fsdp", "rep"), None),
            P(),
            P("fsdp", None, None),
            P("fsdp", None, None),
            P("fsdp", None, None),
            P("fsdp", None, None),
            P("fsdp", None, None),
            P(),
            P(),
            P(),
        ),
        out_specs=(
            P(("fsdp", "rep"), None),
            P(("fsdp", "rep"), None),
            P("fsdp", None, None),
            P("fsdp", None, None),
            P("fsdp", None, None),
            P("fsdp", None, None),
            P("fsdp", None, None),
            P(),
            P(),
            P(),
        ),
        check_vma=False,
    )
```
